32 devices in a mesh: dp: 16 (over z, y, core), head: 2 (over x).
Axes of the slice: x: 2, y: 2, z: 4, core: 2. Of those that a mesh axis runs over, the one named last changes fastest.
Arguments:
- tokens: bfloat16 [76800, 410], P(('dp', 'head')), may hold values from -6 to 6
- prior_memory: bfloat16 [64, 150, 410], P('dp'), may hold values from -6 to 6
- first_flags: int32 [64], P('dp'), may hold values from 0 to 1
- owners: int32 [7], replicated, may hold values from 0 to 15
- cotangent: float32 [76800, 410], P(('dp', 'head')), may hold values from -6 to 6
- qkvr_master: float32 [4, 410, 410], P(None, None, 'head'), may hold values from -0.3125 to 0.3125
- qkvr_first: float32 [4, 410, 410], P(None, None, 'head'), may hold values from -0.15625 to 0.15625
- qkvr_second: float32 [4, 410, 410], P(None, None, 'head'), may hold values from 5e-05 to 0.0008
- proj_master: float32 [410, 410], P('head'), may hold values from -2.5 to 2.5
- proj_first: float32 [410, 410], P('head'), may hold values from -0.15625 to 0.15625
- proj_second: float32 [410, 410], P('head'), may hold values from 5e-05 to 0.0008
- expand_master: float32 [410, 2100], P(None, 'head'), may hold values from -0.3125 to 0.3125
- expand_first: float32 [410, 2100], P(None, 'head'), may hold values from -0.15625 to 0.15625
- expand_second: float32 [410, 2100], P(None, 'head'), may hold values from 5e-05 to 0.0008
- reduce_master: float32 [2100, 410], P('head'), may hold values from -0.125 to 0.125
- reduce_first: float32 [2100, 410], P('head'), may hold values from -0.15625 to 0.15625
- reduce_second: float32 [2100, 410], P('head'), may hold values from 5e-05 to 0.0008
- headbias_master: float32 [2, 410], P(None, 'head'), may hold values from -3 to 3
- headbias_first: float32 [2, 410], P(None, 'head'), may hold values from -0.15625 to 0.15625
- headbias_second: float32 [2, 410], P(None, 'head'), may hold values from 5e-05 to 0.0008
- expbias_master: float32 [2100], P('head'), may hold values from -3 to 3
- expbias_first: float32 [2100], P('head'), may hold values from -0.15625 to 0.15625
- expbias_second: float32 [2100], P('head'), may hold values from 5e-05 to 0.0008
- norms_master: float32 [5, 410], replicated, may hold values from 0.5 to 1.5
- norms_first: float32 [5, 410], replicated, may hold values from -0.15625 to 0.15625
- norms_second: float32 [5, 410], replicated, may hold values from 5e-05 to 0.0008
Outputs:
- layer_output: float32 [76800, 410], P(('dp', 'head'))
- input_grad: float32 [76800, 410], P(('dp', 'head'))
- group_rms: float32 [7], replicated
- qkvr_grad: float32 [4, 410, 410], P(None, None, 'head')
- qkvr_newfirst: float32 [4, 410, 410], P(None, None, 'head')
- qkvr_newsecond: float32 [4, 410, 410], P(None, None, 'head')
- qkvr_newmaster: float32 [4, 410, 410], P(None, None, 'head')
- proj_grad: float32 [410, 410], P('head')
- proj_newfirst: float32 [410, 410], P('head')
- proj_newsecond: float32 [410, 410], P('head')
- proj_newmaster: float32 [410, 410], P('head')
- expand_grad: float32 [410, 2100], P(None, 'head')
- expand_newfirst: float32 [410, 2100], P(None, 'head')
- expand_newsecond: float32 [410, 2100], P(None, 'head')
- expand_newmaster: float32 [410, 2100], P(None, 'head')
- reduce_grad: float32 [2100, 410], P('head')
- reduce_newfirst: float32 [2100, 410], P('head')
- reduce_newsecond: float32 [2100, 410], P('head')
- reduce_newmaster: float32 [2100, 410], P('head')
- headbias_grad: float32 [2, 410], P(None, 'head')
- headbias_newfirst: float32 [2, 410], P(None, 'head')
- headbias_newsecond: float32 [2, 410], P(None, 'head')
- headbias_newmaster: float32 [2, 410], P(None, 'head')
- expbias_grad: float32 [2100], P('head')
- expbias_newfirst: float32 [2100], P('head')
- expbias_newsecond: float32 [2100], P('head')
- expbias_newmaster: float32 [2100], P('head')
- norms_grad: float32 [5, 410], replicated
- norms_newfirst: float32 [5, 410], replicated
- norms_newsecond: float32 [5, 410], replicated
- norms_newmaster: float32 [5, 410], replicated
- qkvr_copy: bfloat16 [4, 410, 410], P(None, None, 'head')
- proj_copy: bfloat16 [410, 410], P('head')
- expand_copy: bfloat16 [410, 2100], P(None, 'head')
- reduce_copy: bfloat16 [2100, 410], P('head')
The draws below stay inside these ranges and needn't reach their ends.
Inputs may be any that keep to these rules, and one draw needn't show every extreme that they name: `owners`: several tensors may share an owner.
All inputs are finite; a program needn't handle non-finite values.
Results may differ from the reference program's by a relative error of at most 0.02.
The reference program's roundings to bfloat16 on the way count: a program that leaves them out, or rounds other values in their place, can miss the bound.
Values may be sent and summed in bfloat16 or wider, within the bound.
No kernel may reach another device: no remote copies, remote signals or barrier semaphores. Data moves between devices by JAX's collectives and lax.ppermute only.
A program may use at most 384 MiB of HBM per device.

```python
import math
import jax
import jax.numpy as jnp
import numpy as np
from jax import lax

D = 410
H = 10
DH = 41
FF = 2100
HD = 410
SEG = 150
SEGS = 8
LEN = 1200
STREAMS = 64
TOKENS = 76800
NPAR = 7
STEP = 10
N_DP = 16


def set_ends(values, rng, smallest, high):
    shape = values.shape
    place = [jax.random.randint(jax.random.fold_in(rng, axis), (), 0, shape[axis]) for axis in range(len(shape))]
    values = values.at[tuple(place)].set(smallest)
    longest = shape.index(max(shape))
    place[longest] = (place[longest] + 1) % shape[longest]
    return values.at[tuple(place)].set(high)


def block_levels(rng, shape, split, low, high):
    level = 1.0
    for axis_at, parts in split:
        draws = jax.random.uniform(jax.random.fold_in(jax.random.fold_in(rng, 6), axis_at), (parts,), jnp.float32, low / len(split), high / len(split))
        level = level * jnp.repeat(jnp.exp(draws), shape[axis_at] // parts).reshape((-1,) + (1,) * (len(shape) - 1 - axis_at))
    return level


def cumulative_ranks(amount, slope):
    loads = [(1 << 20) // math.isqrt(standing ** slope) + 1 for standing in range(1, amount + 1)]
    deviation = 1 + sum(loads) // (1 << 30)
    return np.cumsum(np.array([max(1, weight // deviation) for weight in loads]))


def ranked(key, shape, count, slope):
    grid = cumulative_ranks(count, slope)
    pick = jax.random.randint(jax.random.fold_in(key, 1), shape, 0, int(grid[count - 1]))
    grade = jnp.searchsorted(jnp.asarray(grid, jnp.int32), pick, side="right")
    return jax.random.permutation(jax.random.fold_in(key, 2), count)[grade].astype(jnp.int32)


def gaussian(own_key, dims, deviation, most, cuts=(), kind=jnp.bfloat16):
    loudness = block_levels(own_key, dims, cuts, -0.22, 0.18) if cuts else 1.0
    drawn = jax.random.normal(own_key, dims, jnp.float32) * deviation * loudness
    return jnp.minimum(jnp.maximum(drawn, -most), most).astype(kind)


def setup_inputs(seed: int = 0) -> dict:
    splits = jax.random.split(jax.random.key(seed), 27)
    tokens = gaussian(splits[0], (TOKENS, D), 1.0, 6.0, ((0, 32),))
    prior_memory = gaussian(splits[1], (STREAMS, SEG, D), 1.0, 6.0, ((0, 16),))
    first_flags = set_ends(jax.random.randint(splits[2], (STREAMS,), 0, 2), jax.random.fold_in(splits[2], 1), 0, 1).astype(jnp.int32)
    owners = set_ends(ranked(splits[3], (NPAR,), N_DP, 2), jax.random.fold_in(splits[3], 3), 0, N_DP - 1).astype(jnp.int32)
    cotangent = gaussian(splits[4], (TOKENS, D), 1.0, 6.0, ((0, 32),), jnp.float32)
    qkvr_master = gaussian(splits[5], (4, D, HD), D ** -0.5, 0.3125, ((2, 2),), jnp.float32)
    qkvr_first = gaussian(splits[6], (4, D, HD), 0.01, 0.15625, ((2, 2),), jnp.float32)
    qkvr_second = jnp.clip(jnp.exp(math.log(0.0008) - 2.7725887 * jax.random.uniform(splits[7], (4, D, HD), jnp.float32) ** block_levels(splits[7], (4, D, HD), ((2, 2),), -0.2, 0.2)), 4.999999873689376e-05, 0.0008)
    proj_master = gaussian(splits[8], (HD, D), (max(HD // 64, 1)) ** -0.5, 2.5, ((0, 2),), jnp.float32)
    proj_first = gaussian(splits[9], (HD, D), 0.01, 0.15625, ((0, 2),), jnp.float32)
    proj_second = jnp.clip(jnp.exp(math.log(0.0008) - 2.7725887 * jax.random.uniform(splits[10], (HD, D), jnp.float32) ** block_levels(splits[10], (HD, D), ((0, 2),), -0.2, 0.2)), 4.999999873689376e-05, 0.0008)
    expand_master = gaussian(splits[11], (D, FF), D ** -0.5, 0.3125, ((1, 2),), jnp.float32)
    expand_first = gaussian(splits[12], (D, FF), 0.01, 0.15625, ((1, 2),), jnp.float32)
    expand_second = jnp.clip(jnp.exp(math.log(0.0008) - 2.7725887 * jax.random.uniform(splits[13], (D, FF), jnp.float32) ** block_levels(splits[13], (D, FF), ((1, 2),), -0.2, 0.2)), 4.999999873689376e-05, 0.0008)
    reduce_master = gaussian(splits[14], (FF, D), FF ** -0.5, 0.125, ((0, 2),), jnp.float32)
    reduce_first = gaussian(splits[15], (FF, D), 0.01, 0.15625, ((0, 2),), jnp.float32)
    reduce_second = jnp.clip(jnp.exp(math.log(0.0008) - 2.7725887 * jax.random.uniform(splits[16], (FF, D), jnp.float32) ** block_levels(splits[16], (FF, D), ((0, 2),), -0.2, 0.2)), 4.999999873689376e-05, 0.0008)
    headbias_master = gaussian(splits[17], (2, HD), 0.5, 3.0, ((1, 2),), jnp.float32)
    headbias_first = gaussian(splits[18], (2, HD), 0.01, 0.15625, ((1, 2),), jnp.float32)
    headbias_second = jnp.clip(jnp.exp(math.log(0.0008) - 2.7725887 * jax.random.uniform(splits[19], (2, HD), jnp.float32) ** block_levels(splits[19], (2, HD), ((1, 2),), -0.2, 0.2)), 4.999999873689376e-05, 0.0008)
    expbias_master = gaussian(splits[20], (FF,), 0.5, 3.0, ((0, 2),), jnp.float32)
    expbias_first = gaussian(splits[21], (FF,), 0.01, 0.15625, ((0, 2),), jnp.float32)
    expbias_second = jnp.clip(jnp.exp(math.log(0.0008) - 2.7725887 * jax.random.uniform(splits[22], (FF,), jnp.float32) ** block_levels(splits[22], (FF,), ((0, 2),), -0.2, 0.2)), 4.999999873689376e-05, 0.0008)
    norms_master = jnp.clip(jax.random.uniform(splits[23], (5, D), jnp.float32, 0.5, 1.5), 0.5, 1.5)
    norms_first = gaussian(splits[24], (5, D), 0.01, 0.15625, (), jnp.float32)
    norms_second = jnp.clip(jnp.exp(jax.random.uniform(splits[25], (5, D), jnp.float32, math.log(4.999999873689376e-05), math.log(0.0008))), 4.999999873689376e-05, 0.0008)
    return {"tokens": tokens, "prior_memory": prior_memory, "first_flags": first_flags, "owners": owners, "cotangent": cotangent, "qkvr_master": qkvr_master, "qkvr_first": qkvr_first, "qkvr_second": qkvr_second, "proj_master": proj_master, "proj_first": proj_first, "proj_second": proj_second, "expand_master": expand_master, "expand_first": expand_first, "expand_second": expand_second, "reduce_master": reduce_master, "reduce_first": reduce_first, "reduce_second": reduce_second, "headbias_master": headbias_master, "headbias_first": headbias_first, "headbias_second": headbias_second, "expbias_master": expbias_master, "expbias_first": expbias_first, "expbias_second": expbias_second, "norms_master": norms_master, "norms_first": norms_first, "norms_second": norms_second}


@jax.custom_vjp
def low(v):
    return lax.optimization_barrier(v.astype(jnp.bfloat16)).astype(jnp.float32)

@jax.custom_vjp
def low_back(v):
    return v

def low_keep(v):
    return (low(v), None)

def low_pass(kept, grad):
    return (grad,)

def back_keep(v):
    return (v, None)

def back_low(kept, grad):
    return (low(grad),)
low.defvjp(low_keep, low_pass)
low_back.defvjp(back_keep, back_low)
HIGHEST = lax.Precision.HIGHEST
NORM_EPS = 1e-05
CLIP_LEVEL = 0.01
BETA_ONE = 0.5
BETA_TWO = 0.5
ADAM_EPSILON = 1e-08
WEIGHT_DECAY = 0.1
STEP_RATES = (0.03, 0.2, 0.03, 0.015, 0.3, 0.3, 0.3)
GATE_COEF = 0.7978845608028654

def round_both(array_in):
    return low(low_back(array_in))

def matmul_high(first_op, second_op):
    return jnp.dot(first_op, second_op, precision=HIGHEST, preferred_element_type=jnp.float32)

def layer_norm(row_vals, norm_gain, norm_shift):
    center = row_vals - lax.optimization_barrier(jnp.mean(row_vals, axis=-1, keepdims=True))
    spread = lax.optimization_barrier(jnp.mean(center * center, axis=-1, keepdims=True))
    return center * lax.rsqrt(spread + NORM_EPS) * norm_gain + norm_shift

def smooth_gate(pre_act):
    return 0.5 * pre_act * (1.0 + jnp.tanh(GATE_COEF * (pre_act + 0.044715 * pre_act * pre_act * pre_act)))

def positions(key_len, model_width):
    distance = (key_len - 1 - jnp.arange(key_len)).astype(jnp.float32)
    frequency = jnp.exp(jnp.arange(model_width // 2).astype(jnp.float32) * (-2.0 * math.log(10000.0) / model_width))
    angles = distance[:, None] * frequency[None, :]
    return jnp.concatenate([jnp.sin(angles), jnp.cos(angles)], axis=1)

def rel_shift(scores):
    leading = scores.shape[:-2]
    query_len = scores.shape[-2]
    key_len = scores.shape[-1]
    padded = jnp.concatenate([jnp.zeros(leading + (query_len, 1), scores.dtype), scores], axis=-1)
    padded = padded.reshape(leading + (key_len + 1, query_len))
    return padded[..., 1:, :].reshape(scores.shape)

def forward(params, tokens_in, prior_in, flags_in):
    qkvr_all, proj_all, expand_all, reduce_all, headbias_all, expbias_all, norms_all = params
    query_low = low(qkvr_all[0])
    key_low = low(qkvr_all[1])
    value_low = low(qkvr_all[2])
    relw_low = low(qkvr_all[3])
    proj_low = low(proj_all)
    expand_low = low(expand_all)
    reduce_low = low(reduce_all)
    expbias_low = low(expbias_all)
    table = low(positions(2 * SEG, D))
    rel_keys = round_both(matmul_high(table, relw_low)).reshape(2 * SEG, H, DH)
    bias_u = headbias_all[0].reshape(H, DH)
    bias_v = headbias_all[1].reshape(H, DH)
    row_ids = jnp.arange(SEG)[:, None]
    col_ids = jnp.arange(2 * SEG)[None, :]
    causal = col_ids <= row_ids + SEG
    own_keys = col_ids >= SEG
    scale = 1.0 / math.sqrt(DH)

    def one_stream(stream_item):
        stream, memory, stream_flag = stream_item
        queries = round_both(matmul_high(stream, query_low)).reshape(SEGS, SEG, H, DH)
        keys = round_both(matmul_high(stream, key_low)).reshape(SEGS, SEG, H, DH)
        values = round_both(matmul_high(stream, value_low)).reshape(SEGS, SEG, H, DH)
        mem_keys = round_both(matmul_high(memory, key_low)).reshape(1, SEG, H, DH)
        mem_values = round_both(matmul_high(memory, value_low)).reshape(1, SEG, H, DH)
        key_cat = jnp.concatenate([jnp.concatenate([mem_keys, keys[:-1]], axis=0), keys], axis=1)
        value_cat = jnp.concatenate([jnp.concatenate([mem_values, values[:-1]], axis=0), values], axis=1)
        with_u = low(queries + bias_u)
        with_v = low(queries + bias_v)
        content = jnp.einsum('sihd,sjhd->shij', with_u, key_cat, precision=HIGHEST)
        position = rel_shift(jnp.einsum('sihd,jhd->shij', with_v, rel_keys, precision=HIGHEST))
        raw_scores = low_back(content + position)
        has_memory = (jnp.arange(SEGS) > 0) | (stream_flag == 1)
        allowed = causal[None, None] & (own_keys[None, None] | has_memory[:, None, None, None])
        scores = jnp.where(allowed, raw_scores * scale, -1e+30)
        row_peak = lax.optimization_barrier(jnp.max(scores, axis=-1, keepdims=True))
        expo_vals = jnp.exp(scores - row_peak)
        probs = low(expo_vals / lax.optimization_barrier(jnp.sum(expo_vals, axis=-1, keepdims=True)))
        attended = jnp.einsum('shij,sjhd->sihd', probs, value_cat, precision=HIGHEST)
        attended = round_both(attended.reshape(LEN, HD))
        attn = low_back(matmul_high(attended, proj_low))
        normed = layer_norm(stream + attn, norms_all[0], norms_all[1])
        pre_act = low_back(matmul_high(low(normed), expand_low)) + expbias_low
        act_low = low(smooth_gate(pre_act))
        second = normed + low_back(matmul_high(act_low, reduce_low)) + norms_all[2]
        return layer_norm(second, norms_all[3], norms_all[4])
    return lax.map(jax.checkpoint(one_stream), (tokens_in, prior_in, flags_in))

def adam_step(grad_in, first_in, second_in, master_in, clip_factor, step_rate):
    clipped = grad_in * clip_factor
    first_new = BETA_ONE * first_in + (1.0 - BETA_ONE) * clipped
    second_new = BETA_TWO * second_in + (1.0 - BETA_TWO) * clipped * clipped
    first_hat = first_new / (1.0 - BETA_ONE ** STEP)
    second_hat = second_new / (1.0 - BETA_TWO ** STEP)
    master_new = master_in - step_rate * (first_hat / (jnp.sqrt(second_hat) + ADAM_EPSILON) + WEIGHT_DECAY * master_in)
    return (clipped, first_new, second_new, master_new)

def clip_factors(squares, counts, owner_ids):
    same = (owner_ids[:, None] == owner_ids[None, :]).astype(jnp.float32)
    mean_sq = lax.optimization_barrier(jnp.sum(same * squares[None, :], axis=1)) / lax.optimization_barrier(jnp.sum(same * counts[None, :], axis=1))
    return (jnp.sqrt(mean_sq), jnp.minimum(1.0, CLIP_LEVEL * lax.rsqrt(mean_sq + 1e-06)))

def reference(tokens, prior_memory, first_flags, owners, cotangent, qkvr_master, qkvr_first, qkvr_second, proj_master, proj_first, proj_second, expand_master, expand_first, expand_second, reduce_master, reduce_first, reduce_second, headbias_master, headbias_first, headbias_second, expbias_master, expbias_first, expbias_second, norms_master, norms_first, norms_second):
    masters = (qkvr_master, proj_master, expand_master, reduce_master, headbias_master, expbias_master, norms_master)
    firsts = (qkvr_first, proj_first, expand_first, reduce_first, headbias_first, expbias_first, norms_first)
    seconds = (qkvr_second, proj_second, expand_second, reduce_second, headbias_second, expbias_second, norms_second)
    streams_in = tokens.astype(jnp.float32).reshape(STREAMS, LEN, D)
    prior_in = prior_memory.astype(jnp.float32)

    def forward_fn(params, tokens_in):
        return forward(params, tokens_in, prior_in, first_flags)
    outputs, pullback = jax.vjp(forward_fn, masters, streams_in)
    grads, token_grad = pullback(cotangent.reshape(STREAMS, LEN, D))
    squares = jnp.stack([jnp.sum(gradient * gradient) for gradient in grads])
    counts = jnp.array([float(gradient.size) for gradient in grads], jnp.float32)
    group_rms, clips = clip_factors(squares, counts, owners)
    res = [adam_step(grads[number], firsts[number], seconds[number], masters[number], clips[number], STEP_RATES[number]) for number in range(NPAR)]
    return (outputs.reshape(TOKENS, D), token_grad.reshape(TOKENS, D), group_rms, res[0][0], res[0][1], res[0][2], res[0][3], res[1][0], res[1][1], res[1][2], res[1][3], res[2][0], res[2][1], res[2][2], res[2][3], res[3][0], res[3][1], res[3][2], res[3][3], res[4][0], res[4][1], res[4][2], res[4][3], res[5][0], res[5][1], res[5][2], res[5][3], res[6][0], res[6][1], res[6][2], res[6][3], res[0][3].astype(jnp.bfloat16), res[1][3].astype(jnp.bfloat16), res[2][3].astype(jnp.bfloat16), res[3][3].astype(jnp.bfloat16))
```

```python
from jax.sharding import PartitionSpec as P
import math
import jax, jax.numpy as jnp
from jax import lax
from jax.experimental import pallas as pl
from jax.experimental.pallas import tpu as pltpu
BF=jnp.bfloat16; F32=jnp.float32
NT=(((1,),(1,)),((),())); TN=(((0,),(0,)),((),()))
def dot(a,b,dn=(((1,),(0,)),((),()))): return lax.dot_general(a,b,dn,preferred_element_type=F32)
SEG=150; NSEG=8; LEN=1200; DH=41; HG=5; CG=205; D=410
RA=96; RQ=160; KA_=256; KB_=384; KC=304
SCALE=1.0/math.sqrt(DH); LOG2E=1.4426950408889634

def fill_rows(x_ref, prior_ref, xs, xcat, xq):
    xs[0:SEG,:]=prior_ref[0].astype(F32)
    xs[SEG:SEG+LEN,:]=x_ref[...].astype(F32)
    xs[SEG+LEN:,:]=jnp.zeros((xs.shape[0]-SEG-LEN,D),F32)
    for s in range(NSEG):
        xcat[s]=xs[SEG*s:SEG*s+KC,:].astype(BF)
        xq[s]=xs[SEG*(s+1):SEG*(s+1)+RQ,:].astype(BF)

def head_masks(rows):
    lane=lax.broadcasted_iota(jnp.int32,(rows,CG),1)
    return [(lane>=DH*h)&(lane<DH*(h+1)) for h in range(HG)]

def ka_kernel(meta, x_ref, prior_ref, wq, wk, wv, relA, relB, bias, att_ref, p_ref, xs, xcat, xq, kbuf, vbuf, attS, biasA, biasB):
    n=pl.program_id(0); s=pl.program_id(1)
    @pl.when(s==0)
    def _():
        fill_rows(x_ref,prior_ref,xs,xcat,xq)
        kbuf[KC:,:]=jnp.zeros((KB_-KC,CG),BF)
        vbuf[KC:,:]=jnp.zeros((KB_-KC,CG),BF)
    has_mem=(s>0)|(meta[1+n]==1)
    jmin=jnp.where(has_mem,0,SEG)
    mem_b=jnp.where(has_mem,0.0,-1e30).astype(F32)
    @pl.when(s<2)
    def _():
        i=lax.broadcasted_iota(jnp.int32,(RA,128),0); j=lax.broadcasted_iota(jnp.int32,(RA,128),1)+128
        biasA[...]=jnp.where((j<=i+SEG)&(j>=jmin),0.0,-1e30)
        i=lax.broadcasted_iota(jnp.int32,(RQ-RA,KB_),0)+RA; j=lax.broadcasted_iota(jnp.int32,(RQ-RA,KB_),1)
        biasB[...]=jnp.where((j<=i+SEG)&(j>=jmin)&(j<2*SEG),0.0,-1e30)
    xc=xcat[s]
    kbuf[0:KC,:]=dot(xc,wk[...]).astype(BF)
    vbuf[0:KC,:]=dot(xc,wv[...]).astype(BF)
    q=dot(xq[s],wq[...]).astype(BF).astype(F32)
    wu=(q+bias[0:1,:]).astype(BF); wvv=(q+bias[1:2,:]).astype(BF)
    hm=head_masks(RQ)
    zero=jnp.zeros((),BF)
    wum=[jnp.where(m,wu,zero) for m in hm]
    wvm=[jnp.where(m,wvv,zero) for m in hm]
    NA=RA; NB=RQ-RA
    SA=dot(jnp.concatenate([w[0:RA] for w in wum],0),kbuf[0:KA_,:],NT)
    PA=dot(jnp.concatenate([w[0:RA] for w in wvm],0),relA[...],NT)
    SB=dot(jnp.concatenate([w[RA:] for w in wum],0),kbuf[...],NT)
    PB=dot(jnp.concatenate([w[RA:] for w in wvm],0),relB[...],NT)
    iA=lax.broadcasted_iota(jnp.int32,(RA,128),0); lA=lax.broadcasted_iota(jnp.int32,(RA,128),1)
    mA=(lA+(105-iA))<128
    iB=lax.broadcasted_iota(jnp.int32,(NB,128),0); lB=lax.broadcasted_iota(jnp.int32,(NB,128),1)
    mB=(lB+(69-iB))<128
    c=SCALE*LOG2E
    pas=[];pbs=[]
    for h in range(HG):
        pa=PA[NA*h:NA*(h+1)]; sa=SA[NA*h:NA*(h+1)]
        r0=pltpu.roll(pa[:,0:128],23,1,stride=1,stride_axis=0)
        r1=pltpu.roll(pa[:,128:256],23,1,stride=1,stride_axis=0)
        t0=(sa[:,0:128]+jnp.where(mA,r0,r1))*c+mem_b
        t1=(sa[:,128:256]+r1)*c+biasA[...]
        mx=jnp.max(jnp.maximum(t0,t1),axis=1,keepdims=True)
        e0=jnp.exp2(t0-mx); e1=jnp.exp2(t1-mx)
        li=1.0/jnp.sum(e0+e1,axis=1,keepdims=True)
        p=jnp.concatenate([(e0*li).astype(BF),(e1*li).astype(BF)],1)
        p_ref[0,0,h,0:RA,0:KA_]=p
        pas.append(p)
        pb=PB[NB*h:NB*(h+1)]; sb=SB[NB*h:NB*(h+1)]
        r0=pltpu.roll(pb[:,0:128],59,1,stride=1,stride_axis=0)
        r1=pltpu.roll(pb[:,128:256],59,1,stride=1,stride_axis=0)
        r2=pltpu.roll(pb[:,256:384],59,1,stride=1,stride_axis=0)
        t0=(sb[:,0:128]+jnp.where(mB,r0,r1))*c+biasB[:,0:128]
        t1=(sb[:,128:256]+jnp.where(mB,r1,r2))*c+biasB[:,128:256]
        t2=(sb[:,256:384]+r2)*c+biasB[:,256:384]
        mx=jnp.max(jnp.maximum(jnp.maximum(t0,t1),t2),axis=1,keepdims=True)
        e0=jnp.exp2(t0-mx); e1=jnp.exp2(t1-mx); e2=jnp.exp2(t2-mx)
        li=1.0/jnp.sum(e0+e1+e2,axis=1,keepdims=True)
        p=jnp.concatenate([(e0*li).astype(BF),(e1*li).astype(BF),(e2*li).astype(BF)],1)
        p_ref[0,0,h,RA:RQ,0:KB_]=p
        pbs.append(p)
    OA=dot(jnp.concatenate(pas,0),vbuf[0:KA_,:])
    OB=dot(jnp.concatenate(pbs,0),vbuf[...])
    hmA=[m[0:RA] for m in hm]; hmB=[m[RA:] for m in hm]
    aA=OA[0:NA]; aB=OB[0:NB]
    for h in range(1,HG):
        aA=jnp.where(hmA[h],OA[NA*h:NA*(h+1)],aA)
        aB=jnp.where(hmB[h],OB[NB*h:NB*(h+1)],aB)
    attS[s,0:RA,:]=aA
    attS[s,RA:RQ,:]=aB
    @pl.when(s==NSEG-1)
    def _():
        for t in range(NSEG):
            xs[SEG*t:SEG*t+152,0:CG]=attS[t,0:152,:]
        att_ref[...]=xs[0:LEN,0:CG].astype(BF)

def attention_fwd(meta,x,prior,wq,wk,wv,relA,relB,bias):
    cst=lambda *sh: pl.BlockSpec(sh,lambda n,s,m: (0,)*len(sh))
    gs=pltpu.PrefetchScalarGridSpec(num_scalar_prefetch=1,grid=(2,NSEG),
      in_specs=[pl.BlockSpec((LEN,D),lambda n,s,m:(n,0)),
        pl.BlockSpec((1,SEG,D),lambda n,s,m:(m[0]*2+n,0,0)),
        cst(D,CG),cst(D,CG),cst(D,CG),cst(KA_,CG),cst(KB_,CG),cst(2,CG)],
      out_specs=[pl.BlockSpec((LEN,CG),lambda n,s,m:(n,0)),
        pl.BlockSpec((1,1,HG,RQ,KB_),lambda n,s,m:(n,s,0,0,0))],
      scratch_shapes=[pltpu.VMEM((1376,D),F32),pltpu.VMEM((NSEG,KC,D),BF),pltpu.VMEM((NSEG,RQ,D),BF),
        pltpu.VMEM((KB_,CG),BF),pltpu.VMEM((KB_,CG),BF),pltpu.VMEM((NSEG,RQ,CG),F32),
        pltpu.VMEM((RA,128),F32),pltpu.VMEM((RQ-RA,KB_),F32)])
    return pl.pallas_call(ka_kernel,grid_spec=gs,name="attn_fwd",
      out_shape=[jax.ShapeDtypeStruct((2*LEN,CG),BF),jax.ShapeDtypeStruct((2,NSEG,HG,RQ,KB_),BF)],
      compiler_params=pltpu.CompilerParams(vmem_limit_bytes=56*2**20))(meta,x,prior,wq,wk,wv,relA,relB,bias)

NORM_EPS = 1e-05
CLIP_LEVEL = 0.01
BETA_ONE = 0.5
BETA_TWO = 0.5
ADAM_EPSILON = 1e-08
WEIGHT_DECAY = 0.1
STEP = 10
STEP_RATES = (0.03, 0.2, 0.03, 0.015, 0.3, 0.3, 0.3)
T=480; HF=1050
G0=0.7978845608028654; G1=0.044715; EPS=1e-5
def ln_fwd(z):
    m=jnp.mean(z,axis=-1,keepdims=True)
    c=z-m
    v=jnp.mean(c*c,axis=-1,keepdims=True)
    r=lax.rsqrt(v+EPS)
    return c*r,r
def ln_bwd(n,r,e):
    return r*(e-jnp.mean(e,axis=-1,keepdims=True)-n*jnp.mean(e*n,axis=-1,keepdims=True))
def kf_kernel(ao,at,x,ct,woo,wot,w1o,w1t,w2o,w2t,b1,nm, lo_ref,dres_ref,g_o,g_t,awo_o,awo_t,aw1_o,aw1_t,aw2_o,aw2_t,gnm_acc):
    i=pl.program_id(0); last=pl.num_programs(0)-1
    @pl.when(i==0)
    def _():
        for r in (awo_o,awo_t,aw1_o,aw1_t,aw2_o,aw2_t,gnm_acc): r[...]=jnp.zeros(r.shape,F32)
    attn=dot(ao[...],woo[...])+dot(at[...],wot[...])
    z=x[...].astype(F32)+attn
    n1,r1=ln_fwd(z)
    normed=n1*nm[0:1]+nm[1:2]
    nl=normed.astype(BF)
    def gate(pre):
        p2=pre*pre
        t=jnp.tanh(G0*pre*(1.0+G1*p2))
        hp=0.5*(1.0+t)
        act=pre*hp
        der=hp+0.5*pre*(1.0-t*t)*(G0*(1.0+3.0*G1*p2))
        return act.astype(BF),der
    acts=[];ders=[]
    second=normed+nm[2:3]
    for k,(w1,w2) in enumerate(((w1o,w2o),(w1t,w2t))):
        pre=dot(nl,w1[...])+b1[k:k+1]
        a,dd=gate(pre)
        acts.append(a);ders.append(dd)
        second=second+dot(a,w2[...])
    n2,r2=ln_fwd(second)
    lo_ref[...]=n2*nm[3:4]+nm[4:5]
    c=ct[...]
    d2=ln_bwd(n2,r2,c*nm[3:4])
    d2l=d2.astype(BF)
    dn=d2
    for k,(w1,w2,aw1,aw2) in enumerate(((w1o,w2o,aw1_o,aw2_o),(w1t,w2t,aw1_t,aw2_t))):
        aw2[0:D]+=dot(d2l,acts[k],TN)
        dpre=dot(d2l,w2[...],NT)*ders[k]
        aw1[D:D+1]+=jnp.sum(dpre,axis=0,keepdims=True)
        dpl=dpre.astype(BF)
        aw1[0:D]+=dot(nl,dpl,TN)
        dn=dn+dot(dpl,w1[...],NT)
    dz=ln_bwd(n1,r1,dn*nm[0:1])
    dres_ref[...]=dz
    dal=dz.astype(BF)
    awo_o[0:CG]+=dot(ao[...],dal,TN)
    awo_t[0:CG]+=dot(at[...],dal,TN)
    gnm=jnp.concatenate([jnp.sum(v,axis=0,keepdims=True) for v in (dn*n1,dn,d2,c*n2,c)],0)
    gnm_acc[0:5]+=gnm
    @pl.when(i==last)
    def _():
        for g,a1,a2,aw in ((g_o,aw1_o,aw2_o,awo_o),(g_t,aw1_t,aw2_t,awo_t)):
            a2[D:D+5,0:D]=gnm_acc[0:5]
            g[0:416]=a1[...].astype(BF)
            g[416:832]=a2[...].astype(BF)
            g[832:960]=jnp.zeros((128,HF),BF)
            g[832:936,0:D]=aw[0:104].astype(BF)
            g[832:936,512:512+D]=aw[104:208].astype(BF)
def ff(ao,at,x,ct,woo,wot,w1o,w1t,w2o,w2t,b1,nm):
    n=x.shape[0]
    row=lambda w: pl.BlockSpec((T,w),lambda i:(i,0))
    cst=lambda *sh: pl.BlockSpec(sh,lambda i:(0,)*len(sh))
    S=jax.ShapeDtypeStruct
    gs=[(960,HF),(960,HF)]
    spec=pl.GridSpec(grid=(n//T,),
      in_specs=[row(CG),row(CG),row(D),row(D),cst(CG,D),cst(CG,D),cst(D,HF),cst(D,HF),cst(HF,D),cst(HF,D),cst(2,HF),cst(5,D)],
      out_specs=[row(D),row(D)]+[cst(*s) for s in gs],
      scratch_shapes=[pltpu.VMEM((208,D),F32)]*2+[pltpu.VMEM((416,HF),F32)]*4+[pltpu.VMEM((8,D),F32)])
    return pl.pallas_call(kf_kernel,name="ff",grid_spec=spec,
      out_shape=[S((n,D),F32),S((n,D),F32)]+[S(s,BF) for s in gs],
      compiler_params=pltpu.CompilerParams(vmem_limit_bytes=60*2**20))(ao,at,x,ct,woo,wot,w1o,w1t,w2o,w2t,b1,nm)
HP=48; GP=HP*HG
def rev8(v):
    idx=7-lax.broadcasted_iota(jnp.int32,v.shape,0)
    return jnp.take_along_axis(v,idx,axis=0)
def unskew(blocks, base, rows):
    nb=len(blocks)
    lane=lax.broadcasted_iota(jnp.int32,(8,128),1); sub=lax.broadcasted_iota(jnp.int32,(8,128),0)
    outs=[[] for _ in blocks]
    for r in range(rows//8):
        sh=base-8*r-7
        rot=[pltpu.roll(rev8(b[8*r:8*r+8]),sh%128,1,stride=1,stride_axis=0) for b in blocks]
        m=lane<(sh+sub)
        for k in range(nb):
            if k==0: o=jnp.where(m,0.0,rot[0])
            else: o=jnp.where(m,rot[k-1],rot[k])
            outs[k].append(rev8(o))
    return [jnp.concatenate(o,0) for o in outs]

def kb_kernel(meta, x_ref, prior_ref, p_ref, dres_ref, base_ref, wq, wk, wv, wo, wqT, wkvT, woT, relA, relB, bias, biasT,
              ig_ref, dwq, dwk, dwv, drA, drB, dbias, xs, xcat, xq, dalS, kbuf, vbuf, ig, draw, dpos, G):
    n=pl.program_id(0); s=pl.program_id(1)
    NA=RA; NB=RQ-RA
    @pl.when((s==0)&(n==0))
    def _():
        for r in (dwq,dwk,dwv,drA,drB,dbias): r[...]=jnp.zeros(r.shape,F32)
        kbuf[KC:,:]=jnp.zeros((KB_-KC,CG),BF)
        vbuf[KC:,:]=jnp.zeros((KB_-KC,CG),BF)
    @pl.when(s==0)
    def _():
        xs[LEN:,:]=jnp.zeros((xs.shape[0]-LEN,D),F32)
        xs[0:LEN,:]=dres_ref[...]
        rows=lax.broadcasted_iota(jnp.int32,(RQ,D),0)
        for t in range(NSEG):
            dalS[t]=jnp.where(rows<SEG,xs[SEG*t:SEG*t+RQ,:],0.0).astype(BF)
        fill_rows(x_ref,prior_ref,xs,xcat,xq)
        xs[SEG:SEG+LEN,:]=base_ref[...]
        for t in range(NSEG+1):
            ig[t]=xs[SEG*t:SEG*t+152,:]
    xc=xcat[s]; xqs=xq[s]; dal=dalS[s]
    kbuf[0:KC,:]=dot(xc,wk[...]).astype(BF)
    vbuf[0:KC,:]=dot(xc,wv[...]).astype(BF)
    qT=dot(wqT[...],xqs,NT).astype(BF).astype(F32)
    wuT=(qT+biasT[:,0:1]).astype(BF); wvT=(qT+biasT[:,1:2]).astype(BF)
    da=dot(dal,wo[...],NT).astype(BF)
    daT=dot(woT[...],dal,NT).astype(BF)
    hm=head_masks(RQ)
    zero=jnp.zeros((),BF)
    dam=[jnp.where(m,da,zero) for m in hm]
    DA=dot(jnp.concatenate([w[0:RA] for w in dam],0),vbuf[0:KA_,:],NT)
    DB=dot(jnp.concatenate([w[RA:] for w in dam],0),vbuf[...],NT)
    dkT=[];dvT=[]
    for h in range(HG):
        pa=p_ref[0,0,h,0:RA,0:KA_]; pb=p_ref[0,0,h,RA:RQ,:]
        pf=pa.astype(F32); dp=DA[NA*h:NA*(h+1)]
        w=dp*pf
        delta=jnp.sum(w[:,0:128]+w[:,128:256],axis=1,keepdims=True)
        dr=(pf*SCALE)*(dp-delta)
        draw[h,0:RA,0:KA_]=dr.astype(BF)
        o=unskew([dr[:,0:128],dr[:,128:256]],105,RA)
        dpos[h,0:RA,0:KA_]=jnp.concatenate([v.astype(BF) for v in o],1)
        pf=pb.astype(F32); dp=DB[NB*h:NB*(h+1)]
        w=dp*pf
        delta=jnp.sum(w[:,0:128]+w[:,128:256]+w[:,256:384],axis=1,keepdims=True)
        dr=(pf*SCALE)*(dp-delta)
        draw[h,RA:RQ,0:KB_]=dr.astype(BF)
        o=unskew([dr[:,0:128],dr[:,128:256],dr[:,256:384]],69,NB)
        dpos[h,RA:RQ,0:KB_]=jnp.concatenate([v.astype(BF) for v in o],1)
        u_=wuT[HP*h:HP*(h+1)]; v_=wvT[HP*h:HP*(h+1)]; d_=daT[HP*h:HP*(h+1)]
        k1=dot(u_,draw[h,:,0:KA_]); k2=dot(u_[:,RA:],draw[h,RA:RQ,KA_:KB_])
        dkT.append(jnp.concatenate([k1,k2],1))
        v1=dot(d_,p_ref[0,0,h,:,0:KA_]); v2=dot(d_[:,RA:],p_ref[0,0,h,RA:RQ,KA_:KB_])
        dvT.append(jnp.concatenate([v1,v2],1))
        drA[HP*h:HP*(h+1)]+=dot(v_[:,0:RA],dpos[h,0:RA,0:KA_])
        drB[HP*h:HP*(h+1)]+=dot(v_[:,RA:],dpos[h,RA:RQ,:])
    def comb(buf,rA,rB):
        OA=dot(jnp.concatenate([buf[h,0:RA,0:KA_] for h in range(HG)],0),rA)
        OB=dot(jnp.concatenate([buf[h,RA:RQ,:] for h in range(HG)],0),rB)
        aA=OA[0:NA]; aB=OB[0:NB]
        for h in range(1,HG):
            aA=jnp.where(hm[h][0:RA],OA[NA*h:NA*(h+1)],aA)
            aB=jnp.where(hm[h][RA:],OB[NB*h:NB*(h+1)],aB)
        return aA,aB
    uA,uB=comb(draw,kbuf[0:KA_,:],kbuf[...])
    vA,vB=comb(dpos,relA[...],relB[...])
    dbias[0:1]+=jnp.sum(uA,0,keepdims=True)+jnp.sum(uB,0,keepdims=True)
    dbias[1:2]+=jnp.sum(vA,0,keepdims=True)+jnp.sum(vB,0,keepdims=True)
    dq=jnp.concatenate([(uA+vA).astype(BF),(uB+vB).astype(BF)],0)
    dk=jnp.concatenate(dkT,0).astype(BF); dv=jnp.concatenate(dvT,0).astype(BF)
    dwq[...]+=dot(dq,xqs,TN)
    dwk[...]+=dot(dk[:,0:KC],xc)
    dwv[...]+=dot(dv[:,0:KC],xc)
    kv=jnp.concatenate([dk[:,0:KC],dv[:,0:KC]],0)
    G[...]=dot(kv,wkvT[...],TN)
    ig[s+1]+=dot(dq,wq[...],NT)[0:152]+G[SEG:SEG+152,:]
    ig[s]+=G[0:152,:]
    @pl.when(s==NSEG-1)
    def _():
        for t in range(NSEG):
            xs[SEG*t:SEG*t+152,:]=ig[t+1]
        ig_ref[...]=xs[0:LEN,:]

def attention_bwd(streams,meta,x,prior,p,dres,base,wq,wk,wv,wo,wqT,wkvT,woT,relA,relB,bias,biasT):
    cst=lambda *sh: pl.BlockSpec(sh,lambda n,s,m: (0,)*len(sh))
    off=streams[0]; ns=len(streams)
    row=lambda w: pl.BlockSpec((LEN,w),lambda n,s,m:(n+off,0))
    own=lambda w: pl.BlockSpec((LEN,w),lambda n,s,m:(n,0))
    S=jax.ShapeDtypeStruct
    gs=pltpu.PrefetchScalarGridSpec(num_scalar_prefetch=1,grid=(ns,NSEG),
      in_specs=[row(D),pl.BlockSpec((1,SEG,D),lambda n,s,m:(m[0]*2+n+off,0,0)),
        pl.BlockSpec((1,1,HG,RQ,KB_),lambda n,s,m:(n+off,s,0,0,0)),row(D),row(D),
        cst(D,CG),cst(D,CG),cst(D,CG),cst(CG,D),cst(GP,D),cst(2*GP,D),cst(GP,D),cst(KA_,CG),cst(KB_,CG),cst(2,CG),cst(GP,2)],
      out_specs=[own(D),cst(CG,D),cst(GP,D),cst(GP,D),cst(GP,KA_),cst(GP,KB_),cst(2,CG)],
      scratch_shapes=[pltpu.VMEM((1376,D),F32),pltpu.VMEM((NSEG,KC,D),BF),pltpu.VMEM((NSEG,RQ,D),BF),pltpu.VMEM((NSEG,RQ,D),BF),
        pltpu.VMEM((KB_,CG),BF),pltpu.VMEM((KB_,CG),BF),pltpu.VMEM((NSEG+1,152,D),F32),
        pltpu.VMEM((HG,RQ,KB_),BF),pltpu.VMEM((HG,RQ,KB_),BF),pltpu.VMEM((KC,D),F32)])
    return pl.pallas_call(kb_kernel,grid_spec=gs,name="attn_bwd",
      out_shape=[S((ns*LEN,D),F32),S((CG,D),F32),S((GP,D),F32),S((GP,D),F32),S((GP,KA_),F32),S((GP,KB_),F32),S((2,CG),F32)],
      compiler_params=pltpu.CompilerParams(vmem_limit_bytes=60*2**20))(meta,x,prior,p,dres,base,wq,wk,wv,wo,wqT,wkvT,woT,relA,relB,bias,biasT)

def pad_heads(wT):
    return jnp.pad(wT.reshape(HG,DH,-1),((0,0),(0,HP-DH),(0,0))).reshape(GP,-1)
def unpad_heads(g):
    return g.reshape(HG,HP,-1)[:,:DH].reshape(CG,-1)
def positions(key_len, model_width):
    distance = (key_len - 1 - jnp.arange(key_len)).astype(jnp.float32)
    frequency = jnp.exp(
        jnp.arange(model_width // 2).astype(jnp.float32) * (-2.0 * math.log(10000.0) / model_width)
    )
    angles = distance[:, None] * frequency[None, :]
    return jnp.concatenate([jnp.sin(angles), jnp.cos(angles)], axis=1)


def adam_step(grad_in, first_in, second_in, master_in, clip_factor, step_rate):
    clipped = grad_in * clip_factor
    first_new = BETA_ONE * first_in + (1.0 - BETA_ONE) * clipped
    second_new = BETA_TWO * second_in + (1.0 - BETA_TWO) * clipped * clipped
    first_hat = first_new / (1.0 - BETA_ONE**STEP)
    second_hat = second_new / (1.0 - BETA_TWO**STEP)
    master_new = master_in - step_rate * (
        first_hat / (jnp.sqrt(second_hat) + ADAM_EPSILON) + WEIGHT_DECAY * master_in
    )
    return (clipped, first_new, second_new, master_new)


def clip_factors(squares, counts, owner_ids):
    same = (owner_ids[:, None] == owner_ids[None, :]).astype(jnp.float32)
    mean_sq = jnp.sum(same * squares[None, :], axis=1) / jnp.sum(same * counts[None, :], axis=1)
    return (jnp.sqrt(mean_sq), jnp.minimum(1.0, CLIP_LEVEL * lax.rsqrt(mean_sq + 1e-06)))


def shards(
    tokens,
    prior_memory,
    first_flags,
    owners,
    cotangent,
    qkvr_master,
    qkvr_first,
    qkvr_second,
    proj_master,
    proj_first,
    proj_second,
    expand_master,
    expand_first,
    expand_second,
    reduce_master,
    reduce_first,
    reduce_second,
    headbias_master,
    headbias_first,
    headbias_second,
    expbias_master,
    expbias_first,
    expbias_second,
    norms_master,
    norms_first,
    norms_second,
):
    heads_count = lax.axis_size("head")
    head = lax.axis_index("head")
    swap = [(h, heads_count - 1 - h) for h in range(heads_count)]
    def other(v):
        return lax.ppermute(v, "head", swap)
    qkvr_own = qkvr_master.astype(BF)
    wo_own = proj_master.astype(BF)
    w1_own = expand_master.astype(BF)
    w2_own = reduce_master.astype(BF)
    b1_own = expbias_master.astype(BF).astype(F32)
    qkvr_oth = other(qkvr_own)
    small = other(jnp.concatenate([headbias_master.reshape(-1), b1_own]))
    wo_oth = other(wo_own)
    w1_oth = other(w1_own)
    w2_oth = other(w2_own)
    hb_oth = small[:2 * CG].reshape(2, CG)
    b1_oth = small[2 * CG:]
    meta = jnp.concatenate([head[None].astype(jnp.int32), lax.dynamic_slice_in_dim(first_flags, head * 2, 2, 0)])
    table = positions(2 * SEG, D).astype(BF)
    def rels(wr):
        rel = jnp.dot(table, wr, preferred_element_type=F32).astype(BF)
        return rel[44:300], jnp.pad(rel, ((16, 68), (0, 0)))
    groups = []
    for w, hb, wo in ((qkvr_own, headbias_master, wo_own), (qkvr_oth, hb_oth, wo_oth)):
        rA, rB = rels(w[3])
        groups.append((w, hb, wo, rA, rB))
    fw = [attention_fwd(meta, tokens, prior_memory, w[0], w[1], w[2], rA, rB, hb) for w, hb, wo, rA, rB in groups]
    layer_output, dres, ff_own, ff_oth = ff(
        fw[0][0], fw[1][0], tokens, cotangent, wo_own, wo_oth, w1_own, w1_oth, w2_own, w2_oth,
        jnp.stack([b1_own, b1_oth]), norms_master)
    n_dp = lax.axis_size("dp")
    dp = lax.axis_index("dp")
    def half_sum(own, oth):
        return own.astype(F32) + other(oth).astype(F32)
    def sum_dp(x):
        n = lax.axis_size("dp")
        me = lax.axis_index("dp")
        b = 1
        while b < n:
            half = x.shape[0] // 2
            up = (me & b) != 0
            send = jnp.where(up, x[:half], x[half:])
            keep = jnp.where(up, x[half:], x[:half])
            got = lax.ppermute(send, "dp", [(i, i ^ b) for i in range(n)])
            x = (keep.astype(F32) + got.astype(F32)).astype(BF)
            b *= 2
        while b > 1:
            b //= 2
            got = lax.ppermute(x, "dp", [(i, i ^ b) for i in range(n)])
            up = (me & b) != 0
            x = jnp.where(up, jnp.concatenate([got, x], 0), jnp.concatenate([x, got], 0))
        return x
    ff_got = other(ff_oth)
    def back(streams, group, p, base):
        w, hb, wo, rA, rB = group
        ph = pad_heads
        ig, dwq, dwk, dwv, drA, drB, db = attention_bwd(streams, meta, tokens, prior_memory, p, dres, base, w[0], w[1], w[2], wo,
            ph(w[0].T), jnp.concatenate([ph(w[1].T), ph(w[2].T)]), ph(wo), rA, rB, hb, ph(hb.T))
        return ig, (dwq, dwk, dwv, drA, drB, db)
    def payload(dwq, dwk, dwv, drA, drB, db):
        dr = unpad_heads(drB[:, 16:316]) + jnp.pad(unpad_heads(drA), ((0, 0), (44, 0)))
        dwr = jnp.dot(dr.astype(BF), table, preferred_element_type=F32)
        return jnp.concatenate([dwq, unpad_heads(dwk), unpad_heads(dwv), dwr, db.reshape(1, D), jnp.zeros((11, D), F32)], 0)
    ig, g_oth = back((0, 1), groups[1], fw[1][1], dres)
    ff_got, g_oth, ig = lax.optimization_barrier((ff_got, g_oth, ig))
    at_got = other(payload(*g_oth).astype(BF))
    chunk = ff_own.shape[0] // n_dp
    half = (ff_own.astype(F32) + ff_got.astype(F32)).astype(BF).reshape(n_dp // 2, 2, chunk, HF)
    odd = (dp & 1) == 1
    send = jnp.where(odd, half[:, 0], half[:, 1])
    keep = jnp.where(odd, half[:, 1], half[:, 0])
    got = lax.ppermute(send, "dp", [(i, i ^ 1) for i in range(n_dp)])
    pair = (keep.astype(F32) + got.astype(F32)).astype(BF)
    pair, ig = lax.optimization_barrier((pair, ig))
    split = lax.all_to_all(pair, "dp", 0, 0, tiled=True, axis_index_groups=[list(range(c, n_dp, 2)) for c in range(2)])
    ig0, g0 = back((0,), groups[0], fw[0][1], ig)
    part = jnp.sum(split.astype(F32), 0).astype(BF)
    part, ig = lax.optimization_barrier((part, ig))
    ff_sum = lax.all_gather(part, "dp", axis=0, tiled=True).astype(F32)
    ig1, g1 = back((1,), groups[0], fw[0][1], ig)
    at_got, ig1, g1 = lax.optimization_barrier((at_got, ig1, g1))
    input_grad = jnp.concatenate([ig0, ig1], 0)
    at_own = payload(*[a + b for a, b in zip(g0, g1)])
    at_half = (at_own + at_got.astype(F32)).astype(BF)
    at_sum = sum_dp(at_half).astype(F32)
    expand_grad = ff_sum[:D]
    expbias_grad = ff_sum[D]
    reduce_grad = ff_sum[416:416 + D].T
    norms_grad = ff_sum[416 + D:416 + D + 5, :D]
    proj_grad = jnp.concatenate([ff_sum[832:936, :D], ff_sum[832:936, 512:512 + D]], 0)[:CG]
    qkvr_grad = jnp.transpose(at_sum[:4 * CG].reshape(4, CG, D), (0, 2, 1))
    headbias_grad = at_sum[4 * CG].reshape(2, CG)
    grads = (
        qkvr_grad,
        proj_grad,
        expand_grad,
        reduce_grad,
        headbias_grad,
        expbias_grad,
        norms_grad,
    )
    masters = (
        qkvr_master,
        proj_master,
        expand_master,
        reduce_master,
        headbias_master,
        expbias_master,
        norms_master,
    )
    firsts = (
        qkvr_first,
        proj_first,
        expand_first,
        reduce_first,
        headbias_first,
        expbias_first,
        norms_first,
    )
    seconds = (
        qkvr_second,
        proj_second,
        expand_second,
        reduce_second,
        headbias_second,
        expbias_second,
        norms_second,
    )
    shard_squares = jnp.stack([jnp.sum(gradient * gradient) for gradient in grads[:6]])
    shard_squares = shard_squares + other(shard_squares)
    squares = jnp.concatenate([shard_squares, jnp.sum(norms_grad * norms_grad)[None]])
    counts = jnp.array(
        [float(gradient.size * heads_count) for gradient in grads[:6]] + [float(norms_grad.size)],
        jnp.float32,
    )
    group_rms, clips = clip_factors(squares, counts, owners)
    res = [
        adam_step(
            grads[number],
            firsts[number],
            seconds[number],
            masters[number],
            clips[number],
            STEP_RATES[number],
        )
        for number in range(7)
    ]
    return (
        layer_output,
        input_grad,
        group_rms,
        res[0][0],
        res[0][1],
        res[0][2],
        res[0][3],
        res[1][0],
        res[1][1],
        res[1][2],
        res[1][3],
        res[2][0],
        res[2][1],
        res[2][2],
        res[2][3],
        res[3][0],
        res[3][1],
        res[3][2],
        res[3][3],
        res[4][0],
        res[4][1],
        res[4][2],
        res[4][3],
        res[5][0],
        res[5][1],
        res[5][2],
        res[5][3],
        res[6][0],
        res[6][1],
        res[6][2],
        res[6][3],
        res[0][3].astype(jnp.bfloat16),
        res[1][3].astype(jnp.bfloat16),
        res[2][3].astype(jnp.bfloat16),
        res[3][3].astype(jnp.bfloat16),
    )


def solution(mesh):
    in_specs = (
        P(("dp", "head"), None),
        P("dp", None, None),
        P("dp"),
        P(),
        P(("dp", "head"), None),
        P(None, None, "head"),
        P(None, None, "head"),
        P(None, None, "head"),
        P("head", None),
        P("head", None),
        P("head", None),
        P(None, "head"),
        P(None, "head"),
        P(None, "head"),
        P("head", None),
        P("head", None),
        P("head", None),
        P(None, "head"),
        P(None, "head"),
        P(None, "head"),
        P("head"),
        P("head"),
        P("head"),
        P(),
        P(),
        P(),
    )
    out_specs = (
        P(("dp", "head"), None),
        P(("dp", "head"), None),
        P(),
        P(None, None, "head"),
        P(None, None, "head"),
        P(None, None, "head"),
        P(None, None, "head"),
        P("head", None),
        P("head", None),
        P("head", None),
        P("head", None),
        P(None, "head"),
        P(None, "head"),
        P(None, "head"),
        P(None, "head"),
        P("head", None),
        P("head", None),
        P("head", None),
        P("head", None),
        P(None, "head"),
        P(None, "head"),
        P(None, "head"),
        P(None, "head"),
        P("head"),
        P("head"),
        P("head"),
        P("head"),
        P(),
        P(),
        P(),
        P(),
        P(None, None, "head"),
        P("head", None),
        P(None, "head"),
        P("head", None),
    )
    return jax.shard_map(shards, mesh=mesh, in_specs=in_specs, out_specs=out_specs, check_vma=False)
```

```python
from jax.sharding import PartitionSpec as P
import math, functools
import jax, jax.numpy as jnp
from jax import lax
from jax.experimental import pallas as pl
from jax.experimental.pallas import tpu as pltpu
BF=jnp.bfloat16; F32=jnp.float32
NT=(((1,),(1,)),((),())); TN=(((0,),(0,)),((),()))
def dot(a,b,dn=(((1,),(0,)),((),()))): return lax.dot_general(a,b,dn,preferred_element_type=F32)
SEG=150; NSEG=8; LEN=1200; DH=41; HG=5; CG=205; D=410
RA=96; RQ=160; KA_=256; KB_=384; KC=304
HP=48; GP=HP*HG
SCALE=1.0/math.sqrt(DH); LOG2E=1.4426950408889634

def fill_rows(x_rows, prior_ref, xs, xcat, xq):
    xs[0:SEG,:]=prior_ref[0].astype(F32)
    xs[SEG:SEG+LEN,:]=x_rows.astype(F32)
    xs[SEG+LEN:1376,:]=jnp.zeros((1376-SEG-LEN,D),F32)
    for s in range(NSEG):
        xcat[s]=xs[SEG*s:SEG*s+KC,:].astype(BF)
        xq[s]=xs[SEG*(s+1):SEG*(s+1)+RQ,:].astype(BF)

def head_masks(rows):
    lane=lax.broadcasted_iota(jnp.int32,(rows,CG),1)
    return [(lane>=DH*h)&(lane<DH*(h+1)) for h in range(HG)]

U=2
GU=4
WR=416; WC=256
def ka_kernel(first, meta, x_ref, prior_ref, w4p, wo, tab, bias, att_ref, p_ref, wT_ref, rel_ref, bT_ref, *rest):
    if first: xn_ref, xs, xcat, xq, attS, biasA, biasB = rest
    else: xs, xcat, xq, attS, biasA, biasB = rest
    w4=[w4p[k,0:D,0:CG] for k in range(4)]
    n=pl.program_id(0); st=pl.program_id(1)
    @pl.when((st==0)&(n==0))
    def _():
        rel_ref[...]=dot(tab[...],w4[3]).astype(BF)
        xs[0:GP,:]=jnp.zeros((GP,D),F32)
        for k in range(4):
            src=w4[k].astype(F32).T if k<3 else wo[...].astype(F32)
            for h in range(HG): xs[HP*h:HP*h+DH,:]=src[DH*h:DH*h+DH]
            wT_ref[k]=xs[0:GP,:].astype(BF)
        bt=jnp.concatenate([bias[...],jnp.zeros((6,CG),F32)],0).T
        xs[0:GP,0:8]=jnp.zeros((GP,8),F32)
        for h in range(HG): xs[HP*h:HP*h+DH,0:8]=bt[DH*h:DH*h+DH]
        bT_ref[...]=xs[0:GP,0:8]
    @pl.when(st==0)
    def _():
        if first:
            @pl.when(n==0)
            def _():
                tiles=2*LEN//128
                for t in range(tiles): xn_ref[128*t:128*t+128,:]=x_ref[:,128*t:128*t+128].T
                xn_ref[128*tiles:,:]=x_ref[:,128*tiles:].T
            fill_rows(xn_ref[pl.ds(pl.multiple_of(n*LEN,16),LEN),:],prior_ref,xs,xcat,xq)
        else: fill_rows(x_ref[...],prior_ref,xs,xcat,xq)
    NA=RA; NB=RQ-RA
    has_mem=(st>0)|(meta[1+n]==1)
    jmin=jnp.where(has_mem,0,SEG)
    @pl.when(st==0)
    def _():
        for u in range(U):
            jm=jmin if u==0 else 0
            i=lax.broadcasted_iota(jnp.int32,(RA,KA_),0); j=lax.broadcasted_iota(jnp.int32,(RA,KA_),1)
            biasA[u]=jnp.where((j<=i+SEG)&(j>=jm),0.0,-1e30)
            i=lax.broadcasted_iota(jnp.int32,(NB,KB_),0)+RA; j=lax.broadcasted_iota(jnp.int32,(NB,KB_),1)
            biasB[u]=jnp.where((j<=i+SEG)&(j>=jm)&(j<2*SEG),0.0,-1e30)
    @pl.when(st==1)
    def _():
        biasA[0]=biasA[1]; biasB[0]=biasB[1]
    hm=head_masks(RQ)
    hmA=[m[0:RA] for m in hm]; hmB=[m[RA:] for m in hm]
    zero=jnp.zeros((),BF)
    iA=lax.broadcasted_iota(jnp.int32,(RA,128),0); lA=lax.broadcasted_iota(jnp.int32,(RA,128),1)
    mA=(lA+(105-iA))<128
    iB=lax.broadcasted_iota(jnp.int32,(NB,128),0); lB=lax.broadcasted_iota(jnp.int32,(NB,128),1)
    mB=(lB+(69-iB))<128
    c=SCALE*LOG2E
    vv=[None]*U
    def scores(u):
        s=st*U+u
        xc=xcat[s]
        zr=jnp.zeros((KB_-KC,CG),BF)
        kk=jnp.concatenate([dot(xc,w4[1]).astype(BF),zr],0)
        vv[u]=jnp.concatenate([dot(xc,w4[2]).astype(BF),zr],0)
        q=dot(xq[s],w4[0]).astype(BF).astype(F32)
        wu=(q+bias[0:1,:]).astype(BF); wvv=(q+bias[1:2,:]).astype(BF)
        wum=[jnp.where(m,wu,zero) for m in hm]
        wvm=[jnp.where(m,wvv,zero) for m in hm]
        SA=dot(jnp.concatenate([w[0:RA] for w in wum],0),kk[0:KA_],NT)
        PA=dot(jnp.concatenate([w[0:RA] for w in wvm],0),rel_ref[0:KA_],NT)
        SB=dot(jnp.concatenate([w[RA:] for w in wum],0),kk,NT)
        PB=dot(jnp.concatenate([w[RA:] for w in wvm],0),rel_ref[KA_:],NT)
        return SA,PA,SB,PB
    def soft(u,sc):
        SA,PA,SB,PB=sc
        units=[]
        for h in range(HG):
            units.append((h,SA,PA,NA,2,0,23,biasA,mA)); units.append((h,SB,PB,NB,3,RA,59,biasB,mB))
        out=[]
        for i0 in range(0,len(units),GU):
            grp=units[i0:i0+GU]
            rolls=[[pltpu.roll(P_[R*h:R*h+R,128*k:128*k+128],b0,1,stride=1,stride_axis=0) for k in range(nt)] for (h,S_,P_,R,nt,r0,b0,bs,m) in grp]
            ts=[]
            for (h,S_,P_,R,nt,r0,b0,bs,m),rr in zip(grp,rolls):
                ts.append([(S_[R*h:R*h+R,128*k:128*k+128]+(jnp.where(m,rr[k],rr[k+1]) if k+1<nt else rr[k]))*c+bs[u,:,128*k:128*k+128] for k in range(nt)])
            mxs=[]
            for t in ts:
                mx=t[0]
                for v in t[1:]: mx=jnp.maximum(mx,v)
                mxs.append(mx)
            mxs=[jnp.max(v,axis=1,keepdims=True) for v in mxs]
            es=[[jnp.exp2(v-mx) for v in t] for t,mx in zip(ts,mxs)]
            sms=[]
            for e in es:
                sm=e[0]
                for v in e[1:]: sm=sm+v
                sms.append(sm)
            lis=[1.0/jnp.sum(v,axis=1,keepdims=True) for v in sms]
            for (h,S_,P_,R,nt,r0,b0,bs,m),e,li in zip(grp,es,lis):
                p=jnp.concatenate([(v*li).astype(BF) for v in e],1)
                late.append((u,h,r0,R,nt,p))
                out.append(p)
        return out[0::2],out[1::2]
    def outp(u,pp):
        pas,pbs=pp
        s=st*U+u
        OA=dot(jnp.concatenate(pas,0),vv[u][0:KA_])
        OB=dot(jnp.concatenate(pbs,0),vv[u])
        aA=OA[0:NA]; aB=OB[0:NB]
        for h in range(1,HG):
            aA=jnp.where(hmA[h],OA[NA*h:NA*(h+1)],aA)
            aB=jnp.where(hmB[h],OB[NB*h:NB*(h+1)],aB)
        lateA.append((s,aA,aB))
    sc=[None]*U; pp=[None]*U; late=[]; lateA=[]
    sc[0]=scores(0)
    for u in range(U):
        if u+1<U: sc[u+1]=scores(u+1)
        pp[u]=soft(u,sc[u])
        if u>0: outp(u-1,pp[u-1])
    outp(U-1,pp[U-1])
    for (u,h,r0,R,nt,p) in late: p_ref[0,u,h,r0:r0+R,0:128*nt]=p
    for (s,aA,aB) in lateA:
        attS[s,0:RA,:]=aA
        attS[s,RA:RQ,:]=aB
    @pl.when(st==NSEG//U-1)
    def _():
        for t in range(NSEG):
            xs[SEG*t:SEG*t+152,0:CG]=attS[t,0:152,:]
        att_ref[...]=xs[0:LEN,0:CG].astype(BF)

def attention_fwd(first,meta,x,prior,w4,wo,tab,bias):
    cst=lambda *sh: pl.BlockSpec(sh,lambda n,s,m: (0,)*len(sh))
    S=jax.ShapeDtypeStruct
    gs=pltpu.PrefetchScalarGridSpec(num_scalar_prefetch=1,grid=(2,NSEG//U),
      in_specs=[cst(D,2*LEN) if first else pl.BlockSpec((LEN,D),lambda n,s,m:(n,0)),
        pl.BlockSpec((1,SEG,D),lambda n,s,m:(m[0]*2+n,0,0)),
        cst(4,WR,WC),cst(CG,D),cst(KA_+KB_,D),cst(2,CG)],
      out_specs=[pl.BlockSpec((LEN,CG),lambda n,s,m:(n,0)),
        pl.BlockSpec((1,U,HG,RQ,KB_),lambda n,s,m:(n,s,0,0,0)),cst(4,GP,D),cst(KA_+KB_,CG),cst(GP,8)]+([cst(2*LEN,D)] if first else []),
      scratch_shapes=[pltpu.VMEM((1376,D),F32),pltpu.VMEM((NSEG,KC,D),BF),pltpu.VMEM((NSEG,RQ,D),BF),
        pltpu.VMEM((NSEG,RQ,CG),F32),
        pltpu.VMEM((U,RA,KA_),F32),pltpu.VMEM((U,RQ-RA,KB_),F32)])
    return pl.pallas_call(functools.partial(ka_kernel,first),grid_spec=gs,name="attn_fwd",
      out_shape=[S((2*LEN,CG),BF),S((2,NSEG,HG,RQ,KB_),BF),S((4,GP,D),BF),S((KA_+KB_,CG),BF),S((GP,8),F32)]+([S((2*LEN,D),BF)] if first else []),
      compiler_params=pltpu.CompilerParams(vmem_limit_bytes=56*2**20))(meta,x,prior,w4,wo,tab,bias)

CLIP_LEVEL = 0.01
BETA_ONE = 0.5
BETA_TWO = 0.5
ADAM_EPSILON = 1e-08
WEIGHT_DECAY = 0.1
STEP = 10
STEP_RATES = (0.03, 0.2, 0.03, 0.015, 0.3, 0.3, 0.3)
T=480; HF=1050; HFP=1152
G0=0.7978845608028654; G1=0.044715; EPS=1e-5
def ln_fwd(z):
    m=jnp.mean(z,axis=-1,keepdims=True)
    c=z-m
    v=jnp.mean(c*c,axis=-1,keepdims=True)
    r=lax.rsqrt(v+EPS)
    return c*r,r
def ln_bwd(n,r,e):
    return r*(e-jnp.mean(e,axis=-1,keepdims=True)-n*jnp.mean(e*n,axis=-1,keepdims=True))
def kf_kernel(ao,at,x,ct,woo,wot,w1o,w1t,w2o,w2t,b1,nm, lo_ref,dres_ref,g_o,g_t,awo_o,awo_t,aw1_o,aw1_t,aw2_o,aw2_t,gnm_acc,ctS):
    i=pl.program_id(0); last=pl.num_programs(0)-1
    @pl.when(i==0)
    def _():
        for r in (awo_o,awo_t,aw1_o,aw1_t,aw2_o,aw2_t,gnm_acc,ctS): r[...]=jnp.zeros(r.shape,F32)
    @pl.when(i==0)
    def _():
        tiles=ctS.shape[0]//128
        for t in range(tiles): ctS[128*t:128*t+128,:]=ct[:,128*t:128*t+128].T
        if tiles*128<ctS.shape[0]: ctS[128*tiles:,:]=ct[:,128*tiles:].T
    c=ctS[pl.ds(i*T,T),:]
    attn=dot(ao[...],woo[...])+dot(at[...],wot[...])
    z=x[...].astype(F32)+attn
    n1,r1=ln_fwd(z)
    normed=n1*nm[0:1]+nm[1:2]
    nl=normed.astype(BF)
    def gate(pre):
        p2=pre*pre
        t=jnp.tanh(G0*pre*(1.0+G1*p2))
        hp=0.5*(1.0+t)
        act=pre*hp
        der=hp+0.5*pre*(1.0-t*t)*(G0*(1.0+3.0*G1*p2))
        return act.astype(BF),der
    acts=[];ders=[]
    second=normed+nm[2:3]
    for k,(w1,w2) in enumerate(((w1o,w2o),(w1t,w2t))):
        pre=dot(nl,w1[...])+b1[k:k+1]
        a,dd=gate(pre)
        acts.append(a);ders.append(dd)
        second=second+dot(a,w2[...],NT)
    n2,r2=ln_fwd(second)
    ctS[pl.ds(i*T,T),:]=n2*nm[3:4]+nm[4:5]
    d2=ln_bwd(n2,r2,c*nm[3:4])
    d2l=d2.astype(BF)
    dn=d2
    for k,(w1,w2,aw1,aw2) in enumerate(((w1o,w2o,aw1_o,aw2_o),(w1t,w2t,aw1_t,aw2_t))):
        aw2[0:D]+=dot(d2l,acts[k],TN)
        dpre=dot(d2l,w2[...])*ders[k]
        aw1[D:D+1]+=jnp.sum(dpre,axis=0,keepdims=True)
        dpl=dpre.astype(BF)
        aw1[0:D]+=dot(nl,dpl,TN)
        dn=dn+dot(dpl,w1[...],NT)
    dz=ln_bwd(n1,r1,dn*nm[0:1])
    dres_ref[...]=dz
    dal=dz.astype(BF)
    awo_o[0:CG]+=dot(ao[...],dal,TN)
    awo_t[0:CG]+=dot(at[...],dal,TN)
    gnm=jnp.concatenate([jnp.sum(v,axis=0,keepdims=True) for v in (dn*n1,dn,d2,c*n2,c)],0)
    gnm_acc[0:5]+=gnm
    @pl.when(i==last)
    def _():
        for g,a1,a2,aw in ((g_o,aw1_o,aw2_o,awo_o),(g_t,aw1_t,aw2_t,awo_t)):
            a2[D:D+5,0:D]=gnm_acc[0:5]
            g[:,1024:HFP]=jnp.zeros((1024,HFP-1024),BF)
            g[0:416,0:HF]=a1[...].astype(BF)
            g[416:448,0:1024]=jnp.zeros((32,1024),BF)
            g[448:864,0:HF]=a2[...].astype(BF)
            g[864:1024,0:1024]=jnp.zeros((160,1024),BF)
            g[896:1008,0:D]=aw[0:112].astype(BF)
            g[896:1008,512:512+D]=aw[112:224].astype(BF)
        tiles=ctS.shape[0]//128
        for t in range(tiles):
            lo_ref[:,128*t:128*t+128]=ctS[128*t:128*t+128,:].T
        if tiles*128<ctS.shape[0]:
            lo_ref[:,128*tiles:]=ctS[128*tiles:,:].T
def ff(ao,at,x,ct,woo,wot,w1o,w1t,w2o,w2t,b1,nm):
    n=x.shape[0]
    row=lambda w: pl.BlockSpec((T,w),lambda i:(i,0))
    cst=lambda *sh: pl.BlockSpec(sh,lambda i:(0,)*len(sh),pipeline_mode=pl.Buffered(1))
    S=jax.ShapeDtypeStruct
    gs=[(1024,HFP),(1024,HFP)]
    spec=pl.GridSpec(grid=(n//T,),
      in_specs=[row(CG),row(CG),row(D),cst(D,n),cst(CG,D),cst(CG,D),cst(D,HF),cst(D,HF),cst(D,HF),cst(D,HF),cst(2,HF),cst(5,D)],
      out_specs=[cst(D,n),row(D)]+[cst(*s) for s in gs],
      scratch_shapes=[pltpu.VMEM((224,D),F32)]*2+[pltpu.VMEM((416,HF),F32)]*4+[pltpu.VMEM((8,D),F32),pltpu.VMEM((n,D),F32)])
    return pl.pallas_call(kf_kernel,name="ff",grid_spec=spec,
      out_shape=[S((D,n),F32),S((n,D),F32)]+[S(s,BF) for s in gs],
      compiler_params=pltpu.CompilerParams(vmem_limit_bytes=60*2**20))(ao,at,x,ct,woo,wot,w1o,w1t,w2o,w2t,b1,nm)
def rev8(v):
    idx=7-lax.broadcasted_iota(jnp.int32,v.shape,0)
    return jnp.take_along_axis(v,idx,axis=0)
def unskew(blocks, base, rows):
    nb=len(blocks)
    lane=lax.broadcasted_iota(jnp.int32,(8,128),1); sub=lax.broadcasted_iota(jnp.int32,(8,128),0)
    outs=[[] for _ in blocks]
    for r in range(rows//8):
        sh=base-8*r-7
        rot=[pltpu.roll(rev8(b[8*r:8*r+8]),sh%128,1,stride=1,stride_axis=0) for b in blocks]
        m=lane<(sh+sub)
        for k in range(nb):
            if k==0: o=jnp.where(m,0.0,rot[0])
            else: o=jnp.where(m,rot[k-1],rot[k])
            outs[k].append(rev8(o))
    return [jnp.concatenate(o,0) for o in outs]

UB=2
def kb_kernel(last, half, meta, x_ref, prior_ref, p_ref, dres_ref, base_ref, w4p, wo, wT, rel, tab, bias, biasT, *rest):
    w4=[w4p[k,0:D,0:CG] for k in range(3)]
    if last:
        prev_ref, gp_ref, ig_ref, g_ref, xs, xcat, xq, dalS, ig, acc, drA, drB, dbias, G = rest
    else:
        ig_ref, g_ref, xs, xcat, xq, dalS, ig, acc, drA, drB, dbias, G = rest
    n=pl.program_id(0); st=pl.program_id(1)
    NA=RA; NB=RQ-RA
    @pl.when((st==0)&(n==0))
    def _():
        for r in (acc,drA,drB,dbias): r[...]=jnp.zeros(r.shape,F32)
    @pl.when(st==0)
    def _():
        xs[LEN:1376,:]=jnp.zeros((1376-LEN,D),F32)
        xs[0:LEN,:]=dres_ref[...]
        rows=lax.broadcasted_iota(jnp.int32,(RQ,D),0)
        for t in range(NSEG):
            dalS[t]=jnp.where(rows<SEG,xs[SEG*t:SEG*t+RQ,:],0.0).astype(BF)
        fill_rows(x_ref[...],prior_ref,xs,xcat,xq)
        xs[SEG:SEG+LEN,:]=base_ref[...]
        for t in range(NSEG+1):
            ig[t]=xs[SEG*t:SEG*t+152,:]
    hm=head_masks(RQ)
    zero=jnp.zeros((),BF)
    zr=jnp.zeros((KB_-KC,CG),BF)
    wqT=wT[0]; wkvT=wT[1:3].reshape(2*GP,D); woT=wT[3]
    def front(u):
        s=st*UB+u
        xc=xcat[s]; xqs=xq[s]; dal=dalS[s]
        kk=jnp.concatenate([dot(xc,w4[1]).astype(BF),zr],0)
        vv=jnp.concatenate([dot(xc,w4[2]).astype(BF),zr],0)
        qT=dot(wqT,xqs,NT).astype(BF).astype(F32)
        wuT=(qT+biasT[:,0:1]).astype(BF); wvT=(qT+biasT[:,1:2]).astype(BF)
        da=dot(dal,wo[...],NT).astype(BF)
        daT=dot(woT,dal,NT).astype(BF)
        dam=[jnp.where(m,da,zero) for m in hm]
        DA=dot(jnp.concatenate([w[0:RA] for w in dam],0),vv[0:KA_],NT)
        DB=dot(jnp.concatenate([w[RA:] for w in dam],0),vv,NT)
        ps=[(p_ref[0,u,h,0:RA,0:KA_],p_ref[0,u,h,RA:RQ,:]) for h in range(HG)]
        return kk,wuT,wvT,daT,DA,DB,ps
    def mid(fr):
        kk,wuT,wvT,daT,DA,DB,ps=fr
        res=[]
        for h in range(HG):
            one=[]
            for p,dp,R,nt,base in ((ps[h][0],DA[NA*h:NA*(h+1)],NA,2,105),(ps[h][1],DB[NB*h:NB*(h+1)],NB,3,69)):
                pf=p.astype(F32)
                w=dp*pf
                sm=w[:,0:128]
                for k in range(1,nt): sm=sm+w[:,128*k:128*k+128]
                delta=jnp.sum(sm,axis=1,keepdims=True)
                dr=(pf*SCALE)*(dp-delta)
                o=unskew([dr[:,128*k:128*k+128] for k in range(nt)],base,R)
                one.append((dr.astype(BF),jnp.concatenate([v.astype(BF) for v in o],1)))
            res.append(one)
        return res
    late=[]
    def back(u,fr,md):
        kk,wuT,wvT,daT,DA,DB,ps=fr
        s=st*UB+u
        dkT=[];dvT=[];rA=[];rB=[]
        for h in range(HG):
            (ra,pa_),(rb,pb_)=md[h]
            u_=wuT[HP*h:HP*(h+1)]; v_=wvT[HP*h:HP*(h+1)]; d_=daT[HP*h:HP*(h+1)]
            pA,pB=ps[h]
            k1=dot(u_,jnp.concatenate([ra,rb[:,0:KA_]],0)); k2=dot(u_[:,RA:],rb[:,KA_:])
            dkT.append(jnp.concatenate([k1,k2],1))
            v1=dot(d_,jnp.concatenate([pA,pB[:,0:KA_]],0)); v2=dot(d_[:,RA:],pB[:,KA_:])
            dvT.append(jnp.concatenate([v1,v2],1))
            rA.append(dot(v_[:,0:RA],pa_)); rB.append(dot(v_[:,RA:],pb_))
        def comb(col,mA_,mB_):
            OA=dot(jnp.concatenate([md[h][0][col] for h in range(HG)],0),mA_)
            OB=dot(jnp.concatenate([md[h][1][col] for h in range(HG)],0),mB_)
            aA=OA[0:NA]; aB=OB[0:NB]
            for h in range(1,HG):
                aA=jnp.where(hm[h][0:RA],OA[NA*h:NA*(h+1)],aA)
                aB=jnp.where(hm[h][RA:],OB[NB*h:NB*(h+1)],aB)
            return aA,aB
        uA,uB=comb(0,kk[0:KA_],kk)
        vA,vB=comb(1,rel[0:KA_],rel[KA_:])
        db=jnp.concatenate([jnp.sum(uA,0,keepdims=True)+jnp.sum(uB,0,keepdims=True),jnp.sum(vA,0,keepdims=True)+jnp.sum(vB,0,keepdims=True)],0)
        dq=jnp.concatenate([(uA+vA).astype(BF),(uB+vB).astype(BF)],0)
        dk=jnp.concatenate(dkT,0).astype(BF); dv=jnp.concatenate(dvT,0).astype(BF)
        xc=xcat[s]; xqs=xq[s]
        kv=jnp.concatenate([dk[:,0:KC],dv[:,0:KC]],0)
        gkv=dot(kv,xc)
        gq=dot(dq,xqs,TN)
        late.append((u,s,jnp.concatenate(rA,0),jnp.concatenate(rB,0),db,gkv,gq,dot(kv,wkvT,TN),dot(dq,w4[0],NT)[0:152]))
    frs=[None]*UB; mds=[None]*UB
    frs[0]=front(0)
    for u in range(UB):
        if u+1<UB: frs[u+1]=front(u+1)
        mds[u]=mid(frs[u])
        if u>0: back(u-1,frs[u-1],mds[u-1])
    back(UB-1,frs[UB-1],mds[UB-1])
    for (u,s,rA,rB,db,gkv,gq,g1,g2) in late:
        drA[...]+=rA; drB[...]+=rB
        dbias[0:2]+=db
        acc[0,0:CG]+=gq
        acc[1]+=gkv[0:GP]; acc[2]+=gkv[GP:]
        G[...]=g1
        ig[s+1]+=g2+G[SEG:SEG+152,:]
        ig[s]+=G[0:152,:]
    @pl.when(st==NSEG//UB-1)
    def _():
        for t in range(NSEG):
            xs[SEG*t:SEG*t+152,:]=ig[t+1]
        if last:
            xs[LEN:2*LEN,:]=xs[0:LEN,:]
            xs[0:LEN,:]=prev_ref[...]
            tiles=2*LEN//128
            for t in range(tiles):
                ig_ref[:,128*t:128*t+128]=xs[128*t:128*t+128,:].T
            ig_ref[:,128*tiles:]=xs[128*tiles:2*LEN,:].T
        else:
            ig_ref[...]=xs[0:LEN,:]
    @pl.when((st==NSEG//UB-1)&(n==pl.num_programs(0)-1))
    def _():
        a=jnp.concatenate([drA[...],jnp.zeros((GP,KB_-KA_),F32)],1)
        dr=drB[...]+pltpu.roll(a,60,1)
        acc[3]=dot(dr.astype(BF),tab[KA_:,:])
        xs[0:CG,:]=acc[0,0:CG]
        for k in range(1,4):
            for h in range(HG):
                o=CG*k+DH*h
                xs[o:o+DH,:]=acc[k,HP*h:HP*h+DH]
        xs[4*CG:832,:]=jnp.zeros((832-4*CG,D),F32)
        xs[4*CG:4*CG+2,0:CG]=dbias[0:2]
        g_ref[:,384:512]=jnp.zeros((832,128),g_ref.dtype)
        if last:
            g_ref[:,0:D]=xs[0:832,:]+gp_ref[:,0:D]
        else:
            g_ref[:,0:D]=xs[0:832,:].astype(g_ref.dtype)

def attention_bwd(streams,meta,x,prior,p,dres,base,w4,wo,wT,rel,tab,bias,biasT,half=False,prev=None):
    cst=lambda *sh: pl.BlockSpec(sh,lambda n,s,m: (0,)*len(sh))
    off=streams[0]; ns=len(streams); last=prev is not None
    row=lambda w: pl.BlockSpec((LEN,w),lambda n,s,m:(n+off,0))
    S=jax.ShapeDtypeStruct
    ig_spec=cst(D,2*LEN) if last else pl.BlockSpec((LEN,D),lambda n,s,m:(n,0))
    ig_shape=S((D,2*LEN),F32) if last else S((ns*LEN,D),F32)
    gs=pltpu.PrefetchScalarGridSpec(num_scalar_prefetch=1,grid=(ns,NSEG//UB),
      in_specs=[row(D),pl.BlockSpec((1,SEG,D),lambda n,s,m:(m[0]*2+n+off,0,0)),
        pl.BlockSpec((1,UB,HG,RQ,KB_),lambda n,s,m:(n+off,s,0,0,0)),row(D),row(D),
        cst(4,WR,WC),cst(CG,D),cst(4,GP,D),cst(KA_+KB_,CG),cst(KA_+KB_,D),cst(2,CG),cst(GP,8)]+([cst(LEN,D),cst(832,512)] if last else []),
      out_specs=[ig_spec,cst(832,512)],
      scratch_shapes=[pltpu.VMEM((1376+LEN if last else 1376,D),F32),pltpu.VMEM((NSEG,KC,D),BF),pltpu.VMEM((NSEG,RQ,D),BF),pltpu.VMEM((NSEG,RQ,D),BF),
        pltpu.VMEM((NSEG+1,152,D),F32),pltpu.VMEM((4,GP,D),F32),pltpu.VMEM((GP,KA_),F32),pltpu.VMEM((GP,KB_),F32),pltpu.VMEM((8,CG),F32),pltpu.VMEM((KC,D),F32)])
    ops=[meta,x,prior,p,dres,base,w4,wo,wT,rel,tab,bias,biasT]+(list(prev) if last else [])
    return pl.pallas_call(functools.partial(kb_kernel,last,half),grid_spec=gs,name="attn_bwd",
      out_shape=[ig_shape,S((832,512),BF if half else F32)],
      compiler_params=pltpu.CompilerParams(vmem_limit_bytes=62*2**20))(*ops)
RB=112
COUNTS=(4*D*D,D*D,D*2*HF,D*2*HF,2*D,2*HF,5*D)
def sq_kernel(at, f, out):
    a=at[...].astype(F32); a=a*a
    rows=lax.broadcasted_iota(jnp.int32,(832,512),0)
    tot=lambda v: jnp.sum(jnp.sum(v,axis=0,keepdims=True),axis=1,keepdims=True)
    t0=tot(jnp.where(rows<4*CG,a,0.0)); t4=tot(a[816:832])-tot(jnp.where(rows[816:832]<4*CG,a[816:832],0.0))
    def part(lo,n):
        v=f[lo:lo+n].astype(F32)
        return v*v
    w=part(0,416); r=lax.broadcasted_iota(jnp.int32,(416,HFP),0)
    t2=tot(jnp.where(r<D,w,0.0)); t5=tot(jnp.where(r[400:416]==D,w[400:416],0.0))
    w=part(448,416)
    t3=tot(jnp.where(r<D,w,0.0)); t6=tot(jnp.where(r[400:416]>=D,w[400:416],0.0))
    t1=tot(part(896,112))
    row=lax.broadcasted_iota(jnp.int32,(8,128),0)
    acc=jnp.zeros((8,128),F32)
    for k,t in enumerate((t0,t1,t2,t3,t4,t5,t6)): acc=jnp.where(row==k,t,acc)
    out[...]=acc

def squares(at,f):
    v=pl.BlockSpec(memory_space=pltpu.VMEM)
    return pl.pallas_call(sq_kernel,name="squares",in_specs=[v,v],out_specs=v,out_shape=jax.ShapeDtypeStruct((8,128),F32),
        compiler_params=pltpu.CompilerParams(vmem_limit_bytes=62*2**20))(at,f)

def adam_math(g,m,v,w,clip,rate):
    c=g*clip
    m2=BETA_ONE*m+(1.0-BETA_ONE)*c
    v2=BETA_TWO*v+(1.0-BETA_TWO)*c*c
    mh=m2*(1.0/(1.0-BETA_ONE**STEP)); vh=v2*(1.0/(1.0-BETA_TWO**STEP))
    w2=w-rate*(mh/(jnp.sqrt(vh)+ADAM_EPSILON)+WEIGHT_DECAY*w)
    return c,m2,v2,w2

def adam_kernel(own, so, sg, at, gp, g1, g2, gm, gv, gw, pm, pv, pw, em, ev, ew, rm, rv, rw, rms_ref, *rest):
    i=pl.program_id(0)
    outs=rest[:-1]; g3=rest[-1]
    @pl.when(i==0)
    def _():
        for k in range(4):
            g3[0:D,k,:]=at[CG*k:CG*k+CG,:].astype(F32).T[0:D]
    tot=[so[k,0]+sg[k,0] if k<6 else so[k,0] for k in range(7)]
    clips=[]; row=lax.broadcasted_iota(jnp.int32,(8,128),0); rms=jnp.zeros((8,128),F32); cl=jnp.zeros((8,128),F32)
    for k in range(7):
        num=jnp.float32(0); den=jnp.float32(0)
        for j in range(7):
            same=own[k]==own[j]
            num=num+jnp.where(same,tot[j],0.0); den=den+jnp.where(same,jnp.float32(COUNTS[j]),0.0)
        ms=jnp.full((8,128),num,F32)/jnp.full((8,128),den,F32)
        c=jnp.minimum(1.0,CLIP_LEVEL*lax.rsqrt(ms+1e-6))
        clips.append(c[0:1,0:1]); rms=jnp.where(row==k,jnp.sqrt(ms),rms); cl=jnp.where(row==k,c,cl)
    rms_ref[0]=rms; rms_ref[1]=cl
    def put(o,res):
        for r,v in zip(o[:4],res): r[...]=v
        o[4][...]=res[3].astype(BF)
    put(outs[0:5],adam_math(g3[pl.ds(pl.multiple_of(i*RB,RB),RB)],gm[...],gv[...],gw[...],clips[0].reshape(1,1,1),STEP_RATES[0]))
    put(outs[10:15],adam_math(g1[:,0:HF].astype(F32),em[...],ev[...],ew[...],clips[2],STEP_RATES[2]))
    put(outs[15:20],adam_math(g2[:,0:HF].astype(F32),rm[...],rv[...],rw[...],clips[3],STEP_RATES[3]))
    @pl.when(i==0)
    def _():
        for lo,hi,l in ((0,112,0),(112,CG,512)):
            g=gp[0:hi-lo,l:l+D].astype(F32)
            res=adam_math(g,pm[lo:hi],pv[lo:hi],pw[lo:hi],clips[1],STEP_RATES[1])
            for r,v in zip(outs[5:9],res): r[lo:hi]=v
            outs[9][lo:hi]=res[3].astype(BF)

def adam(owners,so,sg,at,f,q3,p3,e3,r3):
    S=jax.ShapeDtypeStruct
    bq=pl.BlockSpec((RB,4,CG),lambda i,o:(i,0,0)); be=pl.BlockSpec((RB,HF),lambda i,o:(i,0)); bp=pl.BlockSpec((CG,D),lambda i,o:(0,0))
    sm=pl.BlockSpec(memory_space=pltpu.SMEM)
    spec=pltpu.PrefetchScalarGridSpec(num_scalar_prefetch=1,grid=(4,),
      in_specs=[sm,sm,pl.BlockSpec((832,512),lambda i,o:(0,0)),pl.BlockSpec((RB,HFP),lambda i,o:(8,0)),pl.BlockSpec((RB,HFP),lambda i,o:(i,0)),pl.BlockSpec((RB,HFP),lambda i,o:(4+i,0))]+[bq]*3+[bp]*3+[be]*6,
      out_specs=[pl.BlockSpec((2,8,128),lambda i,o:(0,0,0))]+[bq]*5+[bp]*5+[be]*10,
      scratch_shapes=[pltpu.VMEM((4*RB,4,CG),F32)])
    outs=[S((2,8,128),F32)]
    for sh in ((D,4,CG),(CG,D),(D,HF),(D,HF)): outs+= [S(sh,F32)]*4+[S(sh,BF)]
    return pl.pallas_call(adam_kernel,name="adam",grid_spec=spec,out_shape=outs,
      compiler_params=pltpu.CompilerParams(vmem_limit_bytes=62*2**20))(owners,so,sg,at,f,f,f,*q3,*p3,*e3,*r3)
def positions(key_len, model_width):
    distance = (key_len - 1 - jnp.arange(key_len)).astype(jnp.float32)
    frequency = jnp.exp(
        jnp.arange(model_width // 2).astype(jnp.float32) * (-2.0 * math.log(10000.0) / model_width)
    )
    angles = distance[:, None] * frequency[None, :]
    return jnp.concatenate([jnp.sin(angles), jnp.cos(angles)], axis=1)


def shards(
    tokens,
    prior_memory,
    first_flags,
    owners,
    cotangent,
    qkvr_master,
    qkvr_first,
    qkvr_second,
    proj_master,
    proj_first,
    proj_second,
    expand_master,
    expand_first,
    expand_second,
    reduce_master,
    reduce_first,
    reduce_second,
    headbias_master,
    headbias_first,
    headbias_second,
    expbias_master,
    expbias_first,
    expbias_second,
    norms_master,
    norms_first,
    norms_second,
):
    heads_count = lax.axis_size("head")
    head = lax.axis_index("head")
    n_dp = lax.axis_size("dp")
    dp = lax.axis_index("dp")
    swap = [(h, heads_count - 1 - h) for h in range(heads_count)]
    def other(v):
        return lax.ppermute(v, "head", swap)
    def dp_swap(v, b):
        return lax.ppermute(v, "dp", [(i, i ^ b) for i in range(n_dp)])
    qkvr_own = jnp.pad(qkvr_master.astype(BF), ((0, 0), (0, WR - D), (0, WC - CG)))
    wo_own = proj_master.astype(BF)
    w1_own = expand_master.astype(BF)
    w2_own = reduce_master.T.astype(BF)
    b1_own = expbias_master.astype(BF).astype(F32)
    qkvr_oth = other(qkvr_own)
    small = other(jnp.concatenate([headbias_master.reshape(-1), b1_own]))
    wo_oth = other(wo_own)
    w1_oth = other(w1_own)
    w2_oth = other(w2_own)
    hb_oth = small[:2 * CG].reshape(2, CG)
    b1_oth = small[2 * CG:]
    meta = jnp.concatenate([head[None].astype(jnp.int32), lax.dynamic_slice_in_dim(first_flags, head * 2, 2, 0)])
    rows = positions(2 * SEG, D).astype(BF)
    tab = jnp.concatenate([rows[44:300], jnp.pad(rows, ((16, 68), (0, 0)))], 0)
    own = (qkvr_own, wo_own, headbias_master)
    oth = (qkvr_oth, wo_oth, hb_oth)
    att_own, p_own, *pre_own, x_rows = attention_fwd(True, meta, tokens.T, prior_memory, qkvr_own, wo_own, tab, headbias_master)
    att_oth, p_oth, *pre_oth = attention_fwd(False, meta, x_rows, prior_memory, qkvr_oth, wo_oth, tab, hb_oth)
    lo_t, dres, ff_own, ff_oth = ff(
        att_own, att_oth, x_rows, cotangent.T, wo_own, wo_oth, w1_own, w1_oth, w2_own, w2_oth,
        jnp.stack([b1_own, b1_oth]), norms_master)
    ff_got = other(ff_oth)
    def back(streams, group, p, pre, base, half=False, prev=None):
        w4, wo, hb = group
        wT, rel, bT = pre
        return attention_bwd(streams, meta, x_rows, prior_memory, p, dres, base, w4, wo, wT, rel, tab, hb, bT, half, prev)
    ig, at_oth = back((0, 1), oth, p_oth, pre_oth, dres, True)
    ff_got, at_oth, ig = lax.optimization_barrier((ff_got, at_oth, ig))
    at_got = other(at_oth)
    chunk = ff_own.shape[0] // n_dp
    half = (ff_own.astype(F32) + ff_got.astype(F32)).astype(BF).reshape(n_dp // 2, 2, chunk, HFP)
    odd = (dp & 1) == 1
    send = jnp.where(odd, half[:, 0], half[:, 1])
    keep = jnp.where(odd, half[:, 1], half[:, 0])
    pair = (keep.astype(F32) + dp_swap(send, 1).astype(F32)).astype(BF)
    pair, ig = lax.optimization_barrier((pair, ig))
    split = lax.all_to_all(pair, "dp", 0, 0, tiled=True, axis_index_groups=[list(range(c, n_dp, 2)) for c in range(2)])
    ig0, at0 = back((0,), own, p_own, pre_own, ig)
    part = jnp.sum(split.astype(F32), 0).astype(BF)
    part, ig0 = lax.optimization_barrier((part, ig0))
    ff_sum = lax.all_gather(part, "dp", axis=0, tiled=True)
    ig_t, at1 = back((1,), own, p_own, pre_own, ig, False, (ig0, at0))
    at_got, at1 = lax.optimization_barrier((at_got, at1))
    at_sum = (at1 + at_got.astype(F32)).astype(BF)
    bit = 1
    while bit < n_dp:
        part_rows = at_sum.shape[0] // 2
        up = (dp & bit) != 0
        send = jnp.where(up, at_sum[:part_rows], at_sum[part_rows:])
        keep = jnp.where(up, at_sum[part_rows:], at_sum[:part_rows])
        at_sum = (keep.astype(F32) + dp_swap(send, bit).astype(F32)).astype(BF)
        bit *= 2
    while bit > 1:
        bit //= 2
        got = dp_swap(at_sum, bit)
        up = (dp & bit) != 0
        at_sum = jnp.where(up, jnp.concatenate([got, at_sum], 0), jnp.concatenate([at_sum, got], 0))
    sq_own = squares(at_sum, ff_sum)
    sq_got = other(sq_own)
    flip = lambda v: jnp.transpose(v, (1, 0, 2))
    stats, *res = adam(
        owners, sq_own, sq_got, at_sum, ff_sum,
        (flip(qkvr_first), flip(qkvr_second), flip(qkvr_master)),
        (proj_first, proj_second, proj_master),
        (expand_first, expand_second, expand_master),
        (reduce_first.T, reduce_second.T, reduce_master.T))
    big = [[flip(v) for v in res[0:5]], res[5:10], res[10:15], [v.T for v in res[15:20]]]
    def small_step(k, g, m, v, w):
        return adam_math(g.astype(F32), m, v, w, stats[1, k, 0], STEP_RATES[k])
    rest = [
        small_step(4, at_sum[4 * CG:4 * CG + 2, :CG], headbias_first, headbias_second, headbias_master),
        small_step(5, ff_sum[D, :HF], expbias_first, expbias_second, expbias_master),
        small_step(6, ff_sum[448 + D:448 + D + 5, :D], norms_first, norms_second, norms_master),
    ]
    outs = [lo_t.T, ig_t.T, stats[0, :7, 0]]
    for r in big:
        outs += r[:4]
    for r in rest:
        outs += r
    return tuple(outs + [r[4] for r in big])


def solution(mesh):
    in_specs = (
        P(("dp", "head"), None),
        P("dp", None, None),
        P("dp"),
        P(),
        P(("dp", "head"), None),
        P(None, None, "head"),
        P(None, None, "head"),
        P(None, None, "head"),
        P("head", None),
        P("head", None),
        P("head", None),
        P(None, "head"),
        P(None, "head"),
        P(None, "head"),
        P("head", None),
        P("head", None),
        P("head", None),
        P(None, "head"),
        P(None, "head"),
        P(None, "head"),
        P("head"),
        P("head"),
        P("head"),
        P(),
        P(),
        P(),
    )
    out_specs = (
        P(("dp", "head"), None),
        P(("dp", "head"), None),
        P(),
        P(None, None, "head"),
        P(None, None, "head"),
        P(None, None, "head"),
        P(None, None, "head"),
        P("head", None),
        P("head", None),
        P("head", None),
        P("head", None),
        P(None, "head"),
        P(None, "head"),
        P(None, "head"),
        P(None, "head"),
        P("head", None),
        P("head", None),
        P("head", None),
        P("head", None),
        P(None, "head"),
        P(None, "head"),
        P(None, "head"),
        P(None, "head"),
        P("head"),
        P("head"),
        P("head"),
        P("head"),
        P(),
        P(),
        P(),
        P(),
        P(None, None, "head"),
        P("head", None),
        P(None, "head"),
        P("head", None),
    )
    return jax.shard_map(shards, mesh=mesh, in_specs=in_specs, out_specs=out_specs, check_vma=False)
```

```python
from jax.sharding import PartitionSpec as P
import math, functools
import jax, jax.numpy as jnp
from jax import lax
from jax.experimental import pallas as pl
from jax.experimental.pallas import tpu as pltpu
BF=jnp.bfloat16; F32=jnp.float32
NT=(((1,),(1,)),((),())); TN=(((0,),(0,)),((),()))
def dot(a,b,dn=(((1,),(0,)),((),()))): return lax.dot_general(a,b,dn,preferred_element_type=F32)
SEG=150; NSEG=8; LEN=1200; DH=41; HG=5; CG=205; D=410
RA=96; RQ=160; KA_=256; KB_=384; KC=304
HP=48; GP=HP*HG
LV={2:RA,3:56}
def fill(v,rows):
    return v if v.shape[0]==rows else jnp.concatenate([v,jnp.zeros((rows-v.shape[0],v.shape[1]),v.dtype)],0)
SCALE=1.0/math.sqrt(DH); LOG2E=1.4426950408889634

def fill_rows(x_rows, prior_ref, xs, xcat, xq):
    xs[0:SEG,:]=prior_ref[0].astype(F32)
    xs[SEG:SEG+LEN,:]=x_rows.astype(F32)
    xs[SEG+LEN:1376,:]=jnp.zeros((1376-SEG-LEN,D),F32)
    for s in range(NSEG):
        xcat[s]=xs[SEG*s:SEG*s+KC,:].astype(BF)
        xq[s]=xs[SEG*(s+1):SEG*(s+1)+RQ,:].astype(BF)

def head_masks(rows):
    lane=lax.broadcasted_iota(jnp.int32,(rows,CG),1)
    return [(lane>=DH*h)&(lane<DH*(h+1)) for h in range(HG)]

U=4
GU=4
WR=416; WC=256
def ka_kernel(first, meta, x_ref, prior_ref, w4p, wo, tab, bias, att_ref, p_ref, kv_ref, wuv_ref, wT_ref, rel_ref, bT_ref, *rest):
    if first: xn_ref, xs, xcat, xq, attS, biasA, biasB = rest
    else: xs, xcat, xq, attS, biasA, biasB = rest
    w4=[w4p[k,0:D,0:CG] for k in range(4)]
    n=pl.program_id(0); st=pl.program_id(1)
    @pl.when((st==0)&(n==0))
    def _():
        rel_ref[...]=dot(tab[...],w4[3]).astype(BF)
        xs[0:GP,:]=jnp.zeros((GP,D),F32)
        for k in range(4):
            src=w4[k].astype(F32).T if k<3 else wo[...].astype(F32)
            for h in range(HG): xs[HP*h:HP*h+DH,:]=src[DH*h:DH*h+DH]
            wT_ref[k]=xs[0:GP,:].astype(BF)
        bt=jnp.concatenate([bias[...],jnp.zeros((6,CG),F32)],0).T
        xs[0:GP,0:8]=jnp.zeros((GP,8),F32)
        for h in range(HG): xs[HP*h:HP*h+DH,0:8]=bt[DH*h:DH*h+DH]
        bT_ref[...]=xs[0:GP,0:8]
    @pl.when(st==0)
    def _():
        if first:
            @pl.when(n==0)
            def _():
                tiles=2*LEN//128
                for t in range(tiles): xn_ref[128*t:128*t+128,:]=x_ref[:,128*t:128*t+128].T
                xn_ref[128*tiles:,:]=x_ref[:,128*tiles:].T
            fill_rows(xn_ref[pl.ds(pl.multiple_of(n*LEN,16),LEN),:],prior_ref,xs,xcat,xq)
        else: fill_rows(x_ref[...],prior_ref,xs,xcat,xq)
    NA=RA; NB=RQ-RA
    has_mem=(st>0)|(meta[1+n]==1)
    jmin=jnp.where(has_mem,0,SEG)
    @pl.when(st==0)
    def _():
        for u in range(U):
            jm=jmin if u==0 else 0
            i=lax.broadcasted_iota(jnp.int32,(RA,KA_),0); j=lax.broadcasted_iota(jnp.int32,(RA,KA_),1)
            biasA[u]=jnp.where((j<=i+SEG)&(j>=jm),0.0,-1e30)
            i=lax.broadcasted_iota(jnp.int32,(NB,KB_),0)+RA; j=lax.broadcasted_iota(jnp.int32,(NB,KB_),1)
            biasB[u]=jnp.where((j<=i+SEG)&(j>=jm)&(j<2*SEG),0.0,-1e30)
    @pl.when(st==1)
    def _():
        biasA[0]=biasA[1]; biasB[0]=biasB[1]
    hm=head_masks(RQ)
    hmA=[m[0:RA] for m in hm]; hmB=[m[RA:] for m in hm]
    zero=jnp.zeros((),BF)
    iA=lax.broadcasted_iota(jnp.int32,(RA,128),0); lA=lax.broadcasted_iota(jnp.int32,(RA,128),1)
    mA=(lA+(105-iA))<128
    iB=lax.broadcasted_iota(jnp.int32,(NB,128),0); lB=lax.broadcasted_iota(jnp.int32,(NB,128),1)
    mB=(lB+(69-iB))<128
    c=SCALE*LOG2E
    vv=[None]*U
    def scores(u):
        s=st*U+u
        xc=xcat[s]
        zr=jnp.zeros((KB_-KC,CG),BF)
        kk=jnp.concatenate([dot(xc,w4[1]).astype(BF),zr],0)
        vv[u]=jnp.concatenate([dot(xc,w4[2]).astype(BF),zr],0)
        qT=dot(wT_ref[0],xq[s],NT).astype(BF).astype(F32)
        lateT.append((u,kk,vv[u],(qT+bT_ref[:,0:1]).astype(BF),(qT+bT_ref[:,1:2]).astype(BF)))
        q=dot(xq[s],w4[0]).astype(BF).astype(F32)
        wu=(q+bias[0:1,:]).astype(BF); wvv=(q+bias[1:2,:]).astype(BF)
        wum=[jnp.where(m,wu,zero) for m in hm]
        wvm=[jnp.where(m,wvv,zero) for m in hm]
        SA=dot(jnp.concatenate([w[0:RA] for w in wum],0),kk[0:KA_],NT)
        PA=dot(jnp.concatenate([w[0:RA] for w in wvm],0),rel_ref[0:KA_],NT)
        SB=dot(jnp.concatenate([w[RA:] for w in wum],0),kk,NT)
        PB=dot(jnp.concatenate([w[RA:] for w in wvm],0),rel_ref[KA_:],NT)
        return SA,PA,SB,PB
    def soft(u,sc):
        SA,PA,SB,PB=sc
        units=[]
        for h in range(HG):
            units.append((h,SA,PA,NA,2,0,23,biasA,mA)); units.append((h,SB,PB,NB,3,RA,59,biasB,mB))
        out=[]
        for i0 in range(0,len(units),GU):
            grp=units[i0:i0+GU]
            rolls=[[pltpu.roll(P_[R*h:R*h+min(R,LV[nt]),128*k:128*k+128],b0,1,stride=1,stride_axis=0) for k in range(nt)] for (h,S_,P_,R,nt,r0,b0,bs,m) in grp]
            ts=[]
            for (h,S_,P_,R,nt,r0,b0,bs,m),rr in zip(grp,rolls):
                L=LV[nt]
                ts.append([(S_[R*h:R*h+L,128*k:128*k+128]+(jnp.where(m[0:L],rr[k],rr[k+1]) if k+1<nt else rr[k]))*c+bs[u,0:L,128*k:128*k+128] for k in range(nt)])
            mxs=[]
            for t in ts:
                mx=t[0]
                for v in t[1:]: mx=jnp.maximum(mx,v)
                mxs.append(mx)
            mxs=[jnp.max(v,axis=1,keepdims=True) for v in mxs]
            es=[[jnp.exp2(v-mx) for v in t] for t,mx in zip(ts,mxs)]
            sms=[]
            for e in es:
                sm=e[0]
                for v in e[1:]: sm=sm+v
                sms.append(sm)
            lis=[1.0/jnp.sum(v,axis=1,keepdims=True) for v in sms]
            for (h,S_,P_,R,nt,r0,b0,bs,m),e,li in zip(grp,es,lis):
                p=jnp.concatenate([fill(v*li,R).astype(BF) for v in e],1)
                late.append((u,h,r0,R,nt,p))
                out.append(p)
        return out[0::2],out[1::2]
    def outp(u,pp):
        pas,pbs=pp
        s=st*U+u
        OA=dot(jnp.concatenate(pas,0),vv[u][0:KA_])
        OB=dot(jnp.concatenate(pbs,0),vv[u])
        aA=OA[0:NA]; aB=OB[0:NB]
        for h in range(1,HG):
            aA=jnp.where(hmA[h],OA[NA*h:NA*(h+1)],aA)
            aB=jnp.where(hmB[h],OB[NB*h:NB*(h+1)],aB)
        lateA.append((s,aA,aB))
    sc=[None]*U; pp=[None]*U; late=[]; lateA=[]; lateT=[]
    sc[0]=scores(0)
    for u in range(U):
        if u+1<U: sc[u+1]=scores(u+1)
        pp[u]=soft(u,sc[u])
        if u>0: outp(u-1,pp[u-1])
    outp(U-1,pp[U-1])
    for (u,h,r0,R,nt,p) in late: p_ref[0,u,h,r0:r0+R,0:128*nt]=p
    for (u,a,b,c_,d_) in lateT:
        kv_ref[0,u,0]=a[0:KC]; kv_ref[0,u,1]=b[0:KC]; wuv_ref[0,u,0]=c_; wuv_ref[0,u,1]=d_
    for (s,aA,aB) in lateA:
        attS[s,0:RA,:]=aA
        attS[s,RA:RQ,:]=aB
    @pl.when(st==NSEG//U-1)
    def _():
        for t in range(NSEG):
            xs[SEG*t:SEG*t+152,0:CG]=attS[t,0:152,:]
        att_ref[...]=xs[0:LEN,0:CG].astype(BF)

def attention_fwd(first,meta,x,prior,w4,wo,tab,bias):
    cst=lambda *sh: pl.BlockSpec(sh,lambda n,s,m: (0,)*len(sh))
    S=jax.ShapeDtypeStruct
    gs=pltpu.PrefetchScalarGridSpec(num_scalar_prefetch=1,grid=(2,NSEG//U),
      in_specs=[cst(D,2*LEN) if first else pl.BlockSpec((LEN,D),lambda n,s,m:(n,0)),
        pl.BlockSpec((1,SEG,D),lambda n,s,m:(m[0]*2+n,0,0)),
        cst(4,WR,WC),cst(CG,D),cst(KA_+KB_,D),cst(2,CG)],
      out_specs=[pl.BlockSpec((LEN,CG),lambda n,s,m:(n,0)),
        pl.BlockSpec((1,U,HG,RQ,KB_),lambda n,s,m:(n,s,0,0,0)),pl.BlockSpec((1,U,2,KC,CG),lambda n,s,m:(n,s,0,0,0)),pl.BlockSpec((1,U,2,GP,RQ),lambda n,s,m:(n,s,0,0,0)),cst(4,GP,D),cst(KA_+KB_,CG),cst(GP,8)]+([cst(2*LEN,D)] if first else []),
      scratch_shapes=[pltpu.VMEM((1376,D),F32),pltpu.VMEM((NSEG,KC,D),BF),pltpu.VMEM((NSEG,RQ,D),BF),
        pltpu.VMEM((NSEG,RQ,CG),F32),
        pltpu.VMEM((U,RA,KA_),F32),pltpu.VMEM((U,RQ-RA,KB_),F32)])
    return pl.pallas_call(functools.partial(ka_kernel,first),grid_spec=gs,name="attn_fwd",
      out_shape=[S((2*LEN,CG),BF),S((2,NSEG,HG,RQ,KB_),BF),S((2,NSEG,2,KC,CG),BF),S((2,NSEG,2,GP,RQ),BF),S((4,GP,D),BF),S((KA_+KB_,CG),BF),S((GP,8),F32)]+([S((2*LEN,D),BF)] if first else []),
      compiler_params=pltpu.CompilerParams(vmem_limit_bytes=56*2**20))(meta,x,prior,w4,wo,tab,bias)

CLIP_LEVEL = 0.01
BETA_ONE = 0.5
BETA_TWO = 0.5
ADAM_EPSILON = 1e-08
WEIGHT_DECAY = 0.1
STEP = 10
STEP_RATES = (0.03, 0.2, 0.03, 0.015, 0.3, 0.3, 0.3)
T=480; HF=1050; HFP=1152
G0=0.7978845608028654; G1=0.044715; EPS=1e-5
def ln_fwd(z):
    m=jnp.mean(z,axis=-1,keepdims=True)
    c=z-m
    v=jnp.mean(c*c,axis=-1,keepdims=True)
    r=lax.rsqrt(v+EPS)
    return c*r,r
def ln_bwd(n,r,e):
    return r*(e-jnp.mean(e,axis=-1,keepdims=True)-n*jnp.mean(e*n,axis=-1,keepdims=True))
def kf_kernel(ao,at,x,ct,woo,wot,w1o,w1t,w2o,w2t,b1,nm, lo_ref,dres_ref,g_o,g_t,awo_o,awo_t,aw1,aw2,gnm_acc,ctS,w1c,w2c):
    i=pl.program_id(0); last=pl.num_programs(0)-1
    @pl.when(i==0)
    def _():
        for r in (awo_o,awo_t,aw1,aw2,gnm_acc): r[...]=jnp.zeros(r.shape,F32)
        for r,u,v in ((w1c,w1o,w1t),(w2c,w2o,w2t)):
            r[...]=jnp.concatenate([u[...].astype(F32),v[...].astype(F32)],1).astype(BF)
    @pl.when(i==0)
    def _():
        tiles=ctS.shape[0]//128
        for t in range(tiles): ctS[128*t:128*t+128,:]=ct[:,128*t:128*t+128].T
        if tiles*128<ctS.shape[0]: ctS[128*tiles:,:]=ct[:,128*tiles:].T
    c=ctS[pl.ds(i*T,T),:]
    attn=dot(ao[...],woo[...])+dot(at[...],wot[...])
    z=x[...].astype(F32)+attn
    n1,r1=ln_fwd(z)
    normed=n1*nm[0:1]+nm[1:2]
    nl=normed.astype(BF)
    def gate(pre):
        p2=pre*pre
        t=jnp.tanh(G0*pre*(1.0+G1*p2))
        hp=0.5*(1.0+t)
        act=pre*hp
        der=hp+0.5*pre*(1.0-t*t)*(G0*(1.0+3.0*G1*p2))
        return act.astype(BF),der
    parts=((0,768),(768,1536),(1536,2*HF))
    pres=[dot(nl,w1c[:,lo:hi])+b1[:,lo:hi] for lo,hi in parts[:1]]
    acts=[];ders=[]
    second=normed+nm[2:3]
    for k,(lo,hi) in enumerate(parts):
        if k+1<len(parts):
            l2,h2=parts[k+1]
            pres.append(dot(nl,w1c[:,l2:h2])+b1[:,l2:h2])
        a_,d_=gate(pres[k])
        acts.append(a_); ders.append(d_)
        second=second+dot(a_,w2c[:,lo:hi],NT)
    n2,r2=ln_fwd(second)
    ctS[pl.ds(i*T,T),:]=n2*nm[3:4]+nm[4:5]
    d2=ln_bwd(n2,r2,c*nm[3:4])
    d2l=d2.astype(BF)
    dn=d2
    for k,(lo,hi) in enumerate(parts):
        dpre=dot(d2l,w2c[:,lo:hi])*ders[k]
        aw2[0:D,lo:hi]+=dot(d2l,acts[k],TN)
        aw1[D:D+1,lo:hi]+=jnp.sum(dpre,axis=0,keepdims=True)
        dpl=dpre.astype(BF)
        aw1[0:D,lo:hi]+=dot(nl,dpl,TN)
        dn=dn+dot(dpl,w1c[:,lo:hi],NT)
    dz=ln_bwd(n1,r1,dn*nm[0:1])
    dres_ref[...]=dz
    dal=dz.astype(BF)
    awo_o[0:CG]+=dot(ao[...],dal,TN)
    awo_t[0:CG]+=dot(at[...],dal,TN)
    gnm=jnp.concatenate([jnp.sum(v,axis=0,keepdims=True) for v in (dn*n1,dn,d2,c*n2,c)],0)
    gnm_acc[0:5]+=gnm
    @pl.when(i==last)
    def _():
        aw2[D:D+5,0:D]=gnm_acc[0:5]
        aw2[D:D+5,HF:HF+D]=gnm_acc[0:5]
        for g,lo,aw in ((g_o,0,awo_o),(g_t,HF,awo_t)):
            g[:,1024:HFP]=jnp.zeros((1024,HFP-1024),BF)
            g[0:416,0:HF]=aw1[:,lo:lo+HF].astype(BF)
            g[416:448,0:1024]=jnp.zeros((32,1024),BF)
            g[448:864,0:HF]=aw2[:,lo:lo+HF].astype(BF)
            g[864:1024,0:1024]=jnp.zeros((160,1024),BF)
            g[896:1008,0:D]=aw[0:112].astype(BF)
            g[896:1008,512:512+D]=aw[112:224].astype(BF)
        tiles=ctS.shape[0]//128
        for t in range(tiles):
            lo_ref[:,128*t:128*t+128]=ctS[128*t:128*t+128,:].T
        if tiles*128<ctS.shape[0]:
            lo_ref[:,128*tiles:]=ctS[128*tiles:,:].T
def ff(ao,at,x,ct,woo,wot,w1o,w1t,w2o,w2t,b1,nm):
    n=x.shape[0]
    row=lambda w: pl.BlockSpec((T,w),lambda i:(i,0))
    cst=lambda *sh: pl.BlockSpec(sh,lambda i:(0,)*len(sh),pipeline_mode=pl.Buffered(1))
    S=jax.ShapeDtypeStruct
    gs=[(1024,HFP),(1024,HFP)]
    spec=pl.GridSpec(grid=(n//T,),
      in_specs=[row(CG),row(CG),row(D),cst(D,n),cst(CG,D),cst(CG,D),cst(D,HF),cst(D,HF),cst(D,HF),cst(D,HF),cst(1,2*HF),cst(5,D)],
      out_specs=[cst(D,n),row(D)]+[cst(*s) for s in gs],
      scratch_shapes=[pltpu.VMEM((224,D),F32)]*2+[pltpu.VMEM((416,2*HF),F32)]*2+[pltpu.VMEM((8,D),F32),pltpu.VMEM((n,D),F32)]+[pltpu.VMEM((D,2*HF),BF)]*2)
    return pl.pallas_call(kf_kernel,name="ff",grid_spec=spec,
      out_shape=[S((D,n),F32),S((n,D),F32)]+[S(s,BF) for s in gs],
      compiler_params=pltpu.CompilerParams(vmem_limit_bytes=60*2**20))(ao,at,x,ct,woo,wot,w1o,w1t,w2o,w2t,b1,nm)
def rev8(v):
    idx=7-lax.broadcasted_iota(jnp.int32,v.shape,0)
    return jnp.take_along_axis(v,idx,axis=0)
def unskew(blocks, base, rows):
    nb=len(blocks)
    lane=lax.broadcasted_iota(jnp.int32,(8,128),1); sub=lax.broadcasted_iota(jnp.int32,(8,128),0)
    outs=[[] for _ in blocks]
    for r in range(rows//8):
        sh=base-8*r-7
        rot=[pltpu.roll(rev8(b[8*r:8*r+8]),sh%128,1,stride=1,stride_axis=0) for b in blocks]
        m=lane<(sh+sub)
        for k in range(nb):
            if k==0: o=jnp.where(m,0.0,rot[0])
            else: o=jnp.where(m,rot[k-1],rot[k])
            outs[k].append(rev8(o))
    return [jnp.concatenate(o,0) for o in outs]

UB=4
def kb_kernel(last, half, meta, x_ref, prior_ref, p_ref, dres_ref, base_ref, w4p, wo, wT, rel, tab, kv_ref, wuv_ref, *rest):
    w4=[w4p[k,0:D,0:CG] for k in range(3)]
    if last:
        prev_ref, gp_ref, ig_ref, g_ref, xs, xcat, xq, dalS, ig, acc, drA, drB, dbias, G = rest
    else:
        ig_ref, g_ref, xs, xcat, xq, dalS, ig, acc, drA, drB, dbias, G = rest
    n=pl.program_id(0); st=pl.program_id(1)
    NA=RA; NB=RQ-RA
    @pl.when((st==0)&(n==0))
    def _():
        for r in (acc,drA,drB,dbias): r[...]=jnp.zeros(r.shape,F32)
    @pl.when(st==0)
    def _():
        xs[LEN:1376,:]=jnp.zeros((1376-LEN,D),F32)
        xs[0:LEN,:]=dres_ref[...]
        rows=lax.broadcasted_iota(jnp.int32,(RQ,D),0)
        for t in range(NSEG):
            dalS[t]=jnp.where(rows<SEG,xs[SEG*t:SEG*t+RQ,:],0.0).astype(BF)
        fill_rows(x_ref[...],prior_ref,xs,xcat,xq)
        xs[SEG:SEG+LEN,:]=base_ref[...]
        for t in range(NSEG+1):
            ig[t]=xs[SEG*t:SEG*t+152,:]
    hm=head_masks(RQ)
    zero=jnp.zeros((),BF)
    zr=jnp.zeros((KB_-KC,CG),BF)
    wkvT=wT[1:3].reshape(2*GP,D); woT=wT[3]
    def front(u):
        s=st*UB+u
        dal=dalS[s]
        kk=jnp.concatenate([kv_ref[0,u,0],zr],0)
        vv=jnp.concatenate([kv_ref[0,u,1],zr],0)
        wuT=wuv_ref[0,u,0]; wvT=wuv_ref[0,u,1]
        da=dot(dal,wo[...],NT).astype(BF)
        daT=dot(woT,dal,NT).astype(BF)
        dam=[jnp.where(m,da,zero) for m in hm]
        DA=dot(jnp.concatenate([w[0:RA] for w in dam],0),vv[0:KA_],NT)
        DB=dot(jnp.concatenate([w[RA:] for w in dam],0),vv,NT)
        ps=[(p_ref[0,u,h,0:RA,0:KA_],p_ref[0,u,h,RA:RQ,:]) for h in range(HG)]
        return kk,wuT,wvT,daT,DA,DB,ps
    def mid(fr):
        kk,wuT,wvT,daT,DA,DB,ps=fr
        res=[]
        for h in range(HG):
            one=[]
            for p,dp,R,nt,base in ((ps[h][0],DA[NA*h:NA*(h+1)],NA,2,105),(ps[h][1],DB[NB*h:NB*(h+1)],NB,3,69)):
                L=LV[nt]
                pf=p.astype(F32)[0:L]; dp=dp[0:L]
                w=dp*pf
                sm=w[:,0:128]
                for k in range(1,nt): sm=sm+w[:,128*k:128*k+128]
                delta=jnp.sum(sm,axis=1,keepdims=True)
                dr=(pf*SCALE)*(dp-delta)
                o=unskew([dr[:,128*k:128*k+128] for k in range(nt)],base,L)
                one.append((fill(dr,R).astype(BF),jnp.concatenate([fill(v,R).astype(BF) for v in o],1)))
            res.append(one)
        return res
    late=[]
    def back(u,fr,md):
        kk,wuT,wvT,daT,DA,DB,ps=fr
        s=st*UB+u
        dkT=[];dvT=[];rA=[];rB=[]
        for h in range(HG):
            (ra,pa_),(rb,pb_)=md[h]
            u_=wuT[HP*h:HP*(h+1)]; v_=wvT[HP*h:HP*(h+1)]; d_=daT[HP*h:HP*(h+1)]
            pA,pB=ps[h]
            k1=dot(u_,jnp.concatenate([ra,rb[:,0:KA_]],0)); k2=dot(u_[:,RA:],rb[:,KA_:])
            dkT.append(jnp.concatenate([k1,k2],1))
            v1=dot(d_,jnp.concatenate([pA,pB[:,0:KA_]],0)); v2=dot(d_[:,RA:],pB[:,KA_:])
            dvT.append(jnp.concatenate([v1,v2],1))
            rA.append(dot(v_[:,0:RA],pa_)); rB.append(dot(v_[:,RA:],pb_))
        def comb(col,mA_,mB_):
            OA=dot(jnp.concatenate([md[h][0][col] for h in range(HG)],0),mA_)
            OB=dot(jnp.concatenate([md[h][1][col] for h in range(HG)],0),mB_)
            aA=OA[0:NA]; aB=OB[0:NB]
            for h in range(1,HG):
                aA=jnp.where(hm[h][0:RA],OA[NA*h:NA*(h+1)],aA)
                aB=jnp.where(hm[h][RA:],OB[NB*h:NB*(h+1)],aB)
            return aA,aB
        uA,uB=comb(0,kk[0:KA_],kk)
        vA,vB=comb(1,rel[0:KA_],rel[KA_:])
        db=jnp.concatenate([jnp.sum(uA,0,keepdims=True)+jnp.sum(uB,0,keepdims=True),jnp.sum(vA,0,keepdims=True)+jnp.sum(vB,0,keepdims=True)],0)
        dq=jnp.concatenate([(uA+vA).astype(BF),(uB+vB).astype(BF)],0)
        dk=jnp.concatenate(dkT,0).astype(BF); dv=jnp.concatenate(dvT,0).astype(BF)
        xc=xcat[s]; xqs=xq[s]
        kv=jnp.concatenate([dk[:,0:KC],dv[:,0:KC]],0)
        gkv=dot(kv,xc)
        gq=dot(dq,xqs,TN)
        late.append((u,s,jnp.concatenate(rA,0),jnp.concatenate(rB,0),db,gkv,gq,dot(kv,wkvT,TN),dot(dq,w4[0],NT)[0:152]))
    frs=[None]*UB; mds=[None]*UB
    frs[0]=front(0)
    for u in range(UB):
        if u+1<UB: frs[u+1]=front(u+1)
        mds[u]=mid(frs[u])
        if u>0: back(u-1,frs[u-1],mds[u-1])
    back(UB-1,frs[UB-1],mds[UB-1])
    for (u,s,rA,rB,db,gkv,gq,g1,g2) in late:
        drA[...]+=rA; drB[...]+=rB
        dbias[0:2]+=db
        acc[0,0:CG]+=gq
        acc[1]+=gkv[0:GP]; acc[2]+=gkv[GP:]
        G[...]=g1
        ig[s+1]+=g2+G[SEG:SEG+152,:]
        ig[s]+=G[0:152,:]
    @pl.when(st==NSEG//UB-1)
    def _():
        for t in range(NSEG):
            xs[SEG*t:SEG*t+152,:]=ig[t+1]
        if last:
            xs[LEN:2*LEN,:]=xs[0:LEN,:]
            xs[0:LEN,:]=prev_ref[...]
            tiles=2*LEN//128
            for t in range(tiles):
                ig_ref[:,128*t:128*t+128]=xs[128*t:128*t+128,:].T
            ig_ref[:,128*tiles:]=xs[128*tiles:2*LEN,:].T
        else:
            ig_ref[...]=xs[0:LEN,:]
    @pl.when((st==NSEG//UB-1)&(n==pl.num_programs(0)-1))
    def _():
        a=jnp.concatenate([drA[...],jnp.zeros((GP,KB_-KA_),F32)],1)
        dr=drB[...]+pltpu.roll(a,60,1)
        acc[3]=dot(dr.astype(BF),tab[KA_:,:])
        xs[0:CG,:]=acc[0,0:CG]
        for k in range(1,4):
            for h in range(HG):
                o=CG*k+DH*h
                xs[o:o+DH,:]=acc[k,HP*h:HP*h+DH]
        xs[4*CG:832,:]=jnp.zeros((832-4*CG,D),F32)
        xs[4*CG:4*CG+2,0:CG]=dbias[0:2]
        g_ref[:,384:512]=jnp.zeros((832,128),g_ref.dtype)
        if last:
            g_ref[:,0:D]=xs[0:832,:]+gp_ref[:,0:D]
        else:
            g_ref[:,0:D]=xs[0:832,:].astype(g_ref.dtype)

def attention_bwd(streams,meta,x,prior,p,dres,base,w4,wo,wT,rel,tab,kv,wuv,half=False,prev=None):
    cst=lambda *sh: pl.BlockSpec(sh,lambda n,s,m: (0,)*len(sh))
    off=streams[0]; ns=len(streams); last=prev is not None
    row=lambda w: pl.BlockSpec((LEN,w),lambda n,s,m:(n+off,0))
    S=jax.ShapeDtypeStruct
    ig_spec=cst(D,2*LEN) if last else pl.BlockSpec((LEN,D),lambda n,s,m:(n,0))
    ig_shape=S((D,2*LEN),F32) if last else S((ns*LEN,D),F32)
    gs=pltpu.PrefetchScalarGridSpec(num_scalar_prefetch=1,grid=(ns,NSEG//UB),
      in_specs=[row(D),pl.BlockSpec((1,SEG,D),lambda n,s,m:(m[0]*2+n+off,0,0)),
        pl.BlockSpec((1,UB,HG,RQ,KB_),lambda n,s,m:(n+off,s,0,0,0)),row(D),row(D),
        cst(4,WR,WC),cst(CG,D),cst(4,GP,D),cst(KA_+KB_,CG),cst(KA_+KB_,D),pl.BlockSpec((1,UB,2,KC,CG),lambda n,s,m:(n+off,s,0,0,0)),pl.BlockSpec((1,UB,2,GP,RQ),lambda n,s,m:(n+off,s,0,0,0))]+([cst(LEN,D),cst(832,512)] if last else []),
      out_specs=[ig_spec,cst(832,512)],
      scratch_shapes=[pltpu.VMEM((1376+LEN if last else 1376,D),F32),pltpu.VMEM((NSEG,KC,D),BF),pltpu.VMEM((NSEG,RQ,D),BF),pltpu.VMEM((NSEG,RQ,D),BF),
        pltpu.VMEM((NSEG+1,152,D),F32),pltpu.VMEM((4,GP,D),F32),pltpu.VMEM((GP,KA_),F32),pltpu.VMEM((GP,KB_),F32),pltpu.VMEM((8,CG),F32),pltpu.VMEM((KC,D),F32)])
    ops=[meta,x,prior,p,dres,base,w4,wo,wT,rel,tab,kv,wuv]+(list(prev) if last else [])
    return pl.pallas_call(functools.partial(kb_kernel,last,half),grid_spec=gs,name="attn_bwd",
      out_shape=[ig_shape,S((832,512),BF if half else F32)],
      compiler_params=pltpu.CompilerParams(vmem_limit_bytes=62*2**20))(*ops)
RB=112
COUNTS=(4*D*D,D*D,D*2*HF,D*2*HF,2*D,2*HF,5*D)
def sq_kernel(at, f, out):
    a=at[...].astype(F32); a=a*a
    rows=lax.broadcasted_iota(jnp.int32,(832,512),0)
    tot=lambda v: jnp.sum(jnp.sum(v,axis=0,keepdims=True),axis=1,keepdims=True)
    t0=tot(jnp.where(rows<4*CG,a,0.0)); t4=tot(a[816:832])-tot(jnp.where(rows[816:832]<4*CG,a[816:832],0.0))
    def part(lo,n):
        v=f[lo:lo+n].astype(F32)
        return v*v
    w=part(0,416); r=lax.broadcasted_iota(jnp.int32,(416,HFP),0)
    t2=tot(jnp.where(r<D,w,0.0)); t5=tot(jnp.where(r[400:416]==D,w[400:416],0.0))
    w=part(448,416)
    t3=tot(jnp.where(r<D,w,0.0)); t6=tot(jnp.where(r[400:416]>=D,w[400:416],0.0))
    t1=tot(part(896,112))
    row=lax.broadcasted_iota(jnp.int32,(8,128),0)
    acc=jnp.zeros((8,128),F32)
    for k,t in enumerate((t0,t1,t2,t3,t4,t5,t6)): acc=jnp.where(row==k,t,acc)
    out[...]=acc

def squares(at,f):
    v=pl.BlockSpec(memory_space=pltpu.VMEM)
    return pl.pallas_call(sq_kernel,name="squares",in_specs=[v,v],out_specs=v,out_shape=jax.ShapeDtypeStruct((8,128),F32),
        compiler_params=pltpu.CompilerParams(vmem_limit_bytes=62*2**20))(at,f)

def adam_math(g,m,v,w,clip,rate):
    c=g*clip
    m2=BETA_ONE*m+(1.0-BETA_ONE)*c
    v2=BETA_TWO*v+(1.0-BETA_TWO)*c*c
    mh=m2*(1.0/(1.0-BETA_ONE**STEP)); vh=v2*(1.0/(1.0-BETA_TWO**STEP))
    w2=w-rate*(mh/(jnp.sqrt(vh)+ADAM_EPSILON)+WEIGHT_DECAY*w)
    return c,m2,v2,w2

QB=128
def adam_kernel(own, so, sg, at, ff, g1, g2, gm, gv, gw, pm, pv, pw, em, ev, ew, rm, rv, rw, hm_, hv_, hw_, bm_, bv_, bw_, nm_, nv_, nw_, rms_ref, *rest):
    i=pl.program_id(0)
    outs=rest[:-1]; g3=rest[-1]
    tot=[so[k,0]+sg[k,0] if k<6 else so[k,0] for k in range(7)]
    clips=[]; lane=lax.broadcasted_iota(jnp.int32,(1,128),1); rms=jnp.zeros((1,128),F32)
    for k in range(7):
        num=jnp.float32(0); den=jnp.float32(0)
        for j in range(7):
            same=own[k]==own[j]
            num=num+jnp.where(same,tot[j],0.0); den=den+jnp.where(same,jnp.float32(COUNTS[j]),0.0)
        ms=jnp.full((1,128),num,F32)/jnp.full((1,128),den,F32)
        c=jnp.minimum(1.0,CLIP_LEVEL*lax.rsqrt(ms+1e-6))
        clips.append(c[0:1,0:1]); rms=jnp.where(lane==k,jnp.sqrt(ms),rms)
    rms_ref[...]=rms
    def put(o,res):
        for r,v in zip(o[:4],res): r[...]=v
        if len(o)>4: o[4][...]=res[3].astype(BF)
    put(outs[10:15],adam_math(g1[:,0:HF].astype(F32),em[...],ev[...],ew[...],clips[2],STEP_RATES[2]))
    put(outs[15:20],adam_math(g2[:,0:HF].astype(F32),rm[...],rv[...],rw[...],clips[3],STEP_RATES[3]))
    blk=at[:,pl.ds(pl.multiple_of(i*QB,QB),QB)].astype(F32)
    for k in range(4): g3[:,k,:]=blk[CG*k:CG*k+CG].T
    put(outs[0:5],adam_math(g3[...],gm[...],gv[...],gw[...],clips[0].reshape(1,1,1),STEP_RATES[0]))
    @pl.when(i==0)
    def _():
        for lo,hi,l in ((0,112,0),(112,CG,512)):
            g=ff[896:896+hi-lo,l:l+D].astype(F32)
            res=adam_math(g,pm[lo:hi],pv[lo:hi],pw[lo:hi],clips[1],STEP_RATES[1])
            for r,v in zip(outs[5:9],res): r[lo:hi]=v
            outs[9][lo:hi]=res[3].astype(BF)
        put(outs[20:24],adam_math(at[816:832,:].astype(F32)[4*CG-816:4*CG-814,0:CG],hm_[...],hv_[...],hw_[...],clips[4],STEP_RATES[4]))
        put(outs[24:28],adam_math(ff[400:416,:].astype(F32)[D-400,0:HF],bm_[...],bv_[...],bw_[...],clips[5][0],STEP_RATES[5]))
        put(outs[28:32],adam_math(ff[848:864,:].astype(F32)[10:15,0:D],nm_[...],nv_[...],nw_[...],clips[6],STEP_RATES[6]))

def adam(owners,so,sg,at,f,q3,p3,e3,r3,h3,b3,n3):
    S=jax.ShapeDtypeStruct
    one=pl.Buffered(1)
    cst=lambda *sh: pl.BlockSpec(sh,lambda i,o:(0,)*len(sh),pipeline_mode=one)
    bq=pl.BlockSpec((QB,4,CG),lambda i,o:(i,0,0)); be=pl.BlockSpec((RB,HF),lambda i,o:(i,0)); bp=cst(CG,D)
    bh,bb,bn=cst(2,CG),cst(HF),cst(5,D)
    sm=pl.BlockSpec(memory_space=pltpu.SMEM)
    spec=pltpu.PrefetchScalarGridSpec(num_scalar_prefetch=1,grid=(4,),
      in_specs=[sm,sm,cst(832,512),cst(1024,HFP),pl.BlockSpec((RB,HFP),lambda i,o:(i,0)),pl.BlockSpec((RB,HFP),lambda i,o:(4+i,0))]+[bq]*3+[bp]*3+[be]*6+[bh]*3+[bb]*3+[bn]*3,
      out_specs=[cst(1,128)]+[bq]*5+[bp]*5+[be]*10+[bh]*4+[bb]*4+[bn]*4,
      scratch_shapes=[pltpu.VMEM((QB,4,CG),F32)])
    outs=[S((1,128),F32)]
    for sh in ((D,4,CG),(CG,D),(D,HF),(D,HF)): outs+= [S(sh,F32)]*4+[S(sh,BF)]
    for sh in ((2,CG),(HF,),(5,D)): outs+=[S(sh,F32)]*4
    return pl.pallas_call(adam_kernel,name="adam",grid_spec=spec,out_shape=outs,
      compiler_params=pltpu.CompilerParams(vmem_limit_bytes=62*2**20))(owners,so,sg,at,f,f,f,*q3,*p3,*e3,*r3,*h3,*b3,*n3)
def positions(key_len, model_width):
    distance = (key_len - 1 - jnp.arange(key_len)).astype(jnp.float32)
    frequency = jnp.exp(
        jnp.arange(model_width // 2).astype(jnp.float32) * (-2.0 * math.log(10000.0) / model_width)
    )
    angles = distance[:, None] * frequency[None, :]
    return jnp.concatenate([jnp.sin(angles), jnp.cos(angles)], axis=1)


def shards(
    tokens,
    prior_memory,
    first_flags,
    owners,
    cotangent,
    qkvr_master,
    qkvr_first,
    qkvr_second,
    proj_master,
    proj_first,
    proj_second,
    expand_master,
    expand_first,
    expand_second,
    reduce_master,
    reduce_first,
    reduce_second,
    headbias_master,
    headbias_first,
    headbias_second,
    expbias_master,
    expbias_first,
    expbias_second,
    norms_master,
    norms_first,
    norms_second,
):
    heads_count = lax.axis_size("head")
    head = lax.axis_index("head")
    n_dp = lax.axis_size("dp")
    dp = lax.axis_index("dp")
    swap = [(h, heads_count - 1 - h) for h in range(heads_count)]
    def other(v):
        return lax.ppermute(v, "head", swap)
    def dp_swap(v, b):
        return lax.ppermute(v, "dp", [(i, i ^ b) for i in range(n_dp)])
    qkvr_own = jnp.pad(qkvr_master.astype(BF), ((0, 0), (0, WR - D), (0, WC - CG)))
    wo_own = proj_master.astype(BF)
    w1_own = expand_master.astype(BF)
    w2_own = reduce_master.T.astype(BF)
    b1_own = expbias_master.astype(BF).astype(F32)
    qkvr_oth = other(qkvr_own)
    small = other(jnp.concatenate([headbias_master.reshape(-1), b1_own]))
    wo_oth = other(wo_own)
    w1_oth = other(w1_own)
    w2_oth = other(w2_own)
    hb_oth = small[:2 * CG].reshape(2, CG)
    b1_oth = small[2 * CG:]
    meta = jnp.concatenate([head[None].astype(jnp.int32), lax.dynamic_slice_in_dim(first_flags, head * 2, 2, 0)])
    rows = positions(2 * SEG, D).astype(BF)
    tab = jnp.concatenate([rows[44:300], jnp.pad(rows, ((16, 68), (0, 0)))], 0)
    own = (qkvr_own, wo_own, headbias_master)
    oth = (qkvr_oth, wo_oth, hb_oth)
    att_own, p_own, *pre_own, _, x_rows = attention_fwd(True, meta, tokens.T, prior_memory, qkvr_own, wo_own, tab, headbias_master)
    att_oth, p_oth, *pre_oth, _ = attention_fwd(False, meta, x_rows, prior_memory, qkvr_oth, wo_oth, tab, hb_oth)
    lo_t, dres, ff_own, ff_oth = ff(
        att_own, att_oth, x_rows, cotangent.T, wo_own, wo_oth, w1_own, w1_oth, w2_own, w2_oth,
        jnp.concatenate([b1_own, b1_oth])[None], norms_master)
    ff_got = other(ff_oth)
    def back(streams, group, p, pre, base, half=False, prev=None):
        w4, wo, hb = group
        kv, wuv, wT, rel = pre
        return attention_bwd(streams, meta, x_rows, prior_memory, p, dres, base, w4, wo, wT, rel, tab, kv, wuv, half, prev)
    ig, at_oth = back((0, 1), oth, p_oth, pre_oth, dres, True)
    ff_got, at_oth, ig = lax.optimization_barrier((ff_got, at_oth, ig))
    at_got = other(at_oth)
    chunk = ff_own.shape[0] // n_dp
    half = (ff_own.astype(F32) + ff_got.astype(F32)).astype(BF).reshape(n_dp // 2, 2, chunk, HFP)
    odd = (dp & 1) == 1
    send = jnp.where(odd, half[:, 0], half[:, 1])
    keep = jnp.where(odd, half[:, 1], half[:, 0])
    pair = (keep.astype(F32) + dp_swap(send, 1).astype(F32)).astype(BF)
    pair, ig = lax.optimization_barrier((pair, ig))
    split = lax.all_to_all(pair, "dp", 0, 0, tiled=True, axis_index_groups=[list(range(c, n_dp, 2)) for c in range(2)])
    ig0, at0 = back((0,), own, p_own, pre_own, ig)
    part = jnp.sum(split.astype(F32), 0).astype(BF)
    part, ig0 = lax.optimization_barrier((part, ig0))
    ff_sum = lax.all_gather(part, "dp", axis=0, tiled=True)
    ig_t, at1 = back((1,), own, p_own, pre_own, ig, False, (ig0, at0))
    at_got, at1 = lax.optimization_barrier((at_got, at1))
    at_sum = (at1 + at_got.astype(F32)).astype(BF)
    bit = 1
    while bit < n_dp:
        part_rows = at_sum.shape[0] // 2
        up = (dp & bit) != 0
        send = jnp.where(up, at_sum[:part_rows], at_sum[part_rows:])
        keep = jnp.where(up, at_sum[part_rows:], at_sum[:part_rows])
        at_sum = (keep.astype(F32) + dp_swap(send, bit).astype(F32)).astype(BF)
        bit *= 2
    while bit > 1:
        bit //= 2
        got = dp_swap(at_sum, bit)
        up = (dp & bit) != 0
        at_sum = jnp.where(up, jnp.concatenate([got, at_sum], 0), jnp.concatenate([at_sum, got], 0))
    sq_own = squares(at_sum, ff_sum)
    sq_got = other(sq_own)
    flip = lambda v: jnp.transpose(v, (1, 0, 2))
    stats, *res = adam(
        owners, sq_own, sq_got, at_sum, ff_sum,
        (flip(qkvr_first), flip(qkvr_second), flip(qkvr_master)),
        (proj_first, proj_second, proj_master),
        (expand_first, expand_second, expand_master),
        (reduce_first.T, reduce_second.T, reduce_master.T),
        (headbias_first, headbias_second, headbias_master),
        (expbias_first, expbias_second, expbias_master),
        (norms_first, norms_second, norms_master))
    big = [[flip(v) for v in res[0:5]], res[5:10], res[10:15], [v.T for v in res[15:20]]]
    outs = [lo_t.T, ig_t.T, stats[0, :7]]
    for r in big:
        outs += r[:4]
    outs += res[20:32]
    return tuple(outs + [r[4] for r in big])


def solution(mesh):
    in_specs = (
        P(("dp", "head"), None),
        P("dp", None, None),
        P("dp"),
        P(),
        P(("dp", "head"), None),
        P(None, None, "head"),
        P(None, None, "head"),
        P(None, None, "head"),
        P("head", None),
        P("head", None),
        P("head", None),
        P(None, "head"),
        P(None, "head"),
        P(None, "head"),
        P("head", None),
        P("head", None),
        P("head", None),
        P(None, "head"),
        P(None, "head"),
        P(None, "head"),
        P("head"),
        P("head"),
        P("head"),
        P(),
        P(),
        P(),
    )
    out_specs = (
        P(("dp", "head"), None),
        P(("dp", "head"), None),
        P(),
        P(None, None, "head"),
        P(None, None, "head"),
        P(None, None, "head"),
        P(None, None, "head"),
        P("head", None),
        P("head", None),
        P("head", None),
        P("head", None),
        P(None, "head"),
        P(None, "head"),
        P(None, "head"),
        P(None, "head"),
        P("head", None),
        P("head", None),
        P("head", None),
        P("head", None),
        P(None, "head"),
        P(None, "head"),
        P(None, "head"),
        P(None, "head"),
        P("head"),
        P("head"),
        P("head"),
        P("head"),
        P(),
        P(),
        P(),
        P(),
        P(None, None, "head"),
        P("head", None),
        P(None, "head"),
        P("head", None),
    )
    return jax.shard_map(shards, mesh=mesh, in_specs=in_specs, out_specs=out_specs, check_vma=False)
```

```python
from jax.sharding import PartitionSpec as P
import math, functools
import jax, jax.numpy as jnp
from jax import lax
from jax.experimental import pallas as pl
from jax.experimental.pallas import tpu as pltpu
BF=jnp.bfloat16; F32=jnp.float32
NT=(((1,),(1,)),((),())); TN=(((0,),(0,)),((),()))
def dot(a,b,dn=(((1,),(0,)),((),()))): return lax.dot_general(a,b,dn,preferred_element_type=F32)
SEG=150; NSEG=8; LEN=1200; DH=41; HG=5; CG=205; D=410
RA=96; RQ=160; KA_=256; KB_=384; KC=304
HP=48; GP=HP*HG
LV={2:RA,3:56}
def fill(v,rows):
    return v if v.shape[0]==rows else jnp.concatenate([v,jnp.zeros((rows-v.shape[0],v.shape[1]),v.dtype)],0)
SCALE=1.0/math.sqrt(DH); LOG2E=1.4426950408889634

def fill_rows(x_rows, prior_ref, xs, xcat, xq):
    xs[0:SEG,:]=prior_ref[0].astype(F32)
    xs[SEG:SEG+LEN,:]=x_rows.astype(F32)
    xs[SEG+LEN:1376,:]=jnp.zeros((1376-SEG-LEN,D),F32)
    for s in range(NSEG):
        xcat[s]=xs[SEG*s:SEG*s+KC,:].astype(BF)
        xq[s]=xs[SEG*(s+1):SEG*(s+1)+RQ,:].astype(BF)

def head_masks(rows):
    lane=lax.broadcasted_iota(jnp.int32,(rows,CG),1)
    return [(lane>=DH*h)&(lane<DH*(h+1)) for h in range(HG)]

U=4
GU=4
WR=416; WC=256
def ka_kernel(first, meta, x_ref, prior_ref, w4p, wo, tab, bias, att_ref, p_ref, kv_ref, wuv_ref, wT_ref, rel_ref, bT_ref, *rest):
    if first: xn_ref, xs, xcat, xq, attS, biasA, biasB = rest
    else: xs, xcat, xq, attS, biasA, biasB = rest
    w4=[w4p[k,0:D,0:CG] for k in range(4)]
    n=pl.program_id(0); st=pl.program_id(1)
    @pl.when((st==0)&(n==0))
    def _():
        rel_ref[...]=dot(tab[...],w4[3]).astype(BF)
        xs[0:GP,:]=jnp.zeros((GP,D),F32)
        for k in range(4):
            src=w4[k].astype(F32).T if k<3 else wo[...].astype(F32)
            for h in range(HG): xs[HP*h:HP*h+DH,:]=src[DH*h:DH*h+DH]
            wT_ref[k]=xs[0:GP,:].astype(BF)
        bt=jnp.concatenate([bias[...],jnp.zeros((6,CG),F32)],0).T
        xs[0:GP,0:8]=jnp.zeros((GP,8),F32)
        for h in range(HG): xs[HP*h:HP*h+DH,0:8]=bt[DH*h:DH*h+DH]
        bT_ref[...]=xs[0:GP,0:8]
    @pl.when(st==0)
    def _():
        if first:
            @pl.when(n==0)
            def _():
                tiles=2*LEN//128
                for t in range(tiles): xn_ref[128*t:128*t+128,:]=x_ref[:,128*t:128*t+128].T
                xn_ref[128*tiles:,:]=x_ref[:,128*tiles:].T
            fill_rows(xn_ref[pl.ds(pl.multiple_of(n*LEN,16),LEN),:],prior_ref,xs,xcat,xq)
        else: fill_rows(x_ref[...],prior_ref,xs,xcat,xq)
    NA=RA; NB=RQ-RA
    has_mem=(st>0)|(meta[1+n]==1)
    jmin=jnp.where(has_mem,0,SEG)
    @pl.when(st==0)
    def _():
        for u in range(U):
            jm=jmin if u==0 else 0
            i=lax.broadcasted_iota(jnp.int32,(RA,KA_),0); j=lax.broadcasted_iota(jnp.int32,(RA,KA_),1)
            biasA[u]=jnp.where((j<=i+SEG)&(j>=jm),0.0,-1e30)
            i=lax.broadcasted_iota(jnp.int32,(NB,KB_),0)+RA; j=lax.broadcasted_iota(jnp.int32,(NB,KB_),1)
            biasB[u]=jnp.where((j<=i+SEG)&(j>=jm)&(j<2*SEG),0.0,-1e30)
    @pl.when(st==1)
    def _():
        biasA[0]=biasA[1]; biasB[0]=biasB[1]
    hm=head_masks(RQ)
    hmA=[m[0:RA] for m in hm]; hmB=[m[RA:] for m in hm]
    zero=jnp.zeros((),BF)
    iA=lax.broadcasted_iota(jnp.int32,(RA,128),0); lA=lax.broadcasted_iota(jnp.int32,(RA,128),1)
    mA=(lA+(105-iA))<128
    iB=lax.broadcasted_iota(jnp.int32,(NB,128),0); lB=lax.broadcasted_iota(jnp.int32,(NB,128),1)
    mB=(lB+(69-iB))<128
    c=SCALE*LOG2E
    vv=[None]*U
    def scores(u):
        s=st*U+u
        xc=xcat[s]
        zr=jnp.zeros((KB_-KC,CG),BF)
        kk=jnp.concatenate([dot(xc,w4[1]).astype(BF),zr],0)
        vv[u]=jnp.concatenate([dot(xc,w4[2]).astype(BF),zr],0)
        qT=dot(wT_ref[0],xq[s],NT).astype(BF).astype(F32)
        lateT.append((u,kk,vv[u],(qT+bT_ref[:,0:1]).astype(BF),(qT+bT_ref[:,1:2]).astype(BF)))
        q=dot(xq[s],w4[0]).astype(BF).astype(F32)
        wu=(q+bias[0:1,:]).astype(BF); wvv=(q+bias[1:2,:]).astype(BF)
        wum=[jnp.where(m,wu,zero) for m in hm]
        wvm=[jnp.where(m,wvv,zero) for m in hm]
        SA=dot(jnp.concatenate([w[0:RA] for w in wum],0),kk[0:KA_],NT)
        PA=dot(jnp.concatenate([w[0:RA] for w in wvm],0),rel_ref[0:KA_],NT)
        SB=dot(jnp.concatenate([w[RA:] for w in wum],0),kk,NT)
        PB=dot(jnp.concatenate([w[RA:] for w in wvm],0),rel_ref[KA_:],NT)
        return SA,PA,SB,PB
    def soft(u,sc):
        SA,PA,SB,PB=sc
        units=[]
        for h in range(HG):
            units.append((h,SA,PA,NA,2,0,23,biasA,mA)); units.append((h,SB,PB,NB,3,RA,59,biasB,mB))
        out=[]
        for i0 in range(0,len(units),GU):
            grp=units[i0:i0+GU]
            rolls=[[pltpu.roll(P_[R*h:R*h+min(R,LV[nt]),128*k:128*k+128],b0,1,stride=1,stride_axis=0) for k in range(nt)] for (h,S_,P_,R,nt,r0,b0,bs,m) in grp]
            ts=[]
            for (h,S_,P_,R,nt,r0,b0,bs,m),rr in zip(grp,rolls):
                L=LV[nt]
                ts.append([(S_[R*h:R*h+L,128*k:128*k+128]+(jnp.where(m[0:L],rr[k],rr[k+1]) if k+1<nt else rr[k]))*c+bs[u,0:L,128*k:128*k+128] for k in range(nt)])
            mxs=[]
            for t in ts:
                mx=t[0]
                for v in t[1:]: mx=jnp.maximum(mx,v)
                mxs.append(mx)
            mxs=[jnp.max(v,axis=1,keepdims=True) for v in mxs]
            es=[[jnp.exp2(v-mx) for v in t] for t,mx in zip(ts,mxs)]
            sms=[]
            for e in es:
                sm=e[0]
                for v in e[1:]: sm=sm+v
                sms.append(sm)
            lis=[1.0/jnp.sum(v,axis=1,keepdims=True) for v in sms]
            for (h,S_,P_,R,nt,r0,b0,bs,m),e,li in zip(grp,es,lis):
                p=jnp.concatenate([fill(v*li,R).astype(BF) for v in e],1)
                late.append((u,h,r0,R,nt,p))
                out.append(p)
        return out[0::2],out[1::2]
    def outp(u,pp):
        pas,pbs=pp
        s=st*U+u
        OA=dot(jnp.concatenate(pas,0),vv[u][0:KA_])
        OB=dot(jnp.concatenate(pbs,0),vv[u])
        aA=OA[0:NA]; aB=OB[0:NB]
        for h in range(1,HG):
            aA=jnp.where(hmA[h],OA[NA*h:NA*(h+1)],aA)
            aB=jnp.where(hmB[h],OB[NB*h:NB*(h+1)],aB)
        lateA.append((s,aA,aB))
    sc=[None]*U; pp=[None]*U; late=[]; lateA=[]; lateT=[]
    sc[0]=scores(0)
    for u in range(U):
        if u+1<U: sc[u+1]=scores(u+1)
        pp[u]=soft(u,sc[u])
        if u>0: outp(u-1,pp[u-1])
    outp(U-1,pp[U-1])
    for (u,h,r0,R,nt,p) in late: p_ref[0,u,h,r0:r0+R,0:128*nt]=p
    for (u,a,b,c_,d_) in lateT:
        kv_ref[0,u,0]=a[0:KC]; kv_ref[0,u,1]=b[0:KC]; wuv_ref[0,u,0]=c_; wuv_ref[0,u,1]=d_
    for (s,aA,aB) in lateA:
        attS[s,0:RA,:]=aA
        attS[s,RA:RQ,:]=aB
    @pl.when(st==NSEG//U-1)
    def _():
        for t in range(NSEG):
            xs[SEG*t:SEG*t+152,0:CG]=attS[t,0:152,:]
        att_ref[...]=xs[0:LEN,0:CG].astype(BF)

def attention_fwd(first,meta,x,prior,w4,wo,tab,bias):
    cst=lambda *sh: pl.BlockSpec(sh,lambda n,s,m: (0,)*len(sh))
    S=jax.ShapeDtypeStruct
    gs=pltpu.PrefetchScalarGridSpec(num_scalar_prefetch=1,grid=(2,NSEG//U),
      in_specs=[cst(D,2*LEN) if first else pl.BlockSpec((LEN,D),lambda n,s,m:(n,0)),
        pl.BlockSpec((1,SEG,D),lambda n,s,m:(m[0]*2+n,0,0)),
        cst(4,WR,WC),cst(CG,D),cst(KA_+KB_,D),cst(2,CG)],
      out_specs=[pl.BlockSpec((LEN,CG),lambda n,s,m:(n,0)),
        pl.BlockSpec((1,U,HG,RQ,KB_),lambda n,s,m:(n,s,0,0,0)),pl.BlockSpec((1,U,2,KC,CG),lambda n,s,m:(n,s,0,0,0)),pl.BlockSpec((1,U,2,GP,RQ),lambda n,s,m:(n,s,0,0,0)),cst(4,GP,D),cst(KA_+KB_,CG),cst(GP,8)]+([cst(2*LEN,D)] if first else []),
      scratch_shapes=[pltpu.VMEM((1376,D),F32),pltpu.VMEM((NSEG,KC,D),BF),pltpu.VMEM((NSEG,RQ,D),BF),
        pltpu.VMEM((NSEG,RQ,CG),F32),
        pltpu.VMEM((U,RA,KA_),F32),pltpu.VMEM((U,RQ-RA,KB_),F32)])
    return pl.pallas_call(functools.partial(ka_kernel,first),grid_spec=gs,name="attn_fwd",
      out_shape=[S((2*LEN,CG),BF),S((2,NSEG,HG,RQ,KB_),BF),S((2,NSEG,2,KC,CG),BF),S((2,NSEG,2,GP,RQ),BF),S((4,GP,D),BF),S((KA_+KB_,CG),BF),S((GP,8),F32)]+([S((2*LEN,D),BF)] if first else []),
      compiler_params=pltpu.CompilerParams(vmem_limit_bytes=56*2**20))(meta,x,prior,w4,wo,tab,bias)

CLIP_LEVEL = 0.01
BETA_ONE = 0.5
BETA_TWO = 0.5
ADAM_EPSILON = 1e-08
WEIGHT_DECAY = 0.1
STEP = 10
STEP_RATES = (0.03, 0.2, 0.03, 0.015, 0.3, 0.3, 0.3)
T=480; HF=1050; HFP=1152
G0=0.7978845608028654; G1=0.044715; EPS=1e-5
def ln_fwd(z):
    m=jnp.mean(z,axis=-1,keepdims=True)
    c=z-m
    v=jnp.mean(c*c,axis=-1,keepdims=True)
    r=lax.rsqrt(v+EPS)
    return c*r,r
def ln_bwd(n,r,e):
    return r*(e-jnp.mean(e,axis=-1,keepdims=True)-n*jnp.mean(e*n,axis=-1,keepdims=True))
def kf_kernel(ao,at,x,ct,woo,wot,w1o,w1t,w2o,w2t,b1,nm, lo_ref,dres_ref,g_o,g_t,awo_o,awo_t,aw1,aw2,gnm_acc,ctS,w1c,w2c):
    i=pl.program_id(0); last=pl.num_programs(0)-1
    @pl.when(i==0)
    def _():
        for r in (awo_o,awo_t,aw1,aw2,gnm_acc): r[...]=jnp.zeros(r.shape,F32)
        for r,u,v in ((w1c,w1o,w1t),(w2c,w2o,w2t)):
            r[...]=jnp.concatenate([u[...].astype(F32),v[...].astype(F32)],1).astype(BF)
    @pl.when(i==0)
    def _():
        tiles=ctS.shape[0]//128
        for t in range(tiles): ctS[128*t:128*t+128,:]=ct[:,128*t:128*t+128].T
        if tiles*128<ctS.shape[0]: ctS[128*tiles:,:]=ct[:,128*tiles:].T
    c=ctS[pl.ds(i*T,T),:]
    attn=dot(ao[...],woo[...])+dot(at[...],wot[...])
    z=x[...].astype(F32)+attn
    n1,r1=ln_fwd(z)
    normed=n1*nm[0:1]+nm[1:2]
    nl=normed.astype(BF)
    def gate(pre):
        p2=pre*pre
        t=jnp.tanh(G0*pre*(1.0+G1*p2))
        hp=0.5*(1.0+t)
        act=pre*hp
        der=hp+0.5*pre*(1.0-t*t)*(G0*(1.0+3.0*G1*p2))
        return act.astype(BF),der
    parts=((0,768),(768,1536),(1536,2*HF))
    pres=[dot(nl,w1c[:,lo:hi])+b1[:,lo:hi] for lo,hi in parts[:1]]
    acts=[];ders=[]
    second=normed+nm[2:3]
    for k,(lo,hi) in enumerate(parts):
        if k+1<len(parts):
            l2,h2=parts[k+1]
            pres.append(dot(nl,w1c[:,l2:h2])+b1[:,l2:h2])
        a_,d_=gate(pres[k])
        acts.append(a_); ders.append(d_)
        second=second+dot(a_,w2c[:,lo:hi],NT)
    n2,r2=ln_fwd(second)
    lo_ref[...]=n2*nm[3:4]+nm[4:5]
    d2=ln_bwd(n2,r2,c*nm[3:4])
    d2l=d2.astype(BF)
    dn=d2
    for k,(lo,hi) in enumerate(parts):
        dpre=dot(d2l,w2c[:,lo:hi])*ders[k]
        aw2[0:D,lo:hi]+=dot(d2l,acts[k],TN)
        aw1[D:D+1,lo:hi]+=jnp.sum(dpre,axis=0,keepdims=True)
        dpl=dpre.astype(BF)
        aw1[0:D,lo:hi]+=dot(nl,dpl,TN)
        dn=dn+dot(dpl,w1c[:,lo:hi],NT)
    dz=ln_bwd(n1,r1,dn*nm[0:1])
    dres_ref[...]=dz
    dal=dz.astype(BF)
    awo_o[0:CG]+=dot(ao[...],dal,TN)
    awo_t[0:CG]+=dot(at[...],dal,TN)
    gnm=jnp.concatenate([jnp.sum(v,axis=0,keepdims=True) for v in (dn*n1,dn,d2,c*n2,c)],0)
    gnm_acc[0:5]+=gnm
    @pl.when(i==last)
    def _():
        aw2[D:D+5,0:D]=gnm_acc[0:5]
        aw2[D:D+5,HF:HF+D]=gnm_acc[0:5]
        for g,lo,aw in ((g_o,0,awo_o),(g_t,HF,awo_t)):
            g[:,1024:HFP]=jnp.zeros((1024,HFP-1024),BF)
            g[0:416,0:HF]=aw1[:,lo:lo+HF].astype(BF)
            g[416:448,0:1024]=jnp.zeros((32,1024),BF)
            g[448:864,0:HF]=aw2[:,lo:lo+HF].astype(BF)
            g[864:1024,0:1024]=jnp.zeros((160,1024),BF)
            g[896:1008,0:D]=aw[0:112].astype(BF)
            g[896:1008,512:512+D]=aw[112:224].astype(BF)
def ff(ao,at,x,ct,woo,wot,w1o,w1t,w2o,w2t,b1,nm):
    n=x.shape[0]
    row=lambda w: pl.BlockSpec((T,w),lambda i:(i,0))
    cst=lambda *sh: pl.BlockSpec(sh,lambda i:(0,)*len(sh),pipeline_mode=pl.Buffered(1))
    S=jax.ShapeDtypeStruct
    gs=[(1024,HFP),(1024,HFP)]
    spec=pl.GridSpec(grid=(n//T,),
      in_specs=[row(CG),row(CG),row(D),cst(D,n),cst(CG,D),cst(CG,D),cst(D,HF),cst(D,HF),cst(D,HF),cst(D,HF),cst(1,2*HF),cst(5,D)],
      out_specs=[row(D),row(D)]+[cst(*s) for s in gs],
      scratch_shapes=[pltpu.VMEM((224,D),F32)]*2+[pltpu.VMEM((416,2*HF),F32)]*2+[pltpu.VMEM((8,D),F32),pltpu.VMEM((n,D),F32)]+[pltpu.VMEM((D,2*HF),BF)]*2)
    return pl.pallas_call(kf_kernel,name="ff",grid_spec=spec,
      out_shape=[S((n,D),F32),S((n,D),F32)]+[S(s,BF) for s in gs],
      compiler_params=pltpu.CompilerParams(vmem_limit_bytes=60*2**20))(ao,at,x,ct,woo,wot,w1o,w1t,w2o,w2t,b1,nm)
def rev8(v):
    idx=7-lax.broadcasted_iota(jnp.int32,v.shape,0)
    return jnp.take_along_axis(v,idx,axis=0)
def unskew(blocks, base, rows):
    nb=len(blocks)
    lane=lax.broadcasted_iota(jnp.int32,(8,128),1); sub=lax.broadcasted_iota(jnp.int32,(8,128),0)
    outs=[[] for _ in blocks]
    for r in range(rows//8):
        sh=base-8*r-7
        rot=[pltpu.roll(rev8(b[8*r:8*r+8]),sh%128,1,stride=1,stride_axis=0) for b in blocks]
        m=lane<(sh+sub)
        for k in range(nb):
            if k==0: o=jnp.where(m,0.0,rot[0])
            else: o=jnp.where(m,rot[k-1],rot[k])
            outs[k].append(rev8(o))
    return [jnp.concatenate(o,0) for o in outs]

UB=4
def kb_kernel(last, half, meta, x_ref, prior_ref, p_ref, dres_ref, *rest):
    if half: base_ref=dres_ref
    else: base_ref, *rest = rest
    w4p, wo, wT, rel, tab, kv_ref, wuv_ref, *rest = rest
    w4=[w4p[k,0:D,0:CG] for k in range(3)]
    if last:
        prev_ref, gp_ref, ig_ref, g_ref, xs, xcat, xq, dalS, ig, acc, drA, drB, dbias, G = rest
    else:
        ig_ref, g_ref, xs, xcat, xq, dalS, ig, acc, drA, drB, dbias, G = rest
    n=pl.program_id(0); st=pl.program_id(1)
    NA=RA; NB=RQ-RA
    @pl.when((st==0)&(n==0))
    def _():
        for r in (acc,drA,drB,dbias): r[...]=jnp.zeros(r.shape,F32)
    @pl.when(st==0)
    def _():
        xs[LEN:1376,:]=jnp.zeros((1376-LEN,D),F32)
        xs[0:LEN,:]=dres_ref[...]
        rows=lax.broadcasted_iota(jnp.int32,(RQ,D),0)
        for t in range(NSEG):
            dalS[t]=jnp.where(rows<SEG,xs[SEG*t:SEG*t+RQ,:],0.0).astype(BF)
        fill_rows(x_ref[...],prior_ref,xs,xcat,xq)
        xs[SEG:SEG+LEN,:]=base_ref[...]
        for t in range(NSEG+1):
            ig[t]=xs[SEG*t:SEG*t+152,:]
    hm=head_masks(RQ)
    zero=jnp.zeros((),BF)
    zr=jnp.zeros((KB_-KC,CG),BF)
    wkvT=wT[1:3].reshape(2*GP,D); woT=wT[3]
    def front(u):
        s=st*UB+u
        dal=dalS[s]
        kk=jnp.concatenate([kv_ref[0,u,0],zr],0)
        vv=jnp.concatenate([kv_ref[0,u,1],zr],0)
        wuT=wuv_ref[0,u,0]; wvT=wuv_ref[0,u,1]
        da=dot(dal,wo[...],NT).astype(BF)
        daT=dot(woT,dal,NT).astype(BF)
        dam=[jnp.where(m,da,zero) for m in hm]
        DA=dot(jnp.concatenate([w[0:RA] for w in dam],0),vv[0:KA_],NT)
        DB=dot(jnp.concatenate([w[RA:] for w in dam],0),vv,NT)
        ps=[(p_ref[0,u,h,0:RA,0:KA_],p_ref[0,u,h,RA:RQ,:]) for h in range(HG)]
        return kk,wuT,wvT,daT,DA,DB,ps
    def mid(fr):
        kk,wuT,wvT,daT,DA,DB,ps=fr
        res=[]
        for h in range(HG):
            one=[]
            for p,dp,R,nt,base in ((ps[h][0],DA[NA*h:NA*(h+1)],NA,2,105),(ps[h][1],DB[NB*h:NB*(h+1)],NB,3,69)):
                L=LV[nt]
                pf=p.astype(F32)[0:L]; dp=dp[0:L]
                w=dp*pf
                sm=w[:,0:128]
                for k in range(1,nt): sm=sm+w[:,128*k:128*k+128]
                delta=jnp.sum(sm,axis=1,keepdims=True)
                dr=(pf*SCALE)*(dp-delta)
                o=unskew([dr[:,128*k:128*k+128] for k in range(nt)],base,L)
                one.append((fill(dr,R).astype(BF),jnp.concatenate([fill(v,R).astype(BF) for v in o],1)))
            res.append(one)
        return res
    late=[]
    def back(u,fr,md):
        kk,wuT,wvT,daT,DA,DB,ps=fr
        s=st*UB+u
        dkT=[];dvT=[];rA=[];rB=[]
        for h in range(HG):
            (ra,pa_),(rb,pb_)=md[h]
            u_=wuT[HP*h:HP*(h+1)]; v_=wvT[HP*h:HP*(h+1)]; d_=daT[HP*h:HP*(h+1)]
            pA,pB=ps[h]
            k1=dot(u_,jnp.concatenate([ra,rb[:,0:KA_]],0)); k2=dot(u_[:,RA:],rb[:,KA_:])
            dkT.append(jnp.concatenate([k1,k2],1))
            v1=dot(d_,jnp.concatenate([pA,pB[:,0:KA_]],0)); v2=dot(d_[:,RA:],pB[:,KA_:])
            dvT.append(jnp.concatenate([v1,v2],1))
            rA.append(dot(v_[:,0:RA],pa_)); rB.append(dot(v_[:,RA:],pb_))
        def comb(col,mA_,mB_):
            OA=dot(jnp.concatenate([md[h][0][col] for h in range(HG)],0),mA_)
            OB=dot(jnp.concatenate([md[h][1][col] for h in range(HG)],0),mB_)
            aA=OA[0:NA]; aB=OB[0:NB]
            for h in range(1,HG):
                aA=jnp.where(hm[h][0:RA],OA[NA*h:NA*(h+1)],aA)
                aB=jnp.where(hm[h][RA:],OB[NB*h:NB*(h+1)],aB)
            return aA,aB
        uA,uB=comb(0,kk[0:KA_],kk)
        vA,vB=comb(1,rel[0:KA_],rel[KA_:])
        db=jnp.concatenate([jnp.sum(uA,0,keepdims=True)+jnp.sum(uB,0,keepdims=True),jnp.sum(vA,0,keepdims=True)+jnp.sum(vB,0,keepdims=True)],0)
        dq=jnp.concatenate([(uA+vA).astype(BF),(uB+vB).astype(BF)],0)
        dk=jnp.concatenate(dkT,0).astype(BF); dv=jnp.concatenate(dvT,0).astype(BF)
        xc=xcat[s]; xqs=xq[s]
        kv=jnp.concatenate([dk[:,0:KC],dv[:,0:KC]],0)
        gkv=dot(kv,xc)
        gq=dot(dq,xqs,TN)
        late.append((u,s,jnp.concatenate(rA,0),jnp.concatenate(rB,0),db,gkv,gq,dot(kv,wkvT,TN),dot(dq,w4[0],NT)[0:152]))
    frs=[None]*UB; mds=[None]*UB
    frs[0]=front(0)
    for u in range(UB):
        if u+1<UB: frs[u+1]=front(u+1)
        mds[u]=mid(frs[u])
        if u>0: back(u-1,frs[u-1],mds[u-1])
    back(UB-1,frs[UB-1],mds[UB-1])
    for (u,s,rA,rB,db,gkv,gq,g1,g2) in late:
        drA[...]+=rA; drB[...]+=rB
        dbias[0:2]+=db
        acc[0,0:CG]+=gq
        acc[1]+=gkv[0:GP]; acc[2]+=gkv[GP:]
        G[...]=g1
        ig[s+1]+=g2+G[SEG:SEG+152,:]
        ig[s]+=G[0:152,:]
    @pl.when(st==NSEG//UB-1)
    def _():
        for t in range(NSEG):
            xs[SEG*t:SEG*t+152,:]=ig[t+1]
        ig_ref[...]=xs[0:LEN,:]
    @pl.when((st==NSEG//UB-1)&(n==pl.num_programs(0)-1))
    def _():
        a=jnp.concatenate([drA[...],jnp.zeros((GP,KB_-KA_),F32)],1)
        dr=drB[...]+pltpu.roll(a,60,1)
        acc[3]=dot(dr.astype(BF),tab[KA_:,:])
        xs[0:CG,:]=acc[0,0:CG]
        for k in range(1,4):
            for h in range(HG):
                o=CG*k+DH*h
                xs[o:o+DH,:]=acc[k,HP*h:HP*h+DH]
        xs[4*CG:832,:]=jnp.zeros((832-4*CG,D),F32)
        xs[4*CG:4*CG+2,0:CG]=dbias[0:2]
        g_ref[:,384:512]=jnp.zeros((832,128),g_ref.dtype)
        if last:
            g_ref[:,0:D]=xs[0:832,:]+gp_ref[:,0:D]
        else:
            g_ref[:,0:D]=xs[0:832,:].astype(g_ref.dtype)

def attention_bwd(streams,meta,x,prior,p,dres,base,w4,wo,wT,rel,tab,kv,wuv,half=False,prev=None):
    cst=lambda *sh: pl.BlockSpec(sh,lambda n,s,m: (0,)*len(sh))
    off=streams[0]; ns=len(streams); last=prev is not None
    row=lambda w: pl.BlockSpec((LEN,w),lambda n,s,m:(n+off,0))
    S=jax.ShapeDtypeStruct
    ig_spec=row(D); ig_shape=S((2*LEN,D),F32)
    gs=pltpu.PrefetchScalarGridSpec(num_scalar_prefetch=1,grid=(ns,NSEG//UB),
      in_specs=[row(D),pl.BlockSpec((1,SEG,D),lambda n,s,m:(m[0]*2+n+off,0,0)),
        pl.BlockSpec((1,UB,HG,RQ,KB_),lambda n,s,m:(n+off,s,0,0,0)),row(D)]+([] if half else [row(D)])+[
        cst(4,WR,WC),cst(CG,D),cst(4,GP,D),cst(KA_+KB_,CG),cst(KA_+KB_,D),pl.BlockSpec((1,UB,2,KC,CG),lambda n,s,m:(n+off,s,0,0,0)),pl.BlockSpec((1,UB,2,GP,RQ),lambda n,s,m:(n+off,s,0,0,0))]+([pl.BlockSpec(memory_space=pl.ANY),cst(832,512)] if last else []),
      out_specs=[ig_spec,cst(832,512)],
      scratch_shapes=[pltpu.VMEM((1376,D),F32),pltpu.VMEM((NSEG,KC,D),BF),pltpu.VMEM((NSEG,RQ,D),BF),pltpu.VMEM((NSEG,RQ,D),BF),
        pltpu.VMEM((NSEG+1,152,D),F32),pltpu.VMEM((4,GP,D),F32),pltpu.VMEM((GP,KA_),F32),pltpu.VMEM((GP,KB_),F32),pltpu.VMEM((8,CG),F32),pltpu.VMEM((KC,D),F32)])
    ops=[meta,x,prior,p,dres]+([] if half else [base])+[w4,wo,wT,rel,tab,kv,wuv]+(list(prev) if last else [])
    return pl.pallas_call(functools.partial(kb_kernel,last,half),grid_spec=gs,name="attn_bwd",
      input_output_aliases={13:0} if last else {},
      out_shape=[ig_shape,S((832,512),BF if half else F32)],
      compiler_params=pltpu.CompilerParams(vmem_limit_bytes=62*2**20))(*ops)
RB=112
COUNTS=(4*D*D,D*D,D*2*HF,D*2*HF,2*D,2*HF,5*D)
def sq_kernel(at, f, out):
    a=at[...].astype(F32); a=a*a
    rows=lax.broadcasted_iota(jnp.int32,(832,512),0)
    tot=lambda v: jnp.sum(jnp.sum(v,axis=0,keepdims=True),axis=1,keepdims=True)
    t0=tot(jnp.where(rows<4*CG,a,0.0)); t4=tot(a[816:832])-tot(jnp.where(rows[816:832]<4*CG,a[816:832],0.0))
    def part(lo,n):
        v=f[lo:lo+n].astype(F32)
        return v*v
    w=part(0,416); r=lax.broadcasted_iota(jnp.int32,(416,HFP),0)
    t2=tot(jnp.where(r<D,w,0.0)); t5=tot(jnp.where(r[400:416]==D,w[400:416],0.0))
    w=part(448,416)
    t3=tot(jnp.where(r<D,w,0.0)); t6=tot(jnp.where(r[400:416]>=D,w[400:416],0.0))
    t1=tot(part(896,112))
    row=lax.broadcasted_iota(jnp.int32,(8,128),0)
    acc=jnp.zeros((8,128),F32)
    for k,t in enumerate((t0,t1,t2,t3,t4,t5,t6)): acc=jnp.where(row==k,t,acc)
    out[...]=acc

def squares(at,f):
    v=pl.BlockSpec(memory_space=pltpu.VMEM)
    return pl.pallas_call(sq_kernel,name="squares",in_specs=[v,v],out_specs=v,out_shape=jax.ShapeDtypeStruct((8,128),F32),
        compiler_params=pltpu.CompilerParams(vmem_limit_bytes=62*2**20))(at,f)

def adam_math(g,m,v,w,clip,rate):
    c=g*clip
    m2=BETA_ONE*m+(1.0-BETA_ONE)*c
    v2=BETA_TWO*v+(1.0-BETA_TWO)*c*c
    mh=m2*(1.0/(1.0-BETA_ONE**STEP)); vh=v2*(1.0/(1.0-BETA_TWO**STEP))
    w2=w-rate*(mh/(jnp.sqrt(vh)+ADAM_EPSILON)+WEIGHT_DECAY*w)
    return c,m2,v2,w2

QB=128
def adam_kernel(own, so, sg, at, ff, g1, g2, gm, gv, gw, pm, pv, pw, em, ev, ew, rm, rv, rw, hm_, hv_, hw_, bm_, bv_, bw_, nm_, nv_, nw_, rms_ref, *rest):
    i=pl.program_id(0)
    outs=rest[:-1]; g3=rest[-1]
    tot=[so[k,0]+sg[k,0] if k<6 else so[k,0] for k in range(7)]
    clips=[]; lane=lax.broadcasted_iota(jnp.int32,(1,128),1); rms=jnp.zeros((1,128),F32)
    for k in range(7):
        num=jnp.float32(0); den=jnp.float32(0)
        for j in range(7):
            same=own[k]==own[j]
            num=num+jnp.where(same,tot[j],0.0); den=den+jnp.where(same,jnp.float32(COUNTS[j]),0.0)
        ms=jnp.full((1,128),num,F32)/jnp.full((1,128),den,F32)
        c=jnp.minimum(1.0,CLIP_LEVEL*lax.rsqrt(ms+1e-6))
        clips.append(c[0:1,0:1]); rms=jnp.where(lane==k,jnp.sqrt(ms),rms)
    rms_ref[...]=rms
    def put(o,res):
        for r,v in zip(o[:4],res): r[...]=v
        if len(o)>4: o[4][...]=res[3].astype(BF)
    put(outs[10:15],adam_math(g1[:,0:HF].astype(F32),em[...],ev[...],ew[...],clips[2],STEP_RATES[2]))
    put(outs[15:20],adam_math(g2[:,0:HF].astype(F32),rm[...],rv[...],rw[...],clips[3],STEP_RATES[3]))
    blk=at[:,pl.ds(pl.multiple_of(i*QB,QB),QB)].astype(F32)
    for k in range(4): g3[:,k,:]=blk[CG*k:CG*k+CG].T
    put(outs[0:5],adam_math(g3[...],gm[...],gv[...],gw[...],clips[0].reshape(1,1,1),STEP_RATES[0]))
    @pl.when(i==0)
    def _():
        for lo,hi,l in ((0,112,0),(112,CG,512)):
            g=ff[896:896+hi-lo,l:l+D].astype(F32)
            res=adam_math(g,pm[lo:hi],pv[lo:hi],pw[lo:hi],clips[1],STEP_RATES[1])
            for r,v in zip(outs[5:9],res): r[lo:hi]=v
            outs[9][lo:hi]=res[3].astype(BF)
        put(outs[20:24],adam_math(at[816:832,:].astype(F32)[4*CG-816:4*CG-814,0:CG],hm_[...],hv_[...],hw_[...],clips[4],STEP_RATES[4]))
        put(outs[24:28],adam_math(ff[400:416,:].astype(F32)[D-400,0:HF],bm_[...],bv_[...],bw_[...],clips[5][0],STEP_RATES[5]))
        put(outs[28:32],adam_math(ff[848:864,:].astype(F32)[10:15,0:D],nm_[...],nv_[...],nw_[...],clips[6],STEP_RATES[6]))

def adam(owners,so,sg,at,f,q3,p3,e3,r3,h3,b3,n3):
    S=jax.ShapeDtypeStruct
    one=pl.Buffered(1)
    cst=lambda *sh: pl.BlockSpec(sh,lambda i,o:(0,)*len(sh),pipeline_mode=one)
    bq=pl.BlockSpec((QB,4,CG),lambda i,o:(i,0,0)); be=pl.BlockSpec((RB,HF),lambda i,o:(i,0)); bp=cst(CG,D)
    bh,bb,bn=cst(2,CG),cst(HF),cst(5,D)
    sm=pl.BlockSpec(memory_space=pltpu.SMEM)
    spec=pltpu.PrefetchScalarGridSpec(num_scalar_prefetch=1,grid=(4,),
      in_specs=[sm,sm,cst(832,512),cst(1024,HFP),pl.BlockSpec((RB,HFP),lambda i,o:(i,0)),pl.BlockSpec((RB,HFP),lambda i,o:(4+i,0))]+[bq]*3+[bp]*3+[be]*6+[bh]*3+[bb]*3+[bn]*3,
      out_specs=[cst(1,128)]+[bq]*5+[bp]*5+[be]*10+[bh]*4+[bb]*4+[bn]*4,
      scratch_shapes=[pltpu.VMEM((QB,4,CG),F32)])
    outs=[S((1,128),F32)]
    for sh in ((D,4,CG),(CG,D),(D,HF),(D,HF)): outs+= [S(sh,F32)]*4+[S(sh,BF)]
    for sh in ((2,CG),(HF,),(5,D)): outs+=[S(sh,F32)]*4
    return pl.pallas_call(adam_kernel,name="adam",grid_spec=spec,out_shape=outs,
      compiler_params=pltpu.CompilerParams(vmem_limit_bytes=62*2**20))(owners,so,sg,at,f,f,f,*q3,*p3,*e3,*r3,*h3,*b3,*n3)
def flip_kernel(x_ref, o_ref):
    o_ref[...]=x_ref[...].T

def feature_major(x):
    n=x.shape[0]; b=512
    return pl.pallas_call(flip_kernel,name="flip",grid=(pl.cdiv(n,b),),in_specs=[pl.BlockSpec((b,D),lambda i:(i,0))],
      out_specs=pl.BlockSpec((D,b),lambda i:(0,i)),out_shape=jax.ShapeDtypeStruct((D,n),F32),
      cost_estimate=pl.CostEstimate(flops=4*10**9,bytes_accessed=8*10**6,transcendentals=0))(x)


def positions(key_len, model_width):
    distance = (key_len - 1 - jnp.arange(key_len)).astype(jnp.float32)
    frequency = jnp.exp(
        jnp.arange(model_width // 2).astype(jnp.float32) * (-2.0 * math.log(10000.0) / model_width)
    )
    angles = distance[:, None] * frequency[None, :]
    return jnp.concatenate([jnp.sin(angles), jnp.cos(angles)], axis=1)


def shards(
    tokens,
    prior_memory,
    first_flags,
    owners,
    cotangent,
    qkvr_master,
    qkvr_first,
    qkvr_second,
    proj_master,
    proj_first,
    proj_second,
    expand_master,
    expand_first,
    expand_second,
    reduce_master,
    reduce_first,
    reduce_second,
    headbias_master,
    headbias_first,
    headbias_second,
    expbias_master,
    expbias_first,
    expbias_second,
    norms_master,
    norms_first,
    norms_second,
):
    heads_count = lax.axis_size("head")
    head = lax.axis_index("head")
    n_dp = lax.axis_size("dp")
    dp = lax.axis_index("dp")
    swap = [(h, heads_count - 1 - h) for h in range(heads_count)]
    def other(v):
        return lax.ppermute(v, "head", swap)
    def dp_swap(v, b):
        return lax.ppermute(v, "dp", [(i, i ^ b) for i in range(n_dp)])
    qkvr_own = jnp.pad(qkvr_master.astype(BF), ((0, 0), (0, WR - D), (0, WC - CG)))
    wo_own = proj_master.astype(BF)
    w1_own = expand_master.astype(BF)
    w2_own = reduce_master.T.astype(BF)
    b1_own = expbias_master.astype(BF).astype(F32)
    qkvr_oth = other(qkvr_own)
    small = other(jnp.concatenate([headbias_master.reshape(-1), b1_own]))
    wo_oth = other(wo_own)
    w1_oth = other(w1_own)
    w2_oth = other(w2_own)
    hb_oth = small[:2 * CG].reshape(2, CG)
    b1_oth = small[2 * CG:]
    meta = jnp.concatenate([head[None].astype(jnp.int32), lax.dynamic_slice_in_dim(first_flags, head * 2, 2, 0)])
    rows = positions(2 * SEG, D).astype(BF)
    tab = jnp.concatenate([rows[44:300], jnp.pad(rows, ((16, 68), (0, 0)))], 0)
    own = (qkvr_own, wo_own, headbias_master)
    oth = (qkvr_oth, wo_oth, hb_oth)
    att_own, p_own, *pre_own, _, x_rows = attention_fwd(True, meta, tokens.T, prior_memory, qkvr_own, wo_own, tab, headbias_master)
    att_oth, p_oth, *pre_oth, _ = attention_fwd(False, meta, x_rows, prior_memory, qkvr_oth, wo_oth, tab, hb_oth)
    lo, dres, ff_own, ff_oth = ff(
        att_own, att_oth, x_rows, cotangent.T, wo_own, wo_oth, w1_own, w1_oth, w2_own, w2_oth,
        jnp.concatenate([b1_own, b1_oth])[None], norms_master)
    ff_got = other(ff_oth)
    def back(streams, group, p, pre, base, half=False, prev=None):
        w4, wo, hb = group
        kv, wuv, wT, rel = pre
        return attention_bwd(streams, meta, x_rows, prior_memory, p, dres, base, w4, wo, wT, rel, tab, kv, wuv, half, prev)
    ig, at_oth = back((0, 1), oth, p_oth, pre_oth, dres, True)
    at_got = other(at_oth)
    ig0, at0 = back((0,), own, p_own, pre_own, ig)
    ff_got, ig0 = lax.optimization_barrier((ff_got, ig0))
    chunk = ff_own.shape[0] // n_dp
    half = (ff_own.astype(F32) + ff_got.astype(F32)).astype(BF).reshape(n_dp // 2, 2, chunk, HFP)
    odd = (dp & 1) == 1
    send = jnp.where(odd, half[:, 0], half[:, 1])
    keep = jnp.where(odd, half[:, 1], half[:, 0])
    pair = (keep.astype(F32) + dp_swap(send, 1).astype(F32)).astype(BF)
    pair, ig0 = lax.optimization_barrier((pair, ig0))
    split = lax.all_to_all(pair, "dp", 0, 0, tiled=True, axis_index_groups=[list(range(c, n_dp, 2)) for c in range(2)])
    input_grad, at1 = back((1,), own, p_own, pre_own, ig, False, (ig0, at0))
    split, at1 = lax.optimization_barrier((split, at1))
    part = jnp.sum(split.astype(F32), 0).astype(BF)
    ff_sum = lax.all_gather(part, "dp", axis=0, tiled=True)
    at_got, at1 = lax.optimization_barrier((at_got, at1))
    at_sum = (at1 + at_got.astype(F32)).astype(BF)
    waiting = [lo, input_grad]
    flipped = []
    bit = 1
    while bit < n_dp:
        part_rows = at_sum.shape[0] // 2
        up = (dp & bit) != 0
        send = jnp.where(up, at_sum[:part_rows], at_sum[part_rows:])
        keep = jnp.where(up, at_sum[part_rows:], at_sum[:part_rows])
        got = dp_swap(send, bit)
        if bit > 1 and waiting:
            got, done = lax.optimization_barrier((got, feature_major(waiting.pop(0))))
            flipped.append(done)
        at_sum = (keep.astype(F32) + got.astype(F32)).astype(BF)
        bit *= 2
    flipped += [feature_major(v) for v in waiting]
    while bit > 1:
        bit //= 2
        got = dp_swap(at_sum, bit)
        up = (dp & bit) != 0
        at_sum = jnp.where(up, jnp.concatenate([got, at_sum], 0), jnp.concatenate([at_sum, got], 0))
    sq_own = squares(at_sum, ff_sum)
    sq_got = other(sq_own)
    flip = lambda v: jnp.transpose(v, (1, 0, 2))
    stats, *res = adam(
        owners, sq_own, sq_got, at_sum, ff_sum,
        (flip(qkvr_first), flip(qkvr_second), flip(qkvr_master)),
        (proj_first, proj_second, proj_master),
        (expand_first, expand_second, expand_master),
        (reduce_first.T, reduce_second.T, reduce_master.T),
        (headbias_first, headbias_second, headbias_master),
        (expbias_first, expbias_second, expbias_master),
        (norms_first, norms_second, norms_master))
    big = [[flip(v) for v in res[0:5]], res[5:10], res[10:15], [v.T for v in res[15:20]]]
    outs = [flipped[0].T, flipped[1].T, stats[0, :7]]
    for r in big:
        outs += r[:4]
    outs += res[20:32]
    return tuple(outs + [r[4] for r in big])


def solution(mesh):
    in_specs = (
        P(("dp", "head"), None),
        P("dp", None, None),
        P("dp"),
        P(),
        P(("dp", "head"), None),
        P(None, None, "head"),
        P(None, None, "head"),
        P(None, None, "head"),
        P("head", None),
        P("head", None),
        P("head", None),
        P(None, "head"),
        P(None, "head"),
        P(None, "head"),
        P("head", None),
        P("head", None),
        P("head", None),
        P(None, "head"),
        P(None, "head"),
        P(None, "head"),
        P("head"),
        P("head"),
        P("head"),
        P(),
        P(),
        P(),
    )
    out_specs = (
        P(("dp", "head"), None),
        P(("dp", "head"), None),
        P(),
        P(None, None, "head"),
        P(None, None, "head"),
        P(None, None, "head"),
        P(None, None, "head"),
        P("head", None),
        P("head", None),
        P("head", None),
        P("head", None),
        P(None, "head"),
        P(None, "head"),
        P(None, "head"),
        P(None, "head"),
        P("head", None),
        P("head", None),
        P("head", None),
        P("head", None),
        P(None, "head"),
        P(None, "head"),
        P(None, "head"),
        P(None, "head"),
        P("head"),
        P("head"),
        P("head"),
        P("head"),
        P(),
        P(),
        P(),
        P(),
        P(None, None, "head"),
        P("head", None),
        P(None, "head"),
        P("head", None),
    )
    return jax.shard_map(shards, mesh=mesh, in_specs=in_specs, out_specs=out_specs, check_vma=False)
```

```python
from jax.sharding import PartitionSpec as P
import math, functools
import jax, jax.numpy as jnp
from jax import lax
from jax.experimental import pallas as pl
from jax.experimental.pallas import tpu as pltpu
BF=jnp.bfloat16; F32=jnp.float32
NT=(((1,),(1,)),((),())); TN=(((0,),(0,)),((),()))
def dot(a,b,dn=(((1,),(0,)),((),()))): return lax.dot_general(a,b,dn,preferred_element_type=F32)
SEG=150; NSEG=8; LEN=1200; DH=41; HG=5; CG=205; D=410
RA=96; RQ=160; KA_=256; KB_=384; KC=304
HP=48; GP=HP*HG
LV={2:RA,3:56}
def fill(v,rows):
    return v if v.shape[0]==rows else jnp.concatenate([v,jnp.zeros((rows-v.shape[0],v.shape[1]),v.dtype)],0)
SCALE=1.0/math.sqrt(DH); LOG2E=1.4426950408889634

def fill_rows(x_rows, prior_ref, xs, xcat, xq):
    xs[0:SEG,:]=prior_ref[0].astype(F32)
    xs[SEG:SEG+LEN,:]=x_rows.astype(F32)
    xs[SEG+LEN:1376,:]=jnp.zeros((1376-SEG-LEN,D),F32)
    for s in range(NSEG):
        xcat[s]=xs[SEG*s:SEG*s+KC,:].astype(BF)
        xq[s]=xs[SEG*(s+1):SEG*(s+1)+RQ,:].astype(BF)

def head_masks(rows):
    lane=lax.broadcasted_iota(jnp.int32,(rows,CG),1)
    return [(lane>=DH*h)&(lane<DH*(h+1)) for h in range(HG)]

U=4
GU=4
WR=416; WC=256
def ka_kernel(first, meta, x_ref, prior_ref, w4p, wo, tab, bias, att_ref, p_ref, kv_ref, wuv_ref, wT_ref, rel_ref, bT_ref, *rest):
    if first: xn_ref, xs, xcat, xq, attS, biasA, biasB = rest
    else: xs, xcat, xq, attS, biasA, biasB = rest
    w4=[w4p[k,0:D,0:CG] for k in range(4)]
    n=pl.program_id(0); st=pl.program_id(1)
    @pl.when((st==0)&(n==0))
    def _():
        rel_ref[...]=dot(tab[...],w4[3]).astype(BF)
        xs[0:GP,:]=jnp.zeros((GP,D),F32)
        for k in range(4):
            src=w4[k].astype(F32).T if k<3 else wo[...].astype(F32)
            for h in range(HG): xs[HP*h:HP*h+DH,:]=src[DH*h:DH*h+DH]
            wT_ref[k]=xs[0:GP,:].astype(BF)
        bt=jnp.concatenate([bias[...],jnp.zeros((6,CG),F32)],0).T
        xs[0:GP,0:8]=jnp.zeros((GP,8),F32)
        for h in range(HG): xs[HP*h:HP*h+DH,0:8]=bt[DH*h:DH*h+DH]
        bT_ref[...]=xs[0:GP,0:8]
    @pl.when(st==0)
    def _():
        if first:
            @pl.when(n==0)
            def _():
                tiles=2*LEN//128
                for t in range(tiles): xn_ref[128*t:128*t+128,:]=x_ref[:,128*t:128*t+128].T
                xn_ref[128*tiles:,:]=x_ref[:,128*tiles:].T
            fill_rows(xn_ref[pl.ds(pl.multiple_of(n*LEN,16),LEN),:],prior_ref,xs,xcat,xq)
        else: fill_rows(x_ref[...],prior_ref,xs,xcat,xq)
    NA=RA; NB=RQ-RA
    has_mem=(st>0)|(meta[1+n]==1)
    jmin=jnp.where(has_mem,0,SEG)
    @pl.when(st==0)
    def _():
        for u in range(U):
            jm=jmin if u==0 else 0
            i=lax.broadcasted_iota(jnp.int32,(RA,KA_),0); j=lax.broadcasted_iota(jnp.int32,(RA,KA_),1)
            biasA[u]=jnp.where((j<=i+SEG)&(j>=jm),0.0,-1e30)
            i=lax.broadcasted_iota(jnp.int32,(NB,KB_),0)+RA; j=lax.broadcasted_iota(jnp.int32,(NB,KB_),1)
            biasB[u]=jnp.where((j<=i+SEG)&(j>=jm)&(j<2*SEG),0.0,-1e30)
    @pl.when(st==1)
    def _():
        biasA[0]=biasA[1]; biasB[0]=biasB[1]
    hm=head_masks(RQ)
    hmA=[m[0:RA] for m in hm]; hmB=[m[RA:] for m in hm]
    zero=jnp.zeros((),BF)
    iA=lax.broadcasted_iota(jnp.int32,(RA,128),0); lA=lax.broadcasted_iota(jnp.int32,(RA,128),1)
    mA=(lA+(105-iA))<128
    iB=lax.broadcasted_iota(jnp.int32,(NB,128),0); lB=lax.broadcasted_iota(jnp.int32,(NB,128),1)
    mB=(lB+(69-iB))<128
    c=SCALE*LOG2E
    vv=[None]*U
    def scores(u):
        s=st*U+u
        xc=xcat[s]
        zr=jnp.zeros((KB_-KC,CG),BF)
        kk=jnp.concatenate([dot(xc,w4[1]).astype(BF),zr],0)
        vv[u]=jnp.concatenate([dot(xc,w4[2]).astype(BF),zr],0)
        qT=dot(wT_ref[0],xq[s],NT).astype(BF).astype(F32)
        lateT.append((u,kk,vv[u],(qT+bT_ref[:,0:1]).astype(BF),(qT+bT_ref[:,1:2]).astype(BF)))
        q=dot(xq[s],w4[0]).astype(BF).astype(F32)
        wu=(q+bias[0:1,:]).astype(BF); wvv=(q+bias[1:2,:]).astype(BF)
        wum=[jnp.where(m,wu,zero) for m in hm]
        wvm=[jnp.where(m,wvv,zero) for m in hm]
        SA=dot(jnp.concatenate([w[0:RA] for w in wum],0),kk[0:KA_],NT)
        PA=dot(jnp.concatenate([w[0:RA] for w in wvm],0),rel_ref[0:KA_],NT)
        SB=dot(jnp.concatenate([w[RA:] for w in wum],0),kk,NT)
        PB=dot(jnp.concatenate([w[RA:] for w in wvm],0),rel_ref[KA_:],NT)
        return SA,PA,SB,PB
    def soft(u,sc):
        SA,PA,SB,PB=sc
        units=[]
        for h in range(HG):
            units.append((h,SA,PA,NA,2,0,23,biasA,mA)); units.append((h,SB,PB,NB,3,RA,59,biasB,mB))
        out=[]
        for i0 in range(0,len(units),GU):
            grp=units[i0:i0+GU]
            rolls=[[pltpu.roll(P_[R*h:R*h+min(R,LV[nt]),128*k:128*k+128],b0,1,stride=1,stride_axis=0) for k in range(nt)] for (h,S_,P_,R,nt,r0,b0,bs,m) in grp]
            ts=[]
            for (h,S_,P_,R,nt,r0,b0,bs,m),rr in zip(grp,rolls):
                L=LV[nt]
                ts.append([(S_[R*h:R*h+L,128*k:128*k+128]+(jnp.where(m[0:L],rr[k],rr[k+1]) if k+1<nt else rr[k]))*c+bs[u,0:L,128*k:128*k+128] for k in range(nt)])
            mxs=[]
            for t in ts:
                mx=t[0]
                for v in t[1:]: mx=jnp.maximum(mx,v)
                mxs.append(mx)
            mxs=[jnp.max(v,axis=1,keepdims=True) for v in mxs]
            es=[[jnp.exp2(v-mx) for v in t] for t,mx in zip(ts,mxs)]
            sms=[]
            for e in es:
                sm=e[0]
                for v in e[1:]: sm=sm+v
                sms.append(sm)
            lis=[1.0/jnp.sum(v,axis=1,keepdims=True) for v in sms]
            for (h,S_,P_,R,nt,r0,b0,bs,m),e,li in zip(grp,es,lis):
                p=jnp.concatenate([fill(v*li,R).astype(BF) for v in e],1)
                late.append((u,h,r0,R,nt,p))
                out.append(p)
        return out[0::2],out[1::2]
    def outp(u,pp):
        pas,pbs=pp
        s=st*U+u
        OA=dot(jnp.concatenate(pas,0),vv[u][0:KA_])
        OB=dot(jnp.concatenate(pbs,0),vv[u])
        aA=OA[0:NA]; aB=OB[0:NB]
        for h in range(1,HG):
            aA=jnp.where(hmA[h],OA[NA*h:NA*(h+1)],aA)
            aB=jnp.where(hmB[h],OB[NB*h:NB*(h+1)],aB)
        lateA.append((s,aA,aB))
    sc=[None]*U; pp=[None]*U; late=[]; lateA=[]; lateT=[]
    sc[0]=scores(0)
    for u in range(U):
        if u+1<U: sc[u+1]=scores(u+1)
        pp[u]=soft(u,sc[u])
        if u>0: outp(u-1,pp[u-1])
    outp(U-1,pp[U-1])
    for (u,h,r0,R,nt,p) in late: p_ref[0,u,h,r0:r0+R,0:128*nt]=p
    for (u,a,b,c_,d_) in lateT:
        kv_ref[0,u,0]=a[0:KC]; kv_ref[0,u,1]=b[0:KC]; wuv_ref[0,u,0]=c_; wuv_ref[0,u,1]=d_
    for (s,aA,aB) in lateA:
        attS[s,0:RA,:]=aA
        attS[s,RA:RQ,:]=aB
    @pl.when(st==NSEG//U-1)
    def _():
        for t in range(NSEG):
            xs[SEG*t:SEG*t+152,0:CG]=attS[t,0:152,:]
        att_ref[...]=xs[0:LEN,0:CG].astype(BF)

def attention_fwd(first,meta,x,prior,w4,wo,tab,bias):
    cst=lambda *sh: pl.BlockSpec(sh,lambda n,s,m: (0,)*len(sh))
    S=jax.ShapeDtypeStruct
    gs=pltpu.PrefetchScalarGridSpec(num_scalar_prefetch=1,grid=(2,NSEG//U),
      in_specs=[cst(D,2*LEN) if first else pl.BlockSpec((LEN,D),lambda n,s,m:(n,0)),
        pl.BlockSpec((1,SEG,D),lambda n,s,m:(m[0]*2+n,0,0)),
        cst(4,WR,WC),cst(CG,D),cst(KA_+KB_,D),cst(2,CG)],
      out_specs=[pl.BlockSpec((LEN,CG),lambda n,s,m:(n,0)),
        pl.BlockSpec((1,U,HG,RQ,KB_),lambda n,s,m:(n,s,0,0,0)),pl.BlockSpec((1,U,2,KC,CG),lambda n,s,m:(n,s,0,0,0)),pl.BlockSpec((1,U,2,GP,RQ),lambda n,s,m:(n,s,0,0,0)),cst(4,GP,D),cst(KA_+KB_,CG),cst(GP,8)]+([cst(2*LEN,D)] if first else []),
      scratch_shapes=[pltpu.VMEM((1376,D),F32),pltpu.VMEM((NSEG,KC,D),BF),pltpu.VMEM((NSEG,RQ,D),BF),
        pltpu.VMEM((NSEG,RQ,CG),F32),
        pltpu.VMEM((U,RA,KA_),F32),pltpu.VMEM((U,RQ-RA,KB_),F32)])
    return pl.pallas_call(functools.partial(ka_kernel,first),grid_spec=gs,name="attn_fwd",
      out_shape=[S((2*LEN,CG),BF),S((2,NSEG,HG,RQ,KB_),BF),S((2,NSEG,2,KC,CG),BF),S((2,NSEG,2,GP,RQ),BF),S((4,GP,D),BF),S((KA_+KB_,CG),BF),S((GP,8),F32)]+([S((2*LEN,D),BF)] if first else []),
      compiler_params=pltpu.CompilerParams(vmem_limit_bytes=56*2**20))(meta,x,prior,w4,wo,tab,bias)

CLIP_LEVEL = 0.01
BETA_ONE = 0.5
BETA_TWO = 0.5
ADAM_EPSILON = 1e-08
WEIGHT_DECAY = 0.1
STEP = 10
STEP_RATES = (0.03, 0.2, 0.03, 0.015, 0.3, 0.3, 0.3)
T=480; HF=1050; HFP=1152
G0=0.7978845608028654; G1=0.044715; EPS=1e-5
def ln_fwd(z):
    m=jnp.mean(z,axis=-1,keepdims=True)
    c=z-m
    v=jnp.mean(c*c,axis=-1,keepdims=True)
    r=lax.rsqrt(v+EPS)
    return c*r,r
def ln_bwd(n,r,e):
    return r*(e-jnp.mean(e,axis=-1,keepdims=True)-n*jnp.mean(e*n,axis=-1,keepdims=True))
def kf_kernel(ao,at,x,ct,woo,wot,w1o,w1t,w2o,w2t,b1,nm, lo_ref,dres_ref,g_o,g_t,awo_o,awo_t,aw1,aw2,gnm_acc,ctS,w1c,w2c):
    i=pl.program_id(0); last=pl.num_programs(0)-1
    @pl.when(i==0)
    def _():
        for r in (awo_o,awo_t,aw1,aw2,gnm_acc): r[...]=jnp.zeros(r.shape,F32)
        for r,u,v in ((w1c,w1o,w1t),(w2c,w2o,w2t)):
            r[...]=jnp.concatenate([u[...].astype(F32),v[...].astype(F32)],1).astype(BF)
    @pl.when(i==0)
    def _():
        tiles=ctS.shape[0]//128
        for t in range(tiles): ctS[128*t:128*t+128,:]=ct[:,128*t:128*t+128].T
        if tiles*128<ctS.shape[0]: ctS[128*tiles:,:]=ct[:,128*tiles:].T
    c=ctS[pl.ds(i*T,T),:]
    attn=dot(ao[...],woo[...])+dot(at[...],wot[...])
    z=x[...].astype(F32)+attn
    n1,r1=ln_fwd(z)
    normed=n1*nm[0:1]+nm[1:2]
    nl=normed.astype(BF)
    def gate(pre):
        p2=pre*pre
        t=jnp.tanh(G0*pre*(1.0+G1*p2))
        hp=0.5*(1.0+t)
        act=pre*hp
        der=hp+0.5*pre*(1.0-t*t)*(G0*(1.0+3.0*G1*p2))
        return act.astype(BF),der
    parts=((0,768),(768,1536),(1536,2*HF))
    pres=[dot(nl,w1c[:,lo:hi])+b1[:,lo:hi] for lo,hi in parts[:1]]
    acts=[];ders=[]
    second=normed+nm[2:3]
    for k,(lo,hi) in enumerate(parts):
        if k+1<len(parts):
            l2,h2=parts[k+1]
            pres.append(dot(nl,w1c[:,l2:h2])+b1[:,l2:h2])
        a_,d_=gate(pres[k])
        acts.append(a_); ders.append(d_)
        second=second+dot(a_,w2c[:,lo:hi],NT)
    n2,r2=ln_fwd(second)
    lo_ref[...]=n2*nm[3:4]+nm[4:5]
    d2=ln_bwd(n2,r2,c*nm[3:4])
    d2l=d2.astype(BF)
    dn=d2
    for k,(lo,hi) in enumerate(parts):
        dpre=dot(d2l,w2c[:,lo:hi])*ders[k]
        aw2[0:D,lo:hi]+=dot(d2l,acts[k],TN)
        aw1[D:D+1,lo:hi]+=jnp.sum(dpre,axis=0,keepdims=True)
        dpl=dpre.astype(BF)
        aw1[0:D,lo:hi]+=dot(nl,dpl,TN)
        dn=dn+dot(dpl,w1c[:,lo:hi],NT)
    dz=ln_bwd(n1,r1,dn*nm[0:1])
    dres_ref[...]=dz
    dal=dz.astype(BF)
    awo_o[0:CG]+=dot(ao[...],dal,TN)
    awo_t[0:CG]+=dot(at[...],dal,TN)
    gnm=jnp.concatenate([jnp.sum(v,axis=0,keepdims=True) for v in (dn*n1,dn,d2,c*n2,c)],0)
    gnm_acc[0:5]+=gnm
    @pl.when(i==last)
    def _():
        aw2[D:D+5,0:D]=gnm_acc[0:5]
        aw2[D:D+5,HF:HF+D]=gnm_acc[0:5]
        for g,lo,aw in ((g_o,0,awo_o),(g_t,HF,awo_t)):
            g[:,1024:HFP]=jnp.zeros((1024,HFP-1024),BF)
            g[0:416,0:HF]=aw1[:,lo:lo+HF].astype(BF)
            g[416:448,0:1024]=jnp.zeros((32,1024),BF)
            g[448:864,0:HF]=aw2[:,lo:lo+HF].astype(BF)
            g[864:1024,0:1024]=jnp.zeros((160,1024),BF)
            g[896:1008,0:D]=aw[0:112].astype(BF)
            g[896:1008,512:512+D]=aw[112:224].astype(BF)
def ff(ao,at,x,ct,woo,wot,w1o,w1t,w2o,w2t,b1,nm):
    n=x.shape[0]
    row=lambda w: pl.BlockSpec((T,w),lambda i:(i,0))
    cst=lambda *sh: pl.BlockSpec(sh,lambda i:(0,)*len(sh),pipeline_mode=pl.Buffered(1))
    S=jax.ShapeDtypeStruct
    gs=[(1024,HFP),(1024,HFP)]
    spec=pl.GridSpec(grid=(n//T,),
      in_specs=[row(CG),row(CG),row(D),cst(D,n),cst(CG,D),cst(CG,D),cst(D,HF),cst(D,HF),cst(D,HF),cst(D,HF),cst(1,2*HF),cst(5,D)],
      out_specs=[row(D),row(D)]+[cst(*s) for s in gs],
      scratch_shapes=[pltpu.VMEM((224,D),F32)]*2+[pltpu.VMEM((416,2*HF),F32)]*2+[pltpu.VMEM((8,D),F32),pltpu.VMEM((n,D),F32)]+[pltpu.VMEM((D,2*HF),BF)]*2)
    return pl.pallas_call(kf_kernel,name="ff",grid_spec=spec,
      out_shape=[S((n,D),F32),S((n,D),F32)]+[S(s,BF) for s in gs],
      compiler_params=pltpu.CompilerParams(vmem_limit_bytes=60*2**20))(ao,at,x,ct,woo,wot,w1o,w1t,w2o,w2t,b1,nm)
def rev8(v):
    idx=7-lax.broadcasted_iota(jnp.int32,v.shape,0)
    return jnp.take_along_axis(v,idx,axis=0)
def unskew(blocks, base, rows):
    nb=len(blocks)
    lane=lax.broadcasted_iota(jnp.int32,(8,128),1); sub=lax.broadcasted_iota(jnp.int32,(8,128),0)
    outs=[[] for _ in blocks]
    for r in range(rows//8):
        sh=base-8*r-7
        rot=[pltpu.roll(rev8(b[8*r:8*r+8]),sh%128,1,stride=1,stride_axis=0) for b in blocks]
        m=lane<(sh+sub)
        for k in range(nb):
            if k==0: o=jnp.where(m,0.0,rot[0])
            else: o=jnp.where(m,rot[k-1],rot[k])
            outs[k].append(rev8(o))
    return [jnp.concatenate(o,0) for o in outs]

UB=4
def kb_kernel(last, half, meta, x_ref, prior_ref, p_ref, dres_ref, *rest):
    if half: base_ref=dres_ref
    else: base_ref, *rest = rest
    w4p, wo, wT, rel, tab, kv_ref, wuv_ref, *rest = rest
    w4=[w4p[k,0:D,0:CG] for k in range(3)]
    if last:
        prev_ref, gp_ref, ig_ref, g_ref, xs, xcat, xq, dalS, ig, acc, drA, drB, dbias, G = rest
    else:
        ig_ref, g_ref, xs, xcat, xq, dalS, ig, acc, drA, drB, dbias, G = rest
    n=pl.program_id(0); st=pl.program_id(1)
    NA=RA; NB=RQ-RA
    @pl.when((st==0)&(n==0))
    def _():
        for r in (acc,drA,drB,dbias): r[...]=jnp.zeros(r.shape,F32)
    @pl.when(st==0)
    def _():
        xs[LEN:1376,:]=jnp.zeros((1376-LEN,D),F32)
        xs[0:LEN,:]=dres_ref[...]
        rows=lax.broadcasted_iota(jnp.int32,(RQ,D),0)
        for t in range(NSEG):
            dalS[t]=jnp.where(rows<SEG,xs[SEG*t:SEG*t+RQ,:],0.0).astype(BF)
        fill_rows(x_ref[...],prior_ref,xs,xcat,xq)
        xs[SEG:SEG+LEN,:]=base_ref[...]
        for t in range(NSEG+1):
            ig[t]=xs[SEG*t:SEG*t+152,:]
    hm=head_masks(RQ)
    zero=jnp.zeros((),BF)
    zr=jnp.zeros((KB_-KC,CG),BF)
    wkvT=wT[1:3].reshape(2*GP,D); woT=wT[3]
    def front(u):
        s=st*UB+u
        dal=dalS[s]
        kk=jnp.concatenate([kv_ref[0,u,0],zr],0)
        vv=jnp.concatenate([kv_ref[0,u,1],zr],0)
        wuT=wuv_ref[0,u,0]; wvT=wuv_ref[0,u,1]
        da=dot(dal,wo[...],NT).astype(BF)
        daT=dot(woT,dal,NT).astype(BF)
        dam=[jnp.where(m,da,zero) for m in hm]
        DA=dot(jnp.concatenate([w[0:RA] for w in dam],0),vv[0:KA_],NT)
        DB=dot(jnp.concatenate([w[RA:] for w in dam],0),vv,NT)
        ps=[(p_ref[0,u,h,0:RA,0:KA_],p_ref[0,u,h,RA:RQ,:]) for h in range(HG)]
        return kk,wuT,wvT,daT,DA,DB,ps
    def mid(fr):
        kk,wuT,wvT,daT,DA,DB,ps=fr
        res=[]
        for h in range(HG):
            one=[]
            for p,dp,R,nt,base in ((ps[h][0],DA[NA*h:NA*(h+1)],NA,2,105),(ps[h][1],DB[NB*h:NB*(h+1)],NB,3,69)):
                L=LV[nt]
                pf=p.astype(F32)[0:L]; dp=dp[0:L]
                w=dp*pf
                sm=w[:,0:128]
                for k in range(1,nt): sm=sm+w[:,128*k:128*k+128]
                delta=jnp.sum(sm,axis=1,keepdims=True)
                dr=(pf*SCALE)*(dp-delta)
                o=unskew([dr[:,128*k:128*k+128] for k in range(nt)],base,L)
                one.append((fill(dr,R).astype(BF),jnp.concatenate([fill(v,R).astype(BF) for v in o],1)))
            res.append(one)
        return res
    late=[]
    def back(u,fr,md):
        kk,wuT,wvT,daT,DA,DB,ps=fr
        s=st*UB+u
        dkT=[];dvT=[];rA=[];rB=[]
        for h in range(HG):
            (ra,pa_),(rb,pb_)=md[h]
            u_=wuT[HP*h:HP*(h+1)]; v_=wvT[HP*h:HP*(h+1)]; d_=daT[HP*h:HP*(h+1)]
            pA,pB=ps[h]
            k1=dot(u_,jnp.concatenate([ra,rb[:,0:KA_]],0)); k2=dot(u_[:,RA:],rb[:,KA_:])
            dkT.append(jnp.concatenate([k1,k2],1))
            v1=dot(d_,jnp.concatenate([pA,pB[:,0:KA_]],0)); v2=dot(d_[:,RA:],pB[:,KA_:])
            dvT.append(jnp.concatenate([v1,v2],1))
            rA.append(dot(v_[:,0:RA],pa_)); rB.append(dot(v_[:,RA:],pb_))
        def comb(col,mA_,mB_):
            OA=dot(jnp.concatenate([md[h][0][col] for h in range(HG)],0),mA_)
            OB=dot(jnp.concatenate([md[h][1][col] for h in range(HG)],0),mB_)
            aA=OA[0:NA]; aB=OB[0:NB]
            for h in range(1,HG):
                aA=jnp.where(hm[h][0:RA],OA[NA*h:NA*(h+1)],aA)
                aB=jnp.where(hm[h][RA:],OB[NB*h:NB*(h+1)],aB)
            return aA,aB
        uA,uB=comb(0,kk[0:KA_],kk)
        vA,vB=comb(1,rel[0:KA_],rel[KA_:])
        db=jnp.concatenate([jnp.sum(uA,0,keepdims=True)+jnp.sum(uB,0,keepdims=True),jnp.sum(vA,0,keepdims=True)+jnp.sum(vB,0,keepdims=True)],0)
        dq=jnp.concatenate([(uA+vA).astype(BF),(uB+vB).astype(BF)],0)
        dk=jnp.concatenate(dkT,0).astype(BF); dv=jnp.concatenate(dvT,0).astype(BF)
        xc=xcat[s]; xqs=xq[s]
        kv=jnp.concatenate([dk[:,0:KC],dv[:,0:KC]],0)
        gkv=dot(kv,xc)
        gq=dot(dq,xqs,TN)
        late.append((u,s,jnp.concatenate(rA,0),jnp.concatenate(rB,0),db,gkv,gq,dot(kv,wkvT,TN),dot(dq,w4[0],NT)[0:152]))
    frs=[None]*UB; mds=[None]*UB
    frs[0]=front(0)
    for u in range(UB):
        if u+1<UB: frs[u+1]=front(u+1)
        mds[u]=mid(frs[u])
        if u>0: back(u-1,frs[u-1],mds[u-1])
    back(UB-1,frs[UB-1],mds[UB-1])
    for (u,s,rA,rB,db,gkv,gq,g1,g2) in late:
        drA[...]+=rA; drB[...]+=rB
        dbias[0:2]+=db
        acc[0,0:CG]+=gq
        acc[1]+=gkv[0:GP]; acc[2]+=gkv[GP:]
        G[...]=g1
        ig[s+1]+=g2+G[SEG:SEG+152,:]
        ig[s]+=G[0:152,:]
    @pl.when(st==NSEG//UB-1)
    def _():
        for t in range(NSEG):
            xs[SEG*t:SEG*t+152,:]=ig[t+1]
        ig_ref[...]=xs[0:LEN,:]
    @pl.when((st==NSEG//UB-1)&(n==pl.num_programs(0)-1))
    def _():
        a=jnp.concatenate([drA[...],jnp.zeros((GP,KB_-KA_),F32)],1)
        dr=drB[...]+pltpu.roll(a,60,1)
        acc[3]=dot(dr.astype(BF),tab[KA_:,:])
        xs[0:CG,:]=acc[0,0:CG]
        for k in range(1,4):
            for h in range(HG):
                o=CG*k+DH*h
                xs[o:o+DH,:]=acc[k,HP*h:HP*h+DH]
        xs[4*CG:832,:]=jnp.zeros((832-4*CG,D),F32)
        xs[4*CG:4*CG+2,0:CG]=dbias[0:2]
        g_ref[:,384:512]=jnp.zeros((832,128),g_ref.dtype)
        if last:
            g_ref[:,0:D]=xs[0:832,:]+gp_ref[:,0:D]
        else:
            g_ref[:,0:D]=xs[0:832,:].astype(g_ref.dtype)

def attention_bwd(streams,meta,x,prior,p,dres,base,w4,wo,wT,rel,tab,kv,wuv,half=False,prev=None):
    cst=lambda *sh: pl.BlockSpec(sh,lambda n,s,m: (0,)*len(sh))
    off=streams[0]; ns=len(streams); last=prev is not None
    row=lambda w: pl.BlockSpec((LEN,w),lambda n,s,m:(n+off,0))
    S=jax.ShapeDtypeStruct
    ig_spec=row(D); ig_shape=S((2*LEN,D),F32)
    gs=pltpu.PrefetchScalarGridSpec(num_scalar_prefetch=1,grid=(ns,NSEG//UB),
      in_specs=[row(D),pl.BlockSpec((1,SEG,D),lambda n,s,m:(m[0]*2+n+off,0,0)),
        pl.BlockSpec((1,UB,HG,RQ,KB_),lambda n,s,m:(n+off,s,0,0,0)),row(D)]+([] if half else [row(D)])+[
        cst(4,WR,WC),cst(CG,D),cst(4,GP,D),cst(KA_+KB_,CG),cst(KA_+KB_,D),pl.BlockSpec((1,UB,2,KC,CG),lambda n,s,m:(n+off,s,0,0,0)),pl.BlockSpec((1,UB,2,GP,RQ),lambda n,s,m:(n+off,s,0,0,0))]+([pl.BlockSpec(memory_space=pl.ANY),cst(832,512)] if last else []),
      out_specs=[ig_spec,cst(832,512)],
      scratch_shapes=[pltpu.VMEM((1376,D),F32),pltpu.VMEM((NSEG,KC,D),BF),pltpu.VMEM((NSEG,RQ,D),BF),pltpu.VMEM((NSEG,RQ,D),BF),
        pltpu.VMEM((NSEG+1,152,D),F32),pltpu.VMEM((4,GP,D),F32),pltpu.VMEM((GP,KA_),F32),pltpu.VMEM((GP,KB_),F32),pltpu.VMEM((8,CG),F32),pltpu.VMEM((KC,D),F32)])
    ops=[meta,x,prior,p,dres]+([] if half else [base])+[w4,wo,wT,rel,tab,kv,wuv]+(list(prev) if last else [])
    return pl.pallas_call(functools.partial(kb_kernel,last,half),grid_spec=gs,name="attn_bwd",
      input_output_aliases={13:0} if last else {},
      out_shape=[ig_shape,S((832,512),BF if half else F32)],
      compiler_params=pltpu.CompilerParams(vmem_limit_bytes=62*2**20))(*ops)
RB=64
COUNTS=(4*D*D,D*D,D*2*HF,D*2*HF,2*D,2*HF,5*D)
def total(v):
    return jnp.sum(jnp.sum(v,axis=0,keepdims=True),axis=1,keepdims=True)

def rows_of(pairs):
    row=lax.broadcasted_iota(jnp.int32,(8,128),0)
    acc=jnp.zeros((8,128),F32)
    for k,t in pairs: acc=jnp.where(row==k,t,acc)
    return acc

def sq_ff_kernel(f, out):
    def part(lo,n):
        v=f[lo:lo+n].astype(F32)
        return v*v
    w=part(0,416); r=lax.broadcasted_iota(jnp.int32,(416,HFP),0)
    t2=total(jnp.where(r<D,w,0.0)); t5=total(jnp.where(r[400:416]==D,w[400:416],0.0))
    w=part(448,416)
    t3=total(jnp.where(r<D,w,0.0)); t6=total(jnp.where(r[400:416]>=D,w[400:416],0.0))
    out[...]=rows_of(((1,total(part(896,112))),(2,t2),(3,t3),(5,t5),(6,t6)))

def sq_at_kernel(at, part, out):
    a=at[...].astype(F32); a=a*a
    r=lax.broadcasted_iota(jnp.int32,(832,512),0)
    out[...]=part[...]+rows_of(((0,total(jnp.where(r<4*CG,a,0.0))),(4,total(jnp.where(r[816:832]>=4*CG,a[816:832],0.0)))))

def squares(kernel,*args):
    v=pl.BlockSpec(memory_space=pltpu.VMEM)
    return pl.pallas_call(kernel,name="squares",in_specs=[v]*len(args),out_specs=v,out_shape=jax.ShapeDtypeStruct((8,128),F32),
        cost_estimate=pl.CostEstimate(flops=2*10**9,bytes_accessed=2*10**6,transcendentals=0),
        compiler_params=pltpu.CompilerParams(vmem_limit_bytes=40*2**20))(*args)

def adam_math(g,m,v,w,clip,rate):
    c=g*clip
    m2=BETA_ONE*m+(1.0-BETA_ONE)*c
    v2=BETA_TWO*v+(1.0-BETA_TWO)*c*c
    mh=m2*(1.0/(1.0-BETA_ONE**STEP)); vh=v2*(1.0/(1.0-BETA_TWO**STEP))
    w2=w-rate*(mh/((vh*lax.rsqrt(vh))+ADAM_EPSILON)+WEIGHT_DECAY*w)
    return c,m2,v2,w2

QB=128
def adam_kernel(own, so, sg, at, fh, fp, fb, fn, g1, g2, gm, gv, gw, pm, pv, pw, em, ev, ew, rm, rv, rw, hm_, hv_, hw_, bm_, bv_, bw_, nm_, nv_, nw_, rms_ref, *rest):
    i=pl.program_id(0)
    outs=rest[:-1]; g3=rest[-1]
    tot=[so[k,0]+sg[k,0] if k<6 else so[k,0] for k in range(7)]
    clips=[]; lane=lax.broadcasted_iota(jnp.int32,(1,128),1); rms=jnp.zeros((1,128),F32)
    for k in range(7):
        num=jnp.float32(0); den=jnp.float32(0)
        for j in range(7):
            same=own[k]==own[j]
            num=num+jnp.where(same,tot[j],0.0); den=den+jnp.where(same,jnp.float32(COUNTS[j]),0.0)
        ms=jnp.full((1,128),num,F32)/jnp.full((1,128),den,F32)
        c=jnp.minimum(1.0,CLIP_LEVEL*lax.rsqrt(ms+1e-6))
        clips.append(c[0:1,0:1]); rms=jnp.where(lane==k,jnp.sqrt(ms),rms)
    rms_ref[...]=rms
    def put(o,res):
        for r,v in zip(o[:4],res): r[...]=v
        if len(o)>4: o[4][...]=res[3].astype(BF)
    put(outs[10:15],adam_math(g1[:,0:HF].astype(F32),em[...],ev[...],ew[...],clips[2],STEP_RATES[2]))
    put(outs[15:20],adam_math(g2[:,0:HF].astype(F32),rm[...],rv[...],rw[...],clips[3],STEP_RATES[3]))
    @pl.when(lax.rem(i,2)==0)
    def _():
        blk=at[...].astype(F32)
        for k in range(4): g3[:,k,:]=blk[CG*k:CG*k+CG].T
    put(outs[0:5],adam_math(g3[pl.ds(pl.multiple_of(lax.rem(i,2)*RB,RB),RB)],gm[...],gv[...],gw[...],clips[0].reshape(1,1,1),STEP_RATES[0]))
    @pl.when(i==0)
    def _():
        for lo,hi,l in ((0,112,0),(112,CG,512)):
            g=fp[0:hi-lo,l:l+D].astype(F32)
            res=adam_math(g,pm[lo:hi],pv[lo:hi],pw[lo:hi],clips[1],STEP_RATES[1])
            for r,v in zip(outs[5:9],res): r[lo:hi]=v
            outs[9][lo:hi]=res[3].astype(BF)
        put(outs[20:24],adam_math(fh[...].astype(F32)[4*CG-816:4*CG-814,0:CG],hm_[...],hv_[...],hw_[...],clips[4],STEP_RATES[4]))
        put(outs[24:28],adam_math(fb[...].astype(F32)[D-400,0:HF],bm_[...],bv_[...],bw_[...],clips[5][0],STEP_RATES[5]))
        put(outs[28:32],adam_math(fn[...].astype(F32)[10:15,0:D],nm_[...],nv_[...],nw_[...],clips[6],STEP_RATES[6]))

def adam(owners,so,sg,at,f,q3,p3,e3,r3,h3,b3,n3):
    S=jax.ShapeDtypeStruct
    one=pl.Buffered(1)
    cst=lambda *sh: pl.BlockSpec(sh,lambda i,o:(0,)*len(sh),pipeline_mode=one)
    bq=pl.BlockSpec((RB,4,CG),lambda i,o:(i,0,0)); be=pl.BlockSpec((RB,HF),lambda i,o:(i,0)); bp=cst(CG,D)
    bh,bb,bn=cst(2,CG),cst(HF),cst(5,D)
    sm=pl.BlockSpec(memory_space=pltpu.SMEM)
    spec=pltpu.PrefetchScalarGridSpec(num_scalar_prefetch=1,grid=(7,),
      in_specs=[sm,sm,pl.BlockSpec((832,QB),lambda i,o:(0,i//2)),pl.BlockSpec((16,512),lambda i,o:(51,0)),pl.BlockSpec((112,HFP),lambda i,o:(8,0)),pl.BlockSpec((16,HFP),lambda i,o:(25,0)),pl.BlockSpec((16,HFP),lambda i,o:(53,0)),pl.BlockSpec((RB,HFP),lambda i,o:(i,0)),pl.BlockSpec((RB,HFP),lambda i,o:(7+i,0))]+[bq]*3+[bp]*3+[be]*6+[bh]*3+[bb]*3+[bn]*3,
      out_specs=[cst(1,128)]+[bq]*5+[bp]*5+[be]*10+[bh]*4+[bb]*4+[bn]*4,
      scratch_shapes=[pltpu.VMEM((QB,4,CG),F32)])
    outs=[S((1,128),F32)]
    for sh in ((D,4,CG),(CG,D),(D,HF),(D,HF)): outs+= [S(sh,F32)]*4+[S(sh,BF)]
    for sh in ((2,CG),(HF,),(5,D)): outs+=[S(sh,F32)]*4
    return pl.pallas_call(adam_kernel,name="adam",grid_spec=spec,out_shape=outs,
      compiler_params=pltpu.CompilerParams(vmem_limit_bytes=62*2**20))(owners,so,sg,at,at,f,f,f,f,f,*q3,*p3,*e3,*r3,*h3,*b3,*n3)
def flip_kernel(x_ref, o_ref):
    o_ref[...]=x_ref[...].T

def feature_major(x):
    n=x.shape[0]; b=512
    return pl.pallas_call(flip_kernel,name="flip",grid=(pl.cdiv(n,b),),in_specs=[pl.BlockSpec((b,D),lambda i:(i,0))],
      out_specs=pl.BlockSpec((D,b),lambda i:(0,i)),out_shape=jax.ShapeDtypeStruct((D,n),F32),
      cost_estimate=pl.CostEstimate(flops=4*10**9,bytes_accessed=8*10**6,transcendentals=0))(x)


def positions(key_len, model_width):
    distance = (key_len - 1 - jnp.arange(key_len)).astype(jnp.float32)
    frequency = jnp.exp(
        jnp.arange(model_width // 2).astype(jnp.float32) * (-2.0 * math.log(10000.0) / model_width)
    )
    angles = distance[:, None] * frequency[None, :]
    return jnp.concatenate([jnp.sin(angles), jnp.cos(angles)], axis=1)


def shards(
    tokens,
    prior_memory,
    first_flags,
    owners,
    cotangent,
    qkvr_master,
    qkvr_first,
    qkvr_second,
    proj_master,
    proj_first,
    proj_second,
    expand_master,
    expand_first,
    expand_second,
    reduce_master,
    reduce_first,
    reduce_second,
    headbias_master,
    headbias_first,
    headbias_second,
    expbias_master,
    expbias_first,
    expbias_second,
    norms_master,
    norms_first,
    norms_second,
):
    heads_count = lax.axis_size("head")
    head = lax.axis_index("head")
    n_dp = lax.axis_size("dp")
    dp = lax.axis_index("dp")
    swap = [(h, heads_count - 1 - h) for h in range(heads_count)]
    def other(v):
        return lax.ppermute(v, "head", swap)
    def dp_swap(v, b):
        return lax.ppermute(v, "dp", [(i, i ^ b) for i in range(n_dp)])
    qkvr_own = jnp.pad(qkvr_master.astype(BF), ((0, 0), (0, WR - D), (0, WC - CG)))
    wo_own = proj_master.astype(BF)
    w1_own = expand_master.astype(BF)
    w2_own = reduce_master.T.astype(BF)
    b1_own = expbias_master.astype(BF).astype(F32)
    qkvr_oth = other(qkvr_own)
    small = other(jnp.concatenate([headbias_master.reshape(-1), b1_own]))
    wo_oth = other(wo_own)
    w1_oth = other(w1_own)
    w2_oth = other(w2_own)
    hb_oth = small[:2 * CG].reshape(2, CG)
    b1_oth = small[2 * CG:]
    meta = jnp.concatenate([head[None].astype(jnp.int32), lax.dynamic_slice_in_dim(first_flags, head * 2, 2, 0)])
    rows = positions(2 * SEG, D).astype(BF)
    tab = jnp.concatenate([rows[44:300], jnp.pad(rows, ((16, 68), (0, 0)))], 0)
    own = (qkvr_own, wo_own, headbias_master)
    oth = (qkvr_oth, wo_oth, hb_oth)
    att_own, p_own, *pre_own, _, x_rows = attention_fwd(True, meta, tokens.T, prior_memory, qkvr_own, wo_own, tab, headbias_master)
    att_oth, p_oth, *pre_oth, _ = attention_fwd(False, meta, x_rows, prior_memory, qkvr_oth, wo_oth, tab, hb_oth)
    lo, dres, ff_own, ff_oth = ff(
        att_own, att_oth, x_rows, cotangent.T, wo_own, wo_oth, w1_own, w1_oth, w2_own, w2_oth,
        jnp.concatenate([b1_own, b1_oth])[None], norms_master)
    ff_got = other(ff_oth)
    def back(streams, group, p, pre, base, half=False, prev=None):
        w4, wo, hb = group
        kv, wuv, wT, rel = pre
        return attention_bwd(streams, meta, x_rows, prior_memory, p, dres, base, w4, wo, wT, rel, tab, kv, wuv, half, prev)
    ig, at_oth = back((0, 1), oth, p_oth, pre_oth, dres, True)
    at_got = other(at_oth)
    ig0, at0 = back((0,), own, p_own, pre_own, ig)
    ff_got, ig0 = lax.optimization_barrier((ff_got, ig0))
    chunk = ff_own.shape[0] // n_dp
    half = (ff_own.astype(F32) + ff_got.astype(F32)).astype(BF).reshape(n_dp // 2, 2, chunk, HFP)
    odd = (dp & 1) == 1
    send = jnp.where(odd, half[:, 0], half[:, 1])
    keep = jnp.where(odd, half[:, 1], half[:, 0])
    pair = (keep.astype(F32) + dp_swap(send, 1).astype(F32)).astype(BF)
    pair, ig0 = lax.optimization_barrier((pair, ig0))
    split = lax.all_to_all(pair, "dp", 0, 0, tiled=True, axis_index_groups=[list(range(c, n_dp, 2)) for c in range(2)])
    input_grad, at1 = back((1,), own, p_own, pre_own, ig, False, (ig0, at0))
    split, at1 = lax.optimization_barrier((split, at1))
    part = jnp.sum(split.astype(F32), 0).astype(BF)
    ff_sum = lax.all_gather(part, "dp", axis=0, tiled=True)
    at_got, at1 = lax.optimization_barrier((at_got, at1))
    at_sum = (at1 + at_got.astype(F32)).astype(BF)
    waiting = [lo, input_grad]
    flipped = []
    bit = 1
    while bit < n_dp:
        part_rows = at_sum.shape[0] // 2
        up = (dp & bit) != 0
        send = jnp.where(up, at_sum[:part_rows], at_sum[part_rows:])
        keep = jnp.where(up, at_sum[part_rows:], at_sum[:part_rows])
        got = dp_swap(send, bit)
        if bit > 1 and waiting:
            got, done = lax.optimization_barrier((got, feature_major(waiting.pop(0))))
            flipped.append(done)
        at_sum = (keep.astype(F32) + got.astype(F32)).astype(BF)
        bit *= 2
    flipped += [feature_major(v) for v in waiting]
    while bit > 1:
        bit //= 2
        got = dp_swap(at_sum, bit)
        if bit == 2:
            got, sq_ff = lax.optimization_barrier((got, squares(sq_ff_kernel, ff_sum)))
        up = (dp & bit) != 0
        at_sum = jnp.where(up, jnp.concatenate([got, at_sum], 0), jnp.concatenate([at_sum, got], 0))
    sq_own = squares(sq_at_kernel, at_sum, sq_ff)
    sq_got = other(sq_own)
    flip = lambda v: jnp.transpose(v, (1, 0, 2))
    stats, *res = adam(
        owners, sq_own, sq_got, at_sum, ff_sum,
        (flip(qkvr_first), flip(qkvr_second), flip(qkvr_master)),
        (proj_first, proj_second, proj_master),
        (expand_first, expand_second, expand_master),
        (reduce_first.T, reduce_second.T, reduce_master.T),
        (headbias_first, headbias_second, headbias_master),
        (expbias_first, expbias_second, expbias_master),
        (norms_first, norms_second, norms_master))
    big = [[flip(v) for v in res[0:5]], res[5:10], res[10:15], [v.T for v in res[15:20]]]
    outs = [flipped[0].T, flipped[1].T, stats[0, :7]]
    for r in big:
        outs += r[:4]
    outs += res[20:32]
    return tuple(outs + [r[4] for r in big])


def solution(mesh):
    in_specs = (
        P(("dp", "head"), None),
        P("dp", None, None),
        P("dp"),
        P(),
        P(("dp", "head"), None),
        P(None, None, "head"),
        P(None, None, "head"),
        P(None, None, "head"),
        P("head", None),
        P("head", None),
        P("head", None),
        P(None, "head"),
        P(None, "head"),
        P(None, "head"),
        P("head", None),
        P("head", None),
        P("head", None),
        P(None, "head"),
        P(None, "head"),
        P(None, "head"),
        P("head"),
        P("head"),
        P("head"),
        P(),
        P(),
        P(),
    )
    out_specs = (
        P(("dp", "head"), None),
        P(("dp", "head"), None),
        P(),
        P(None, None, "head"),
        P(None, None, "head"),
        P(None, None, "head"),
        P(None, None, "head"),
        P("head", None),
        P("head", None),
        P("head", None),
        P("head", None),
        P(None, "head"),
        P(None, "head"),
        P(None, "head"),
        P(None, "head"),
        P("head", None),
        P("head", None),
        P("head", None),
        P("head", None),
        P(None, "head"),
        P(None, "head"),
        P(None, "head"),
        P(None, "head"),
        P("head"),
        P("head"),
        P("head"),
        P("head"),
        P(),
        P(),
        P(),
        P(),
        P(None, None, "head"),
        P("head", None),
        P(None, "head"),
        P("head", None),
    )
    return jax.shard_map(shards, mesh=mesh, in_specs=in_specs, out_specs=out_specs, check_vma=False)
```
